32 devices in a mesh: dp: 8 (over y, x, core), tensor: 4 (over z).
Axes of the slice: x: 2, y: 2, z: 4, core: 2. Of those that a mesh axis runs over, the one named last changes fastest.
Arguments:
- residual: bfloat16 [16384, 1024], P(('dp', 'tensor')), may hold values from -6 to 6
- mixer_in: bfloat16 [1024, 2, 1536], P('dp', None, 'tensor'), may hold values from -0.1875 to 0.1875
- step_in: bfloat16 [1024, 24], P('dp', 'tensor'), may hold values from -0.1875 to 0.1875
- shared_in: bfloat16 [1024, 256], P('dp', 'tensor'), may hold values from -0.1875 to 0.1875
- query_in: bfloat16 [1024, 512], P('dp', 'tensor'), may hold values from -0.1875 to 0.1875
- keyval_in: bfloat16 [1024, 256], P('dp', 'tensor'), may hold values from -0.1875 to 0.1875
- mixer_proj: bfloat16 [1536, 1024], P('tensor', 'dp'), may hold values from -0.15625 to 0.15625
- attn_proj: bfloat16 [512, 1024], P('tensor', 'dp'), may hold values from -1 to 1
- gate_up: bfloat16 [1024, 2, 2048], P('dp', None, 'tensor'), may hold values from -0.1875 to 0.1875
- down_proj: bfloat16 [2048, 1024], P('tensor', 'dp'), may hold values from -0.125 to 0.125
- norm_gain: float32 [1024], replicated, may hold values from 0.5 to 1.5
- mlp_gain: float32 [1024], replicated, may hold values from 0.5 to 1.5
- conv_filter: float32 [4, 1792], replicated, may hold values from -3 to 3
- decay_log: float32 [24], replicated, may hold values from -2 to 1.5
- skip_gain: float32 [24], replicated, may hold values from 0.5 to 1.5
- step_bias: float32 [24], replicated, may hold values from -5 to -1
- gated_gain: float32 [1536], replicated, may hold values from 0.5 to 1.5
- cotangent: bfloat16 [16384, 1024], P(('dp', 'tensor')), may hold values from -6 to 6
Outputs:
- output: float32 [16384, 1024], P(('dp', 'tensor'))
- residual_grad: float32 [16384, 1024], P(('dp', 'tensor'))
- mixer_in_grad: float32 [1024, 2, 1536], P('dp', None, 'tensor')
- step_in_grad: float32 [1024, 24], P('dp', 'tensor')
- shared_in_grad: float32 [1024, 256], P('dp', 'tensor')
- query_in_grad: float32 [1024, 512], P('dp', 'tensor')
- keyval_in_grad: float32 [1024, 256], P('dp', 'tensor')
- mixer_proj_grad: float32 [1536, 1024], P('tensor', 'dp')
- attn_proj_grad: float32 [512, 1024], P('tensor', 'dp')
- gate_up_grad: float32 [1024, 2, 2048], P('dp', None, 'tensor')
- down_proj_grad: float32 [2048, 1024], P('tensor', 'dp')
- norm_gain_grad: float32 [1024], replicated
- mlp_gain_grad: float32 [1024], replicated
- conv_filter_grad: float32 [4, 1792], replicated
- decay_log_grad: float32 [24], replicated
- skip_gain_grad: float32 [24], replicated
- step_bias_grad: float32 [24], replicated
- gated_gain_grad: float32 [1536], replicated
The draws below stay inside these ranges and needn't reach their ends.
All inputs are finite; a program needn't handle non-finite values.
Results may differ from the reference program's by a relative error of at most 0.019.
Values may be sent and summed in bfloat16 or wider, within the bound.
No kernel may reach another device: no remote copies, remote signals or barrier semaphores. Data moves between devices by JAX's collectives and lax.ppermute only.
A program may use at most 192 MiB of HBM per device.

```python
import jax
import jax.numpy as jnp
from jax import lax

D = 1024
MH = 24
PH = 64
NS = 128
KC = 4
AH = 8
KVH = 2
HD = 64
FF = 2048
LEN = 1024
SBLK = 256
QBLK = 512
DSSM = 1536
ROWS = 2048
TOKENS = 16384
N_DP = 8


def steps_of(key, shape, cuts, smallest, largest):
    factor_of = 1.0
    for dim, blocks in cuts:
        steps = jax.random.uniform(jax.random.fold_in(jax.random.fold_in(key, 6), dim), (blocks,), jnp.float32, smallest / len(cuts), largest / len(cuts))
        factor_of = factor_of * jnp.repeat(jnp.exp(steps), shape[dim] // blocks).reshape((-1,) + (1,) * (len(shape) - 1 - dim))
    return factor_of


def noise(rng, dims, width, bound, split=(), kind=jnp.bfloat16):
    result = width * jax.random.normal(rng, dims, jnp.float32)
    if split:
        result = result * steps_of(rng, dims, split, -0.22, 0.18)
    return jnp.clip(result, -bound, bound).astype(kind)


def setup_inputs(seed: int = 0) -> dict:
    arg_keys = jax.random.split(jax.random.key(seed), 19)
    return {
        "residual": noise(arg_keys[0], (TOKENS, D), 1.0, 6.0, ((0, 32),)),
        "mixer_in": noise(arg_keys[1], (D, 2, DSSM), D ** -0.5, 0.1875, ((0, 8), (2, 4))),
        "step_in": noise(arg_keys[2], (D, MH), D ** -0.5, 0.1875, ((0, 8), (1, 4))),
        "shared_in": noise(arg_keys[3], (D, 2 * NS), D ** -0.5, 0.1875, ((0, 8), (1, 4))),
        "query_in": noise(arg_keys[4], (D, AH * HD), D ** -0.5, 0.1875, ((0, 8), (1, 4))),
        "keyval_in": noise(arg_keys[5], (D, 2 * KVH * HD), D ** -0.5, 0.1875, ((0, 8), (1, 4))),
        "mixer_proj": noise(arg_keys[6], (DSSM, D), DSSM ** -0.5, 0.15625, ((0, 4), (1, 8))),
        "attn_proj": noise(arg_keys[7], (AH * HD, D), (AH * HD // 16) ** -0.5, 1.0, ((0, 4), (1, 8))),
        "gate_up": noise(arg_keys[8], (D, 2, FF), D ** -0.5, 0.1875, ((0, 8), (2, 4))),
        "down_proj": noise(arg_keys[9], (FF, D), FF ** -0.5, 0.125, ((0, 4), (1, 8))),
        "norm_gain": jnp.clip(1.0 + 0.1 * jax.random.normal(arg_keys[10], (D,), jnp.float32), 0.5, 1.5),
        "mlp_gain": jnp.clip(1.0 + 0.1 * jax.random.normal(arg_keys[11], (D,), jnp.float32), 0.5, 1.5),
        "conv_filter": noise(arg_keys[12], (KC, DSSM + 2 * NS), KC ** -0.5, 3.0, (), jnp.float32),
        "decay_log": jnp.clip(jax.random.uniform(arg_keys[13], (MH,), jnp.float32, -2.0, 1.5), -2.0, 1.5),
        "skip_gain": jnp.clip(jax.random.uniform(arg_keys[14], (MH,), jnp.float32, 0.5, 1.5), 0.5, 1.5),
        "step_bias": jnp.clip(jax.random.uniform(arg_keys[15], (MH,), jnp.float32, -5.0, -1.0), -5.0, -1.0),
        "gated_gain": jnp.clip(1.0 + 0.1 * jax.random.normal(arg_keys[16], (DSSM,), jnp.float32), 0.5, 1.5),
        "cotangent": noise(arg_keys[17], (TOKENS, D), 1.0, 6.0, ((0, 32),)),
    }


epsilon = 1e-05
rope_base = 100000000000.0
masked_fill = -1e+30
highest = lax.Precision.HIGHEST

@jax.custom_vjp
def low(v):
    return lax.optimization_barrier(v.astype(jnp.bfloat16)).astype(jnp.float32)

@jax.custom_vjp
def low_back(v):
    return v

def low_keep(v):
    return (low(v), None)

def low_pass(kept, grad):
    return (grad,)

def back_keep(v):
    return (v, None)

def back_low(kept, grad):
    return (low(grad),)
low.defvjp(low_keep, low_pass)
low_back.defvjp(back_keep, back_low)

def product(left, right):
    return jnp.dot(left, right, precision=highest, preferred_element_type=jnp.float32)

def normalize(values):
    return values * lax.rsqrt(lax.optimization_barrier(jnp.mean(values * values, axis=-1, keepdims=True)) + epsilon)

def state_scan(block_item):
    head_in, step_size, log_decay, matrix_b, matrix_c = block_item
    local_heads = head_in.shape[1]
    block_count = LEN // SBLK
    weighted = (head_in * step_size[:, :, None]).reshape(block_count, SBLK, local_heads, PH)
    decay_blocks = log_decay.reshape(block_count, SBLK, local_heads)
    b_blocks = matrix_b.reshape(block_count, SBLK, NS)
    c_blocks = matrix_c.reshape(block_count, SBLK, NS)
    cumulated = jnp.cumsum(decay_blocks, axis=1)
    position = jnp.arange(SBLK, dtype=jnp.int32)
    causal = position[:, None] >= position[None, :]
    gaps = cumulated[:, :, None, :] - cumulated[:, None, :, :]
    decays = jnp.exp(jnp.where(causal[None, :, :, None], gaps, masked_fill))
    affinity = jnp.einsum('bin,bjn->bij', c_blocks, b_blocks, precision=highest)
    inside = jnp.einsum('bijh,bjhp->bihp', affinity[:, :, :, None] * decays, weighted, precision=highest)
    to_end = jnp.exp(cumulated[:, -1:, :] - cumulated)
    states = jnp.einsum('bjh,bjhp,bjn->bhpn', to_end, weighted, b_blocks, precision=highest)
    block_fall = jnp.exp(cumulated[:, -1, :])

    def carry_step(state_now, pair_item):
        fall_now, added = pair_item
        return (fall_now[:, None, None] * state_now + added, state_now)
    _, entering = lax.scan(carry_step, jnp.zeros((local_heads, PH, NS), jnp.float32), (block_fall, states))
    carried = jnp.einsum('bin,bhpn->bihp', c_blocks, entering, precision=highest) * jnp.exp(cumulated)[:, :, :, None]
    return (inside + carried).reshape(LEN, local_heads, PH)

def mamba_inner(gate_mix, value_mix, shared_proj, step_proj, conv_filter, step_bias, decay_log, skip_gain):
    row_total, local_width = value_mix.shape
    local_heads = step_proj.shape[1]
    seq_count = row_total // LEN
    joined = jnp.concatenate([value_mix, shared_proj], axis=1).reshape(seq_count, LEN, local_width + 2 * NS)
    padded = jnp.pad(joined, ((0, 0), (KC - 1, 0), (0, 0)))
    convolved = padded[:, 0:LEN, :] * conv_filter[0]
    for offset in range(1, KC):
        convolved = convolved + padded[:, offset:offset + LEN, :] * conv_filter[offset]
    activated = jax.nn.silu(convolved)
    head_in = activated[:, :, :local_width].reshape(seq_count, LEN, local_heads, PH)
    matrix_b = activated[:, :, local_width:local_width + NS]
    matrix_c = activated[:, :, local_width + NS:]
    step_size = jax.nn.softplus(step_proj.reshape(seq_count, LEN, local_heads) + step_bias)
    log_decay = -jnp.exp(decay_log) * step_size
    scanned = lax.map(jax.checkpoint(state_scan), (head_in, step_size, log_decay, matrix_b, matrix_c))
    scanned = scanned + skip_gain[:, None] * head_in
    return scanned.reshape(row_total, local_width) * jax.nn.silu(gate_mix)

def rotary(tensor_in):
    half_size = HD // 2
    frequency = rope_base ** (-2.0 * jnp.arange(half_size, dtype=jnp.float32) / HD)
    angles = jnp.arange(LEN, dtype=jnp.float32)[:, None] * frequency[None, :]
    cosine = jnp.cos(angles)[None, :, None, :]
    sine = jnp.sin(angles)[None, :, None, :]
    front_half = tensor_in[..., :half_size]
    back_half = tensor_in[..., half_size:]
    return jnp.concatenate([front_half * cosine - back_half * sine, back_half * cosine + front_half * sine], axis=-1)

def attend(query_proj, keyval_proj):
    row_total = query_proj.shape[0]
    seq_count = row_total // LEN
    query_heads = query_proj.shape[1] // HD
    key_heads = keyval_proj.shape[1] // (2 * HD)
    group_size = query_heads // key_heads
    queries = rotary(query_proj.reshape(seq_count, LEN, query_heads, HD))
    key_value = keyval_proj.reshape(seq_count, LEN, key_heads, 2, HD)
    keys_rot = jnp.repeat(rotary(key_value[:, :, :, 0]), group_size, axis=2)
    values = jnp.repeat(key_value[:, :, :, 1], group_size, axis=2)
    score_scale = HD ** (-0.5)

    def one_seq(seq_item):
        seq_queries, seq_keys, seq_values = seq_item

        def one_block(first_row):
            block_queries = lax.dynamic_slice_in_dim(seq_queries, first_row, QBLK, 0)
            scores = jnp.einsum('qhd,khd->hqk', block_queries, seq_keys, precision=highest) * score_scale
            visible = (first_row + jnp.arange(QBLK, dtype=jnp.int32))[:, None] >= jnp.arange(LEN, dtype=jnp.int32)[None, :]
            scores = jnp.where(visible[None], scores, masked_fill)
            row_max = lax.optimization_barrier(jnp.max(scores, axis=-1, keepdims=True))
            weights = jnp.exp(scores - row_max)
            weights = weights / lax.optimization_barrier(jnp.sum(weights, axis=-1, keepdims=True))
            return jnp.einsum('hqk,khd->qhd', weights, seq_values, precision=highest)
        starts = jnp.arange(LEN // QBLK, dtype=jnp.int32) * QBLK
        return lax.map(jax.checkpoint(one_block), starts).reshape(LEN, query_heads, HD)
    attended = lax.map(one_seq, (queries, keys_rot, values))
    return attended.reshape(row_total, query_heads * HD)

def layer(group_rows, parameters):
    mixer_in, step_in, shared_in, query_in, keyval_in, mixer_proj, attn_proj, gate_up, down_proj, norm_gain, mlp_gain, conv_filter, decay_log, skip_gain, step_bias, gated_gain = parameters
    normed_in = low(normalize(group_rows) * norm_gain)
    mixed = low_back(product(normed_in, mixer_in.reshape(D, 2 * DSSM)))
    gate_mix = mixed[:, :DSSM]
    value_mix = mixed[:, DSSM:]
    shared_proj = low_back(product(normed_in, shared_in))
    step_proj = low_back(product(normed_in, step_in))
    query_proj = low_back(product(normed_in, query_in))
    keyval_proj = low_back(product(normed_in, keyval_in))
    gated_pre = mamba_inner(gate_mix, value_mix, shared_proj, step_proj, conv_filter, step_bias, decay_log, skip_gain)
    mixer_heads = low(normalize(gated_pre) * gated_gain)
    attn_heads = low(attend(query_proj, keyval_proj))
    middle = group_rows + low_back(product(mixer_heads, mixer_proj) + product(attn_heads, attn_proj))
    mlp_rows = low(normalize(middle) * mlp_gain)
    gate_both = low_back(product(mlp_rows, gate_up.reshape(D, 2 * FF)))
    hidden = low(jax.nn.silu(gate_both[:, :FF]) * gate_both[:, FF:])
    return middle + low_back(product(hidden, down_proj))

def reference(residual, mixer_in, step_in, shared_in, query_in, keyval_in, mixer_proj, attn_proj, gate_up, down_proj, norm_gain, mlp_gain, conv_filter, decay_log, skip_gain, step_bias, gated_gain, cotangent):
    parameters = tuple((item.astype(jnp.float32) for item in (mixer_in, step_in, shared_in, query_in, keyval_in, mixer_proj, attn_proj, gate_up, down_proj, norm_gain, mlp_gain, conv_filter, decay_log, skip_gain, step_bias, gated_gain)))

    def forward(residual_f, *weights_f):

        def one_group(group_rows):
            return layer(group_rows, weights_f)
        groups = residual_f.reshape(N_DP, ROWS, D)
        return lax.map(jax.checkpoint(one_group), groups).reshape(TOKENS, D)
    output, backward = jax.vjp(forward, residual.astype(jnp.float32), *parameters)
    grads = backward(cotangent.astype(jnp.float32))
    return (output, grads[0], grads[1], grads[2], grads[3], grads[4], grads[5], grads[6], grads[7], grads[8], grads[9], grads[10], grads[11], grads[12], grads[13], grads[14], grads[15], grads[16])
```

```python
import functools

import jax
import jax.numpy as jnp
from jax import lax
from jax.experimental import pallas as pl
from jax.experimental.pallas import tpu as pltpu
from jax.sharding import PartitionSpec as P

PH = 64
NS = 128
KC = 4
AH = 8
KVH = 2
HD = 64
LEN = 1024
CHUNK = 128
HALO = 16
GROUP = 4
GW = GROUP * PH

epsilon = 1e-05
rope_base = 100000000000.0
masked_fill = -1e30
highest = lax.Precision.HIGHEST
f32 = jnp.float32
bf16 = jnp.bfloat16
VMEM_BYTES = 52 * 1024 * 1024


def call(kernel, grid, in_specs, out_specs, out_shape, scratch=(), flops=0, moved=0):
    return pl.pallas_call(
        kernel,
        grid=grid,
        in_specs=in_specs,
        out_specs=out_specs,
        out_shape=out_shape,
        scratch_shapes=list(scratch),
        compiler_params=pltpu.CompilerParams(
            vmem_limit_bytes=VMEM_BYTES, dimension_semantics=("arbitrary",) * len(grid)
        ),
        cost_estimate=pl.CostEstimate(flops=flops, bytes_accessed=moved, transcendentals=0),
    )


def spec(block, index):
    return pl.BlockSpec(block, index)


def shape(dims, kind):
    return jax.ShapeDtypeStruct(dims, kind)


def dot(left, right, dims):
    return lax.dot_general(left, right, ((dims[:1], dims[1:]), ((), ())), preferred_element_type=f32)


NN = (1, 0)
NT = (1, 1)
TN = (0, 0)


def sigmoid(value):
    return 1.0 / (1.0 + jnp.exp(-value))


def pair_lanes(left, right, rows):
    lane = lax.broadcasted_iota(jnp.int32, (rows, 2 * PH), 1)
    return jnp.where(lane < PH, left, right)


def spread_heads(columns, first, count, rows):
    parts = [
        pair_lanes(
            columns[:, first + 2 * p : first + 2 * p + 1],
            columns[:, first + 2 * p + 1 : first + 2 * p + 2],
            rows,
        )
        for p in range(count // 2)
    ]
    return jnp.concatenate(parts, axis=1) if len(parts) > 1 else parts[0]


def conv_of(ref, taps, rows):
    total = ref[pl.ds(HALO - KC + 1, rows), :] * taps[0:1, :]
    for offset in range(1, KC):
        total = total + ref[pl.ds(HALO - KC + 1 + offset, rows), :] * taps[offset : offset + 1, :]
    return total


def causal_mask(transposed):
    row = lax.broadcasted_iota(jnp.int32, (CHUNK, CHUNK), 0)
    col = lax.broadcasted_iota(jnp.int32, (CHUNK, CHUNK), 1)
    return col >= row if transposed else row >= col


def mixer_kernel(
    val_ref, shr_ref, tapv_ref, taps_ref, cumc_ref, cumr_ref, dt_ref, skip_ref,
    y_ref, state_ref, bc_ref, aff_ref,
):
    rows = y_ref.shape[0]
    chunks = rows // CHUNK

    @pl.when(pl.program_id(0) == 0)
    def _():
        pre = conv_of(shr_ref, taps_ref[...], rows)
        bc_ref[...] = (pre * sigmoid(pre)).astype(bf16)
        for c in range(chunks):
            sl = pl.ds(c * CHUNK, CHUNK)
            aff_ref[c] = dot(bc_ref[sl, NS:], bc_ref[sl, :NS], NT)

    pre = conv_of(val_ref, tapv_ref[...], rows)
    head_in = pre * sigmoid(pre)
    mask = causal_mask(False)
    skip = skip_ref[...]
    state = jnp.zeros((NS, GW), f32)
    for c in range(chunks):
        sl = pl.ds(c * CHUNK, CHUNK)
        x = head_in[c * CHUNK : (c + 1) * CHUNK]
        cumc = cumc_ref[0, sl, :]
        cumr = cumr_ref[0, :, sl]
        dt = dt_ref[0, sl, :]
        w = x * spread_heads(dt, 0, GROUP, CHUNK)
        w_low = w.astype(bf16)
        inner = []
        for p in range(GROUP // 2):
            both = []
            for h in (2 * p, 2 * p + 1):
                gap = cumc[:, h : h + 1] - cumr[h : h + 1, :]
                decay = jnp.exp(jnp.where(mask, gap, masked_fill))
                weight = (aff_ref[c] * decay).astype(bf16)
                both.append(dot(weight, w_low[:, p * 2 * PH : (p + 1) * 2 * PH], NN))
            inner.append(pair_lanes(both[0], both[1], CHUNK))
        out = jnp.concatenate(inner, axis=1) + skip * x
        b_now = bc_ref[sl, :NS]
        c_now = bc_ref[sl, NS:]
        last = cumc[CHUNK - 1 : CHUNK, :]
        if c > 0:
            grown = spread_heads(jnp.exp(cumc), 0, GROUP, CHUNK)
            out = out + dot(c_now, state.astype(bf16), NN) * grown
        y_ref[sl, :] = out
        to_end = spread_heads(jnp.exp(last - cumc), 0, GROUP, CHUNK)
        added = dot(b_now, (w * to_end).astype(bf16), TN)
        fall = spread_heads(jnp.exp(last), 0, GROUP, 1)
        state = state * fall + added
    state_ref[...] = state


def finish_kernel(y_ref, gate_ref, bc_ref, grow_ref, state_ref, gain_ref, scan_ref, heads_ref):
    rows, width = y_ref.shape
    grown = spread_heads(grow_ref[...], 0, width // PH, rows)
    scan = y_ref[...] + dot(bc_ref[:, NS:], state_ref[...].astype(bf16), NN) * grown
    scan_ref[...] = scan
    gate = gate_ref[...]
    pre = scan * gate * sigmoid(gate)
    inv = lax.rsqrt(jnp.mean(pre * pre, axis=1, keepdims=True) + epsilon)
    heads_ref[...] = (pre * inv * gain_ref[...]).astype(bf16)


def ungate_kernel(
    ga_ref, gb_ref, scan_ref, gate_ref, bc_ref, grow_ref, gain_ref,
    dgate_ref, dscan_ref, dgain_ref, dstate_ref,
):
    rows, width = scan_ref.shape
    scan = scan_ref[...]
    gate = gate_ref[...]
    sig = sigmoid(gate)
    silu = gate * sig
    pre = scan * silu
    inv = lax.rsqrt(jnp.mean(pre * pre, axis=1, keepdims=True) + epsilon)
    normed = pre * inv
    grad = jnp.concatenate([ga_ref[...], gb_ref[...]], axis=1)
    u = grad * gain_ref[...]
    cross = jnp.mean(u * normed, axis=1, keepdims=True)
    dpre = inv * (u - normed * cross)
    dscan = dpre * silu
    dgate_ref[...] = (dpre * scan * sig * (1.0 + gate * (1.0 - sig))).astype(bf16)
    dscan_ref[...] = dscan
    grown = spread_heads(grow_ref[...], 0, width // PH, rows)
    dstate = dot(bc_ref[:, NS:], (dscan * grown).astype(bf16), TN)
    dgain = jnp.sum(grad * normed, axis=0, keepdims=True)
    first = pl.program_id(0) == 0

    @pl.when(first)
    def _():
        dgain_ref[...] = dgain
        dstate_ref[...] = dstate

    @pl.when(jnp.logical_not(first))
    def _():
        dgain_ref[...] += dgain
        dstate_ref[...] += dstate


def split_sum(value, ones_at):
    high = value.astype(bf16)
    low = (value - high.astype(f32)).astype(bf16)
    return dot(high, ones_at, NN) + dot(low, ones_at, NN)


def unconv(ref, taps, dact, pad_ref, out_ref, dtaps_ref, rows):
    pre = conv_of(ref, taps, rows)
    sig = sigmoid(pre)
    dpre = dact * sig * (1.0 + pre * (1.0 - sig))
    lead = HALO + 8
    width = dact.shape[1]
    pad_ref[pl.ds(0, lead), :] = jnp.zeros((lead, width), f32)
    pad_ref[pl.ds(lead + rows, 8), :] = jnp.zeros((8, width), f32)
    pad_ref[pl.ds(lead, rows), :] = dpre
    total = None
    dtaps = []
    for offset in range(KC):
        part = pad_ref[pl.ds(8 + KC - 1 - offset, rows + HALO), :] * taps[offset : offset + 1, :]
        total = part if total is None else total + part
        moved = ref[pl.ds(HALO - KC + 1 + offset, rows), :]
        dtaps.append(jnp.sum(dpre * moved, axis=0, keepdims=True))
    out_ref[...] = total.astype(bf16)
    dtaps_ref[...] = jnp.concatenate(dtaps, axis=0)


def unmix_kernel(
    val_ref, shr_ref, tapv_ref, taps_ref, cumc_ref, cumr_ref, dt_ref, skip_ref, bc_ref,
    dscan_ref, enter_ref, dleave_ref,
    dval_ref, dshr_ref, cols_ref, rows_ref, dlast_ref, dtapv_ref, dtaps_ref, dskip_ref,
    aff_ref, daff_ref, dbc_ref, dx_ref, states_ref, pad_ref,
):
    rows = dscan_ref.shape[0]
    chunks = rows // CHUNK
    step = pl.program_id(0)

    @pl.when(step == 0)
    def _():
        for c in range(chunks):
            sl = pl.ds(c * CHUNK, CHUNK)
            aff_ref[c] = dot(bc_ref[sl, :NS], bc_ref[sl, NS:], NT)
        daff_ref[...] = jnp.zeros(daff_ref.shape, f32)
        dbc_ref[...] = jnp.zeros(dbc_ref.shape, f32)

    pre = conv_of(val_ref, tapv_ref[...], rows)
    dx_ref[...] = pre * sigmoid(pre)
    mask = causal_mask(True)
    skip = skip_ref[...]
    lane = lax.broadcasted_iota(jnp.int32, (GW, 2 * GROUP), 0) // PH
    slot = lax.broadcasted_iota(jnp.int32, (GW, 2 * GROUP), 1)
    ones_dt = jnp.where(lane == slot, 1.0, 0.0).astype(bf16)
    ones_cum = jnp.where(lane + GROUP == slot, 1.0, 0.0).astype(bf16)
    half_lane = lax.broadcasted_iota(jnp.int32, (CHUNK, 2 * PH), 1) // PH
    slot_lane = lax.broadcasted_iota(jnp.int32, (CHUNK, 2 * GROUP), 1)

    state = enter_ref[...]
    states_ref[0] = state
    for c in range(chunks - 1):
        sl = pl.ds(c * CHUNK, CHUNK)
        cumc = cumc_ref[0, sl, :]
        last = cumc[CHUNK - 1 : CHUNK, :]
        scale = spread_heads(dt_ref[0, sl, :] * jnp.exp(last - cumc), 0, GROUP, CHUNK)
        added = dot(bc_ref[sl, :NS], (dx_ref[sl, :] * scale).astype(bf16), TN)
        state = state * spread_heads(jnp.exp(last), 0, GROUP, 1) + added
        states_ref[c + 1] = state

    dstate = dleave_ref[...]
    dskip = jnp.zeros((1, GW), f32)
    for c in reversed(range(chunks)):
        sl = pl.ds(c * CHUNK, CHUNK)
        x = dx_ref[sl, :]
        dy = dscan_ref[sl, :]
        dy_low = dy.astype(bf16)
        cumc = cumc_ref[0, sl, :]
        cumr = cumr_ref[0, :, sl]
        last = cumc[CHUNK - 1 : CHUNK, :]
        dt = spread_heads(dt_ref[0, sl, :], 0, GROUP, CHUNK)
        w = x * dt
        w_low = w.astype(bf16)
        b_now = bc_ref[sl, :NS]
        c_now = bc_ref[sl, NS:]
        affinity = aff_ref[c]
        dcum = jnp.zeros((CHUNK, 2 * GROUP), f32)
        daff = daff_ref[c]
        dw_parts = []
        for p in range(GROUP // 2):
            pair = slice(p * 2 * PH, (p + 1) * 2 * PH)
            both = []
            for h in (2 * p, 2 * p + 1):
                gap = cumr[h : h + 1, :] - cumc[:, h : h + 1]
                decay = jnp.exp(jnp.where(mask, gap, masked_fill))
                weight = affinity * decay
                w_own = jnp.where(half_lane == h - 2 * p, w[:, pair], 0.0).astype(bf16)
                dweight = dot(w_own, dy_low[:, pair], NT)
                daff = daff + dweight * decay
                moved = dweight * weight
                rows_ref[0, h : h + 1, sl] = jnp.sum(moved, axis=0, keepdims=True)
                dcum = dcum - jnp.where(
                    slot_lane == GROUP + h, jnp.sum(moved, axis=1, keepdims=True), 0.0
                )
                both.append(dot(weight.astype(bf16), dy_low[:, pair], NN))
            dw_parts.append(pair_lanes(both[0], both[1], CHUNK))
        daff_ref[c] = daff
        state = states_ref[c]
        state_low = state.astype(bf16)
        dstate_low = dstate.astype(bf16)
        grown = spread_heads(jnp.exp(cumc), 0, GROUP, CHUNK)
        to_end = spread_heads(jnp.exp(last - cumc), 0, GROUP, CHUNK)
        fall = spread_heads(jnp.exp(last), 0, GROUP, 1)
        dy_grown = (dy * grown).astype(bf16)
        carried = dot(c_now, state_low, NN) * grown
        from_end = dot(b_now, dstate_low, NN) * to_end
        dbc_ref[sl, NS:] += dot(dy_grown, state_low, NT)
        dbc_ref[sl, :NS] += dot((w * to_end).astype(bf16), dstate_low, NT)
        dw = jnp.concatenate(dw_parts, axis=1) + from_end
        ended = w * from_end
        cols_ref[0, sl, :] = (
            dcum + split_sum(dw * x, ones_dt) + split_sum(dy * carried - ended, ones_cum)
        )
        dlast_ref[c : c + 1, :] = jnp.sum(ended, axis=0, keepdims=True) + fall * jnp.sum(
            state * dstate, axis=0, keepdims=True
        )
        dstate = fall * dstate + dot(c_now, dy_grown, TN)
        dskip = dskip + jnp.sum(dy * x, axis=0, keepdims=True)
        dx_ref[sl, :] = dw * dt + skip * dy
    dskip_ref[...] = dskip
    unconv(val_ref, tapv_ref[...], dx_ref[...], pad_ref, dval_ref, dtapv_ref, rows)

    @pl.when(step == pl.num_programs(0) - 1)
    def _():
        for c in range(chunks):
            sl = pl.ds(c * CHUNK, CHUNK)
            daff_low = daff_ref[c].astype(bf16)
            dbc_ref[sl, :NS] += dot(daff_low, bc_ref[sl, NS:], NN)
            dbc_ref[sl, NS:] += dot(daff_low, bc_ref[sl, :NS], TN)
        unconv(shr_ref, taps_ref[...], dbc_ref[...], pad_ref, dshr_ref, dtaps_ref, rows)


def swap_halves(value):
    half = HD // 2
    width = value.shape[1]
    lane = lax.broadcasted_iota(jnp.int32, value.shape, 1) % HD
    return jnp.where(
        lane < half, pltpu.roll(value, width - half, 1), pltpu.roll(value, half, 1)
    )


def rotate_kernel(value_ref, cos_ref, sin_ref, out_ref):
    value = value_ref[...]
    out_ref[...] = (value * cos_ref[...] + swap_halves(value) * sin_ref[...]).astype(bf16)


def unrotate_kernel(own_ref, late_ref, cos_ref, sin_ref, out_ref):
    value = own_ref[...] + late_ref[...].astype(f32)
    out_ref[...] = (value * cos_ref[...] + swap_halves(value * sin_ref[...])).astype(bf16)


def head_queries(query, which):
    lane = lax.broadcasted_iota(jnp.int32, query.shape, 1)
    moved = pltpu.roll(query, HD, 1) if which else query
    return jnp.where(lane < HD, moved, 0.0)


def score_weights(query, before, own, allowed):
    early = jnp.where(allowed, dot(query, before, NT), masked_fill)
    late = dot(query, own, NT)
    row = lax.broadcasted_iota(jnp.int32, late.shape, 0)
    col = lax.broadcasted_iota(jnp.int32, late.shape, 1)
    late = jnp.where(row >= col, late, masked_fill)
    top = jnp.maximum(
        jnp.max(early, axis=1, keepdims=True), jnp.max(late, axis=1, keepdims=True)
    )
    early = jnp.exp(early - top)
    late = jnp.exp(late - top)
    total = jnp.sum(early, axis=1, keepdims=True) + jnp.sum(late, axis=1, keepdims=True)
    return early, late, 1.0 / total


def rotated_queries(q_ref, cos_ref, sin_ref):
    query = q_ref[...]
    return (query * cos_ref[...] + swap_halves(query) * sin_ref[...]) * (HD**-0.5)


def attend_kernel(part_ref, q_ref, cos_ref, sin_ref, before_ref, own_ref, out_ref):
    allowed = part_ref[0] > 0
    query = rotated_queries(q_ref, cos_ref, sin_ref)
    before = before_ref[...]
    own = own_ref[...]
    results = []
    for which in range(2):
        q_low = head_queries(query, which).astype(bf16)
        early, late, scale = score_weights(q_low, before, own, allowed)
        result = dot(early.astype(bf16), before, NN) + dot(late.astype(bf16), own, NN)
        results.append(result * scale)
    out_ref[...] = pair_lanes(pltpu.roll(results[0], HD, 1), results[1], query.shape[0]).astype(
        bf16
    )


def unattend_kernel(
    part_ref, q_ref, cos_ref, sin_ref, before_ref, own_ref, dout_ref,
    dq_ref, dbefore_ref, down_ref,
):
    allowed = part_ref[0] > 0
    query = rotated_queries(q_ref, cos_ref, sin_ref)
    before = before_ref[...]
    own = own_ref[...]
    dout = dout_ref[...]
    lane = lax.broadcasted_iota(jnp.int32, dout.shape, 1)
    dqs = []
    dbefore = None
    down = None
    for which in range(2):
        q_low = head_queries(query, which).astype(bf16)
        early, late, scale = score_weights(q_low, before, own, allowed)
        early = early * scale
        late = late * scale
        dout_own = dout if which else pltpu.roll(dout, HD, 1)
        dout_low = jnp.where(lane >= HD, dout_own, 0.0).astype(bf16)
        dearly = dot(dout_low, before, NT)
        dlate = dot(dout_low, own, NT)
        cross = jnp.sum(early * dearly, axis=1, keepdims=True) + jnp.sum(
            late * dlate, axis=1, keepdims=True
        )
        dearly = (early * (dearly - cross)).astype(bf16)
        dlate = (late * (dlate - cross)).astype(bf16)
        dqs.append(dot(dearly, before, NN) + dot(dlate, own, NN))
        part_before = dot(dearly, q_low, TN) + dot(early.astype(bf16), dout_low, TN)
        part_own = dot(dlate, q_low, TN) + dot(late.astype(bf16), dout_low, TN)
        dbefore = part_before if dbefore is None else dbefore + part_before
        down = part_own if down is None else down + part_own
    dq = pair_lanes(dqs[0], pltpu.roll(dqs[1], HD, 1), dout.shape[0]) * (HD**-0.5)
    dq_ref[...] = (dq * cos_ref[...] + swap_halves(dq * sin_ref[...])).astype(bf16)
    first = lax.rem(pl.program_id(0), AH // KVH // 2) == 0

    @pl.when(first)
    def _():
        dbefore_ref[...] = dbefore
        down_ref[...] = down

    @pl.when(jnp.logical_not(first))
    def _():
        dbefore_ref[...] += dbefore
        down_ref[...] += down


def matmul(left, right, dims=NN):
    return dot(left, right, dims)


def partner(value, bit):
    count = lax.axis_size("dp")
    return lax.ppermute(value, "dp", [(i, i ^ (1 << bit)) for i in range(count)])


def bit_axes():
    bits = lax.axis_size("dp").bit_length() - 1
    return [0] + list(range(bits - 1, 0, -1))


def stages(flip):
    bits = lax.axis_size("dp").bit_length() - 1
    high = list(range(1, bits))
    return (high[::-1] if flip else high) + [0]


def spread(piece, flip):
    axes = bit_axes()
    held = piece.reshape((1,) * len(axes) + piece.shape)
    for bit in stages(flip):
        held = jnp.concatenate([held, partner(held, bit)], axis=axes.index(bit))
    return held.reshape((-1,) + piece.shape[1:])


def collect(keep, send, flip):
    axes = bit_axes()[1:]
    got = partner(send.astype(bf16), 0)
    held = (keep + got.astype(f32)).astype(bf16)
    held = held.reshape((2,) * len(axes) + (-1,) + held.shape[1:])
    for bit in stages(flip)[:-1][::-1]:
        axis = axes.index(bit)
        mine = lax.slice_in_dim(held, 0, 1, axis=axis)
        theirs = lax.slice_in_dim(held, 1, 2, axis=axis)
        held = (mine.astype(f32) + partner(theirs, bit).astype(f32)).astype(bf16)
    return held.reshape(held.shape[-2:])


def block_sources():
    count = lax.axis_size("dp")
    half = count // 2
    me = lax.axis_index("dp")
    return [me ^ (((p % half) << 1) | (p // half)) for p in range(count)]


def block_places():
    count = lax.axis_size("dp")
    me = lax.axis_index("dp")
    return [((me ^ b) >> 1) | (((me ^ b) & 1) * (count // 2)) for b in range(count)]


def take_blocks(value, sources):
    width = value.shape[-1] // len(sources)
    axis = value.ndim - 1
    return jnp.concatenate(
        [lax.dynamic_slice_in_dim(value, s * width, width, axis) for s in sources], axis=axis
    )


def permute_features(value):
    return take_blocks(value, block_sources())


def restore_features(value):
    return take_blocks(value, block_places())


def norm_of(rows):
    inv = lax.rsqrt(jnp.mean(rows * rows, axis=-1, keepdims=True) + epsilon)
    return rows * inv, inv


def norm_back(grad, gain, normed, inv):
    scaled = grad * gain
    return inv * (scaled - normed * jnp.mean(scaled * normed, axis=-1, keepdims=True))


def over_tensor(piece):
    return lax.all_gather(piece, "tensor", axis=0)


def columns_of(gathered, start, stop):
    part = gathered[:, :, start:stop]
    count, rows, width = part.shape
    return part.transpose(1, 0, 2).reshape(rows, count * width)


def split_columns(value, count):
    rows, width = value.shape
    return value.reshape(rows, count, width // count).transpose(1, 0, 2)


def shards(
    residual,
    mixer_in,
    step_in,
    shared_in,
    query_in,
    keyval_in,
    mixer_proj,
    attn_proj,
    gate_up,
    down_proj,
    norm_gain,
    mlp_gain,
    conv_filter,
    decay_log,
    skip_gain,
    step_bias,
    gated_gain,
    cotangent,
):
    tensor_count = lax.axis_size("tensor")
    rows, model = residual.shape
    depth = mixer_in.shape[0]
    ssm = conv_filter.shape[1] - 2 * NS
    heads = ssm // PH
    groups = heads // GROUP
    chunks = rows // CHUNK
    span = LEN // rows
    part = lax.axis_index("tensor") % span
    onward = [(i, i + 1) for i in range(tensor_count) if i % span != span - 1]
    backward = [(j, i) for i, j in onward]
    gate_w = mixer_in.shape[2]
    hidden_w = gate_up.shape[2]
    query_w = query_in.shape[1]
    shared_w = shared_in.shape[1]
    keyval_w = keyval_in.shape[1]
    step_w = step_in.shape[1]
    attn_w = AH * HD
    out_w = ssm + attn_w
    ff = hidden_w * tensor_count

    in_piece = over_tensor(
        jnp.concatenate(
            [mixer_in[:, 0], query_in, mixer_in[:, 1], shared_in, keyval_in, step_in], axis=1
        )
    )
    cuts = [0, gate_w, query_w, gate_w, shared_w, keyval_w, step_w]
    ends = [sum(cuts[: i + 1]) for i in range(len(cuts))]
    in_parts = [columns_of(in_piece, ends[i], ends[i + 1]) for i in range(6)]
    step_total = step_w * tensor_count
    step_pad = -step_total % 128
    in_a = spread(
        jnp.concatenate([in_parts[0], in_parts[1], jnp.pad(in_parts[5], ((0, 0), (0, step_pad)))], 1),
        False,
    )
    in_b = spread(jnp.concatenate(in_parts[2:5], axis=1), True)
    out_piece = over_tensor(jnp.concatenate([mixer_proj, attn_proj], axis=0).T)
    out_cut = mixer_proj.shape[0]
    out_all = jnp.concatenate(
        [columns_of(out_piece, 0, out_cut), columns_of(out_piece, out_cut, out_piece.shape[2])], 1
    )
    out_a = spread(out_all[:, : out_w // 2], False)
    out_b = spread(out_all[:, out_w // 2 :], True)
    ff_piece = over_tensor(gate_up.reshape(depth, 2 * hidden_w))
    gate_full = spread(columns_of(ff_piece, 0, hidden_w), False)
    up_full = spread(columns_of(ff_piece, hidden_w, 2 * hidden_w), True)
    down_all = columns_of(over_tensor(down_proj.T), 0, hidden_w)
    down_a = spread(down_all[:, : ff // 2], False)
    down_b = spread(down_all[:, ff // 2 :], True)

    before_rows = lax.ppermute(residual[rows - HALO :], "tensor", onward)
    ext_low = permute_features(jnp.concatenate([before_rows, residual], axis=0))
    cot = permute_features(cotangent)
    gain_first = permute_features(norm_gain)
    gain_second = permute_features(mlp_gain)
    ext_normed, ext_inv = norm_of(ext_low.astype(f32))
    ext_in = (ext_normed * gain_first).astype(bf16)
    normed_first = ext_normed[HALO:]
    inv_first = ext_inv[HALO:]
    normed_in = ext_in[HALO:]
    group_rows = ext_low[HALO:].astype(f32)
    proj_a = matmul(normed_in, in_a)
    proj_b = matmul(ext_in, in_b)

    step_proj = proj_a[:, ssm + attn_w : ssm + attn_w + heads]
    step_size = jax.nn.softplus(step_proj + step_bias)
    rate = jnp.exp(decay_log)
    log_decay = -rate * step_size
    lower = jnp.tril(jnp.ones((CHUNK, CHUNK), f32))
    cum = jnp.einsum(
        "ij,cjh->cih", lower, log_decay.reshape(chunks, CHUNK, heads), precision=highest
    )
    ends_of = cum[:, -1, :]
    prefix = jnp.concatenate([jnp.zeros((1, heads), f32), jnp.cumsum(ends_of, axis=0)[:-1]], 0)
    grow = jnp.exp(cum + prefix[:, None, :]).reshape(rows, heads)
    cum = cum.reshape(rows, heads)
    cum_cols = cum.reshape(rows, groups, GROUP).transpose(1, 0, 2)
    cum_rows = cum.T.reshape(groups, GROUP, rows)
    dt_cols = step_size.reshape(rows, groups, GROUP).transpose(1, 0, 2)
    skip_lanes = jnp.repeat(skip_gain, PH)[None, :]

    ext = rows + HALO
    val_spec = spec((ext, GW), lambda g: (0, g))
    shr_spec = spec((ext, 2 * NS), lambda g: (0, ssm // (2 * NS)))
    tapv_spec = spec((KC, GW), lambda g: (0, g))
    taps_spec = spec((KC, 2 * NS), lambda g: (0, ssm // (2 * NS)))
    col_spec = spec((1, rows, GROUP), lambda g: (g, 0, 0))
    row_spec = spec((1, GROUP, rows), lambda g: (g, 0, 0))
    lane_spec = spec((1, GW), lambda g: (0, g))
    bc_spec = spec((rows, 2 * NS), lambda g: (0, 0))
    grp_spec = spec((rows, GW), lambda g: (0, g))
    state_spec = spec((NS, GW), lambda g: (0, g))
    y_local, state_local, bc_act = call(
        mixer_kernel,
        (groups,),
        [val_spec, shr_spec, tapv_spec, taps_spec, col_spec, row_spec, col_spec, lane_spec],
        [grp_spec, state_spec, bc_spec],
        [shape((rows, ssm), f32), shape((NS, ssm), f32), shape((rows, 2 * NS), bf16)],
        [pltpu.VMEM((chunks, CHUNK, CHUNK), f32)],
        flops=2 * rows * ssm * 512,
        moved=rows * ssm * 8,
    )(proj_b, proj_b, conv_filter, conv_filter, cum_cols, cum_rows, dt_cols, skip_lanes)
    entering = lax.ppermute(state_local, "tensor", onward)

    half = HD // 2
    frequency = rope_base ** (-2.0 * jnp.arange(half, dtype=f32) / HD)
    place = (part * rows + jnp.arange(rows, dtype=jnp.int32)).astype(f32)
    angles = place[:, None] * frequency[None, :]
    cosine = jnp.cos(angles)
    sine = jnp.sin(angles)
    cos_q = jnp.concatenate([cosine] * 4, axis=1)
    sin_q = jnp.concatenate([-sine, sine] * 2, axis=1)
    ones = jnp.ones((rows, HD), f32)
    cos_kv = jnp.concatenate([cosine, cosine, ones] * KVH, axis=1)
    sin_kv = jnp.concatenate([-sine, sine, 0.0 * ones] * KVH, axis=1)
    kv_w = 2 * KVH * HD
    whole = lambda width: spec((rows, width), lambda i: (0, 0))
    own_kv = call(
        rotate_kernel,
        (1,),
        [whole(kv_w)] * 3,
        whole(kv_w),
        shape((rows, kv_w), bf16),
        moved=rows * kv_w * 12,
    )(proj_b[HALO:, ssm + 2 * NS :], cos_kv, sin_kv)
    before_kv = lax.ppermute(own_kv, "tensor", onward)
    part_arg = part.astype(jnp.int32).reshape(1)
    pairs = AH // 2
    per_kv = AH // KVH // 2
    smem = pl.BlockSpec(memory_space=pltpu.SMEM)
    q_spec = spec((rows, 2 * HD), lambda i: (0, ssm // (2 * HD) + i))
    table_spec = spec((rows, 2 * HD), lambda i: (0, 0))
    kv_spec = spec((rows, 2 * HD), lambda i: (0, i // per_kv))
    pair_spec = spec((rows, 2 * HD), lambda i: (0, i))
    attn_heads = call(
        attend_kernel,
        (pairs,),
        [smem, q_spec, table_spec, table_spec, kv_spec, kv_spec],
        pair_spec,
        shape((rows, attn_w), bf16),
        flops=2 * AH * rows * LEN * 256,
        moved=rows * attn_w * 8,
    )(part_arg, proj_a, cos_q, sin_q, before_kv, own_kv)

    block_rows = CHUNK
    wide = spec((block_rows, ssm), lambda i: (i, 0))
    bc_block = spec((block_rows, 2 * NS), lambda i: (i, 0))
    grow_block = spec((block_rows, heads), lambda i: (i, 0))
    state_whole = spec((NS, ssm), lambda i: (0, 0))
    gain_whole = spec((1, ssm), lambda i: (0, 0))
    gated_row = gated_gain[None, :]
    scanned, mixer_heads = call(
        finish_kernel,
        (rows // block_rows,),
        [wide, wide, bc_block, grow_block, state_whole, gain_whole],
        [wide, wide],
        [shape((rows, ssm), f32), shape((rows, ssm), bf16)],
        flops=2 * rows * ssm * NS,
        moved=rows * ssm * 14,
    )(y_local, proj_a, bc_act, grow, entering, gated_row)

    out_half = out_w // 2
    heads_a = mixer_heads[:, :out_half]
    heads_b = jnp.concatenate([mixer_heads[:, out_half:], attn_heads], axis=1)
    middle = group_rows + (matmul(heads_a, out_a, NT) + matmul(heads_b, out_b, NT))
    second_normed, inv_second = norm_of(middle)
    mlp_rows = (second_normed * gain_second).astype(bf16)
    gate_val = matmul(mlp_rows, gate_full)
    up_val = matmul(mlp_rows, up_full)
    sig_gate = jax.nn.sigmoid(gate_val)
    silu_gate = gate_val * sig_gate
    hidden = (silu_gate * up_val).astype(bf16)
    ff_half = ff // 2
    output = middle + (
        matmul(hidden[:, :ff_half], down_a, NT) + matmul(hidden[:, ff_half:], down_b, NT)
    )

    near = model // 2

    def weight_grad(left, right, flip):
        keep = matmul(left[:, :near], right, TN)
        send = matmul(left[:, near:], right, TN)
        return collect(keep, send, flip)

    down_sum_a = weight_grad(cot, hidden[:, :ff_half], False)
    down_sum_b = weight_grad(cot, hidden[:, ff_half:], True)
    hidden_grad = jnp.concatenate([matmul(cot, down_a), matmul(cot, down_b)], axis=1)
    gate_grad = (hidden_grad * up_val * sig_gate * (1.0 + gate_val * (1.0 - sig_gate))).astype(bf16)
    up_grad = (hidden_grad * silu_gate).astype(bf16)
    gate_sum = weight_grad(mlp_rows, gate_grad, False)
    up_sum = weight_grad(mlp_rows, up_grad, True)
    mlp_in_grad = matmul(gate_grad, gate_full, NT) + matmul(up_grad, up_full, NT)
    mlp_gain_part = jnp.sum(mlp_in_grad * second_normed, axis=0)
    middle_grad = cot.astype(f32) + norm_back(mlp_in_grad, gain_second, second_normed, inv_second)

    branch_grad = middle_grad.astype(bf16)
    heads_grad_a = matmul(branch_grad, out_a)
    heads_grad_b = matmul(branch_grad, out_b)
    out_sum_a = weight_grad(branch_grad, heads_a, False)
    out_sum_b = weight_grad(branch_grad, heads_b, True)
    gate_grad_mix, dscan, gated_gain_part, dstate_local = call(
        ungate_kernel,
        (rows // block_rows,),
        [
            spec((block_rows, out_half), lambda i: (i, 0)),
            spec((block_rows, ssm - out_half), lambda i: (i, 0)),
            wide, wide, bc_block, grow_block, gain_whole,
        ],
        [wide, wide, gain_whole, state_whole],
        [
            shape((rows, ssm), bf16),
            shape((rows, ssm), f32),
            shape((1, ssm), f32),
            shape((NS, ssm), f32),
        ],
        flops=2 * rows * ssm * NS,
        moved=rows * ssm * 18,
    )(heads_grad_a, heads_grad_b, scanned, proj_a, bc_act, grow, gated_row)
    leaving_grad = lax.ppermute(dstate_local, "tensor", backward)

    dout_spec = spec((rows, 2 * HD), lambda i: (0, (ssm - out_half) // (2 * HD) + i))
    query_low, before_grad, own_grad = call(
        unattend_kernel,
        (pairs,),
        [smem, q_spec, table_spec, table_spec, kv_spec, kv_spec, dout_spec],
        [pair_spec, kv_spec, kv_spec],
        [shape((rows, attn_w), bf16), shape((rows, kv_w), f32), shape((rows, kv_w), f32)],
        flops=2 * AH * rows * LEN * 640,
        moved=rows * attn_w * 16,
    )(part_arg, proj_a, cos_q, sin_q, before_kv, own_kv, heads_grad_b)
    late_grad = lax.ppermute(before_grad.astype(bf16), "tensor", backward)

    dval, dshr, dcols, drows, dlast, dtapv, dtaps, dskip = call(
        unmix_kernel,
        (groups,),
        [
            val_spec, shr_spec, tapv_spec, taps_spec, col_spec, row_spec, col_spec, lane_spec,
            bc_spec, grp_spec, state_spec, state_spec,
        ],
        [
            val_spec,
            spec((ext, 2 * NS), lambda g: (0, 0)),
            spec((1, rows, 2 * GROUP), lambda g: (g, 0, 0)),
            row_spec,
            spec((chunks, GW), lambda g: (0, g)),
            tapv_spec,
            spec((KC, 2 * NS), lambda g: (0, 0)),
            lane_spec,
        ],
        [
            shape((ext, ssm), bf16),
            shape((ext, 2 * NS), bf16),
            shape((groups, rows, 2 * GROUP), f32),
            shape((groups, GROUP, rows), f32),
            shape((chunks, ssm), f32),
            shape((KC, ssm), f32),
            shape((KC, 2 * NS), f32),
            shape((1, ssm), f32),
        ],
        [
            pltpu.VMEM((chunks, CHUNK, CHUNK), f32),
            pltpu.VMEM((chunks, CHUNK, CHUNK), f32),
            pltpu.VMEM((rows, 2 * NS), f32),
            pltpu.VMEM((rows, GW), f32),
            pltpu.VMEM((chunks, NS, GW), f32),
            pltpu.VMEM((rows + HALO + 16, GW), f32),
        ],
        flops=2 * rows * ssm * 1280,
        moved=rows * ssm * 12,
    )(
        proj_b, proj_b, conv_filter, conv_filter, cum_cols, cum_rows, dt_cols, skip_lanes,
        bc_act, dscan, entering, leaving_grad,
    )
    kv_low = call(
        unrotate_kernel,
        (1,),
        [whole(kv_w)] * 4,
        whole(kv_w),
        shape((rows, kv_w), bf16),
        moved=rows * kv_w * 16,
    )(own_grad, late_grad, cos_kv, sin_kv)

    by_head = dcols.transpose(1, 0, 2)
    dstep_direct = by_head[:, :, :GROUP].reshape(rows, heads)
    dcum = by_head[:, :, GROUP:].reshape(rows, heads) + drows.reshape(heads, rows).T
    dcum = dcum.reshape(chunks, CHUNK, heads)
    at_end = dlast.reshape(chunks, heads, PH).sum(axis=-1)
    dlog = jnp.einsum("ij,cih->cjh", lower, dcum, precision=highest) + at_end[:, None, :]
    dlog = dlog.reshape(rows, heads)
    decay_part = jnp.sum(dlog * log_decay, axis=0)
    dstep = (dstep_direct - rate * dlog) * jax.nn.sigmoid(step_proj + step_bias)
    bias_part = jnp.sum(dstep, axis=0)
    skip_part = dskip.reshape(heads, PH).sum(axis=-1)

    step_low = jnp.pad(dstep.astype(bf16), ((0, 0), (0, step_pad)))
    low_a = jnp.concatenate([gate_grad_mix, query_low, step_low], axis=1)
    low_b = jnp.concatenate([dval, dshr, jnp.pad(kv_low, ((HALO, 0), (0, 0)))], axis=1)
    in_sum_a = weight_grad(normed_in, low_a, False)
    in_sum_b = weight_grad(ext_in, low_b, True)
    grad_b = matmul(low_b, in_b, NT)
    late_rows = lax.ppermute(grad_b[:HALO], "tensor", backward)
    first_grad = grad_b[HALO:] + matmul(low_a, in_a, NT)
    first_grad = jnp.concatenate([first_grad[: rows - HALO], first_grad[rows - HALO :] + late_rows], 0)
    norm_gain_part = jnp.sum(first_grad * normed_first, axis=0)
    residual_grad = middle_grad + norm_back(first_grad, gain_first, normed_first, inv_first)

    def sum_tensor(parts):
        joined = jnp.concatenate([split_columns(p, tensor_count) for p in parts], axis=2)
        total = lax.psum_scatter(joined, "tensor", scatter_dimension=0, tiled=False)
        total = total.astype(f32)
        ends = [0]
        for p in parts:
            ends.append(ends[-1] + p.shape[1] // tensor_count)
        return [total[:, ends[i] : ends[i + 1]] for i in range(len(parts))]

    down_sum = jnp.concatenate([down_sum_a, down_sum_b], axis=1)
    (down_t,) = sum_tensor([down_sum])
    gate_up_sum = jnp.stack(sum_tensor([gate_sum, up_sum]), axis=1)
    mixer_t, attn_t = sum_tensor(
        [
            jnp.concatenate([out_sum_a, out_sum_b[:, : ssm - out_half]], axis=1),
            out_sum_b[:, ssm - out_half :],
        ]
    )
    in_sums = sum_tensor(
        [
            in_sum_a[:, :ssm],
            in_sum_b[:, :ssm],
            in_sum_a[:, ssm : ssm + attn_w],
            in_sum_b[:, ssm : ssm + 2 * NS],
            in_sum_b[:, ssm + 2 * NS :],
            in_sum_a[:, ssm + attn_w : ssm + attn_w + heads],
        ]
    )

    small = [
        restore_features(norm_gain_part),
        restore_features(mlp_gain_part),
        jnp.concatenate([dtapv, dtaps], axis=1).reshape(-1),
        decay_part,
        skip_part,
        bias_part,
        gated_gain_part.reshape(-1),
    ]
    sizes = [item.shape[0] for item in small]
    total = lax.psum(jnp.concatenate(small), ("dp", "tensor"))
    marks = [sum(sizes[:i]) for i in range(len(sizes) + 1)]
    sums = [total[marks[i] : marks[i + 1]] for i in range(len(sizes))]
    return (
        restore_features(output),
        restore_features(residual_grad),
        jnp.stack(in_sums[:2], axis=1),
        in_sums[5],
        in_sums[3],
        in_sums[2],
        in_sums[4],
        mixer_t.T,
        attn_t.T,
        gate_up_sum,
        down_t.T,
        sums[0],
        sums[1],
        sums[2].reshape(conv_filter.shape),
        sums[3],
        sums[4],
        sums[5],
        sums[6],
    )


def solution(mesh):
    rows_spec = P(("dp", "tensor"), None)
    into = P("dp", "tensor")
    out_of = P("tensor", "dp")
    double = P("dp", None, "tensor")
    weights = (double, into, into, into, into, out_of, out_of, double, out_of)
    return jax.shard_map(
        shards,
        mesh=mesh,
        in_specs=(rows_spec,) + weights + (P(),) * 7 + (rows_spec,),
        out_specs=(rows_spec, rows_spec) + weights + (P(),) * 7,
        check_vma=False,
    )
```

```python
import functools

import jax
import jax.numpy as jnp
from jax import lax
from jax.experimental import pallas as pl
from jax.experimental.pallas import tpu as pltpu
from jax.sharding import PartitionSpec as P

PH = 64
NS = 128
KC = 4
AH = 8
KVH = 2
HD = 64
LEN = 1024
CHUNK = 128
HALO = 16
GROUP = 6
SLOT = 8
GW = GROUP * PH

epsilon = 1e-05
rope_base = 100000000000.0
masked_fill = -1e30
highest = lax.Precision.HIGHEST
f32 = jnp.float32
bf16 = jnp.bfloat16
VMEM_BYTES = 52 * 1024 * 1024


def call(
    kernel, grid, in_specs, out_specs, out_shape, scratch=(), flops=0, moved=0, aliases=None, deps=()
):
    late = jax.tree.leaves(deps)
    count = len(in_specs)

    def body(*refs):
        kernel(*refs[:count], *refs[count + len(late) :])

    run = pl.pallas_call(
        body,
        grid=grid,
        in_specs=list(in_specs) + [pl.BlockSpec(memory_space=pl.ANY)] * len(late),
        out_specs=out_specs,
        out_shape=out_shape,
        scratch_shapes=list(scratch),
        input_output_aliases=aliases or {},
        compiler_params=pltpu.CompilerParams(
            vmem_limit_bytes=VMEM_BYTES, dimension_semantics=("arbitrary",) * len(grid)
        ),
        cost_estimate=pl.CostEstimate(flops=1, bytes_accessed=1, transcendentals=0),
    )
    return lambda *args: run(*args, *late)


def spec(block, index):
    return pl.BlockSpec(block, index)


def shape(dims, kind):
    return jax.ShapeDtypeStruct(dims, kind)


def dot(left, right, dims):
    return lax.dot_general(left, right, ((dims[:1], dims[1:]), ((), ())), preferred_element_type=f32)


NN = (1, 0)
NT = (1, 1)
TN = (0, 0)


def sigmoid(value):
    return 1.0 / (1.0 + jnp.exp(-value))


def pair_lanes(left, right, rows):
    lane = lax.broadcasted_iota(jnp.int32, (rows, 2 * PH), 1)
    return jnp.where(lane < PH, left, right)


def spread_heads(columns, first, count, rows):
    parts = [
        pair_lanes(
            columns[:, first + 2 * p : first + 2 * p + 1],
            columns[:, first + 2 * p + 1 : first + 2 * p + 2],
            rows,
        )
        for p in range(count // 2)
    ]
    return jnp.concatenate(parts, axis=1) if len(parts) > 1 else parts[0]


def conv_of(ref, taps, rows):
    width = taps.shape[1]
    total = ref[pl.ds(HALO - KC + 1, rows), :width] * taps[0:1, :]
    for offset in range(1, KC):
        moved = ref[pl.ds(HALO - KC + 1 + offset, rows), :width]
        total = total + moved * taps[offset : offset + 1, :]
    return total


def causal_mask(transposed):
    row = lax.broadcasted_iota(jnp.int32, (CHUNK, CHUNK), 0)
    col = lax.broadcasted_iota(jnp.int32, (CHUNK, CHUNK), 1)
    return col >= row if transposed else row >= col


def exact(left, right, dims):
    return lax.dot_general(
        left,
        right,
        ((dims[:1], dims[1:]), ((), ())),
        precision=highest,
        preferred_element_type=f32,
    )


def lower_ones():
    return jnp.where(causal_mask(False), 1.0, 0.0)


def softplus(value):
    return jnp.maximum(value, 0.0) + jnp.log1p(jnp.exp(-jnp.abs(value)))


def prepare_kernel(
    t0_ref, t1_ref, t2_ref, t3_ref, bias_ref, rate_ref,
    shr_ref, step_ref, cols_ref, rows_ref, grow_ref,
):
    tails = [t0_ref[...], t1_ref[...], t2_ref[...], t3_ref[...]]
    ext = tails[0].shape[0]
    shr_ref[:, :NS] = pair_lanes(tails[0], pltpu.roll(tails[1], PH, 1), ext)
    shr_ref[:, NS:] = pair_lanes(tails[2], pltpu.roll(tails[3], PH, 1), ext)
    rows = ext - HALO
    lane = lax.broadcasted_iota(jnp.int32, (rows, 128), 1)
    steps = jnp.zeros((rows, 128), f32)
    for t in range(4):
        moved = pltpu.roll(tails[t][HALO:], (GROUP * t - PH) % 128, 1)
        steps = jnp.where(lane // GROUP == t, moved, steps)
    steps = steps + bias_ref[...]
    step_ref[...] = steps
    dt = softplus(steps)
    decay = -rate_ref[...] * dt
    lower = lower_ones()
    prefix = jnp.zeros((1, 128), f32)
    parts = []
    for c in range(rows // CHUNK):
        sl = slice(c * CHUNK, (c + 1) * CHUNK)
        cum = exact(lower, decay[sl], NN)
        parts.append(cum)
        grow_ref[sl, :] = jnp.exp(cum + prefix)
        prefix = prefix + cum[CHUNK - 1 : CHUNK]
    cum = jnp.concatenate(parts, axis=0)
    for t in range(4):
        shift = (-GROUP * t) % 128
        dt_own = pltpu.roll(dt, shift, 1) if t else dt
        cum_own = pltpu.roll(cum, shift, 1) if t else cum
        both = jnp.where(lane < SLOT, dt_own, pltpu.roll(cum_own, SLOT, 1))
        cols_ref[t] = both[:, : 2 * SLOT]
        rows_ref[t] = jnp.transpose(cum_own)[:SLOT]


def mixer_kernel(
    val_ref, shr_ref, tapv_ref, taps_ref, cols_ref, cumr_ref, skip_ref,
    y_ref, state_ref, bc_ref, aff_ref,
):
    rows = y_ref.shape[0]
    chunks = rows // CHUNK

    @pl.when(pl.program_id(0) == 0)
    def _():
        pre = conv_of(shr_ref, taps_ref[...], rows)
        bc_ref[...] = (pre * sigmoid(pre)).astype(bf16)
        for c in range(chunks):
            sl = pl.ds(c * CHUNK, CHUNK)
            aff_ref[c] = dot(bc_ref[sl, NS:], bc_ref[sl, :NS], NT)

    pre = conv_of(val_ref, tapv_ref[...], rows)
    head_in = pre * sigmoid(pre)
    mask = causal_mask(False)
    skip = skip_ref[...]
    state = jnp.zeros((NS, GW), f32)
    for c in range(chunks):
        sl = pl.ds(c * CHUNK, CHUNK)
        x = head_in[c * CHUNK : (c + 1) * CHUNK]
        cols = cols_ref[0, sl, :]
        cumc = cols[:, SLOT:]
        cumr = cumr_ref[0, :, sl]
        w = x * spread_heads(cols, 0, GROUP, CHUNK)
        w_low = w.astype(bf16)
        inner = []
        for p in range(GROUP // 2):
            both = []
            for h in (2 * p, 2 * p + 1):
                gap = cumc[:, h : h + 1] - cumr[h : h + 1, :]
                decay = jnp.exp(jnp.where(mask, gap, masked_fill))
                weight = (aff_ref[c] * decay).astype(bf16)
                both.append(dot(weight, w_low[:, p * 2 * PH : (p + 1) * 2 * PH], NN))
            inner.append(pair_lanes(both[0], both[1], CHUNK))
        out = jnp.concatenate(inner, axis=1) + skip * x
        b_now = bc_ref[sl, :NS]
        c_now = bc_ref[sl, NS:]
        last = cumc[CHUNK - 1 : CHUNK, :]
        if c > 0:
            grown = spread_heads(jnp.exp(cumc), 0, GROUP, CHUNK)
            out = out + dot(c_now, state.astype(bf16), NN) * grown
        y_ref[sl, :] = out
        to_end = spread_heads(jnp.exp(last - cumc), 0, GROUP, CHUNK)
        added = dot(b_now, (w * to_end).astype(bf16), TN)
        fall = spread_heads(jnp.exp(last), 0, GROUP, 1)
        state = state * fall + added
    state_ref[...] = state.astype(bf16)


def gate_lanes(ref, width):
    count = ref.shape[1] // (width + 2 * PH * 2)
    step = ref.shape[1] // count
    return jnp.concatenate([ref[:, t * step : t * step + width] for t in range(count)], axis=1)


def finish_kernel(
    y_ref, gate_ref, bc_ref, grow_ref, state_ref, gain_ref, attn_ref, scan_ref, heads_ref
):
    rows, width = y_ref.shape
    grown = spread_heads(grow_ref[...], 0, width // PH, rows)
    scan = y_ref[...] + dot(bc_ref[:, NS:], state_ref[...], NN) * grown
    scan_ref[...] = scan
    gate = gate_lanes(gate_ref, GW)
    pre = scan * gate * sigmoid(gate)
    inv = lax.rsqrt(jnp.mean(pre * pre, axis=1, keepdims=True) + epsilon)
    low = (pre * inv * gain_ref[...]).astype(bf16)
    step = GW + 2 * HD
    for t in range(width // GW):
        heads_ref[:, t * step : t * step + GW] = low[:, t * GW : (t + 1) * GW]
        heads_ref[:, t * step + GW : (t + 1) * step] = attn_ref[:, t * 2 * HD : (t + 1) * 2 * HD]


def ungate_kernel(
    grad_ref, scan_ref, gate_ref, bc_ref, grow_ref, gain_ref,
    dgate_ref, dscan_ref, dgain_ref, dstate_ref,
):
    rows, width = scan_ref.shape
    scan = scan_ref[...]
    gate = gate_lanes(gate_ref, GW)
    sig = sigmoid(gate)
    silu = gate * sig
    pre = scan * silu
    inv = lax.rsqrt(jnp.mean(pre * pre, axis=1, keepdims=True) + epsilon)
    normed = pre * inv
    step = GW + 2 * HD
    grad = jnp.concatenate(
        [grad_ref[:, t * step : t * step + GW] for t in range(width // GW)], axis=1
    )
    u = grad * gain_ref[...]
    cross = jnp.mean(u * normed, axis=1, keepdims=True)
    dpre = inv * (u - normed * cross)
    dscan = dpre * silu
    dgate_ref[...] = (dpre * scan * sig * (1.0 + gate * (1.0 - sig))).astype(bf16)
    dscan_ref[...] = dscan
    grown = spread_heads(grow_ref[...], 0, width // PH, rows)
    dstate = dot(bc_ref[:, NS:], (dscan * grown).astype(bf16), TN)
    dgain = jnp.sum(grad * normed, axis=0, keepdims=True)
    first = pl.program_id(0) == 0

    @pl.when(first)
    def _():
        dgain_ref[...] = dgain
        dstate_ref[...] = dstate

    @pl.when(jnp.logical_not(first))
    def _():
        dgain_ref[...] += dgain
        dstate_ref[...] += dstate


def split_sum(value, ones_at):
    high = value.astype(bf16)
    low = (value - high.astype(f32)).astype(bf16)
    return dot(high, ones_at, NN) + dot(low, ones_at, NN)


def unconv(ref, taps, dact, pad_ref, out_ref, dtaps_ref, rows):
    pre = conv_of(ref, taps, rows)
    sig = sigmoid(pre)
    dpre = dact * sig * (1.0 + pre * (1.0 - sig))
    lead = HALO + 8
    width = dact.shape[1]
    pad_ref[pl.ds(0, lead), :width] = jnp.zeros((lead, width), f32)
    pad_ref[pl.ds(lead + rows, 8), :width] = jnp.zeros((8, width), f32)
    pad_ref[pl.ds(lead, rows), :width] = dpre
    total = None
    dtaps = []
    for offset in range(KC):
        part = pad_ref[pl.ds(8 + KC - 1 - offset, rows + HALO), :width]
        part = part * taps[offset : offset + 1, :]
        total = part if total is None else total + part
        moved = ref[pl.ds(HALO - KC + 1 + offset, rows), :width]
        dtaps.append(jnp.sum(dpre * moved, axis=0, keepdims=True))
    out_ref[:, :width] = total.astype(out_ref.dtype)
    dtaps_ref[...] = jnp.concatenate(dtaps, axis=0)


def unmix_kernel(
    val_ref, shr_ref, tapv_ref, taps_ref, in_ref, cumr_ref, skip_ref, bc_ref,
    dscan_ref, enter_ref, dleave_ref,
    dval_ref, dshr_ref, cols_ref, rows_ref, dlast_ref, dtapv_ref, dtaps_ref, dskip_ref,
    daff_ref, dbc_ref, aff_ref, dx_ref, states_ref, pad_ref,
):
    rows = dscan_ref.shape[0]
    chunks = rows // CHUNK
    step = pl.program_id(0)

    @pl.when(step == 0)
    def _():
        for c in range(chunks):
            sl = pl.ds(c * CHUNK, CHUNK)
            aff_ref[c] = dot(bc_ref[sl, :NS], bc_ref[sl, NS:], NT)
        daff_ref[...] = jnp.zeros(daff_ref.shape, f32)
        dbc_ref[...] = jnp.zeros(dbc_ref.shape, f32)

    pre = conv_of(val_ref, tapv_ref[...], rows)
    dx_ref[...] = pre * sigmoid(pre)
    mask = causal_mask(True)
    skip = skip_ref[...]
    lane = lax.broadcasted_iota(jnp.int32, (GW, 128), 0) // PH
    slot = lax.broadcasted_iota(jnp.int32, (GW, 128), 1)
    ones_dt = jnp.where(lane == slot, 1.0, 0.0).astype(bf16)
    ones_cum = jnp.where(lane + SLOT == slot, 1.0, 0.0).astype(bf16)
    half_lane = lax.broadcasted_iota(jnp.int32, (CHUNK, 2 * PH), 1) // PH
    slot_lane = lax.broadcasted_iota(jnp.int32, (CHUNK, 128), 1)

    state = enter_ref[...].astype(f32)
    states_ref[0] = state
    for c in range(chunks - 1):
        sl = pl.ds(c * CHUNK, CHUNK)
        cumc = in_ref[0, sl, SLOT:]
        last = cumc[CHUNK - 1 : CHUNK, :]
        scale = spread_heads(in_ref[0, sl, :SLOT] * jnp.exp(last - cumc), 0, GROUP, CHUNK)
        added = dot(bc_ref[sl, :NS], (dx_ref[sl, :] * scale).astype(bf16), TN)
        state = state * spread_heads(jnp.exp(last), 0, GROUP, 1) + added
        states_ref[c + 1] = state

    dstate = dleave_ref[...].astype(f32)
    dskip = jnp.zeros((1, GW), f32)
    for c in reversed(range(chunks)):
        sl = pl.ds(c * CHUNK, CHUNK)
        x = dx_ref[sl, :]
        dy = dscan_ref[sl, :]
        dy_low = dy.astype(bf16)
        cumc = in_ref[0, sl, SLOT:]
        cumr = cumr_ref[0, :, sl]
        last = cumc[CHUNK - 1 : CHUNK, :]
        dt = spread_heads(in_ref[0, sl, :SLOT], 0, GROUP, CHUNK)
        w = x * dt
        w_low = w.astype(bf16)
        b_now = bc_ref[sl, :NS]
        c_now = bc_ref[sl, NS:]
        affinity = aff_ref[c]
        dcum = jnp.zeros((CHUNK, 128), f32)
        daff = daff_ref[c]
        dw_parts = []
        for p in range(GROUP // 2):
            pair = slice(p * 2 * PH, (p + 1) * 2 * PH)
            both = []
            for h in (2 * p, 2 * p + 1):
                gap = cumr[h : h + 1, :] - cumc[:, h : h + 1]
                decay = jnp.exp(jnp.where(mask, gap, masked_fill))
                weight = affinity * decay
                w_own = jnp.where(half_lane == h - 2 * p, w[:, pair], 0.0).astype(bf16)
                dweight = dot(w_own, dy_low[:, pair], NT)
                daff = daff + dweight * decay
                moved = dweight * weight
                rows_ref[0, h : h + 1, sl] = jnp.sum(moved, axis=0, keepdims=True)
                dcum = dcum - jnp.where(
                    slot_lane == SLOT + h, jnp.sum(moved, axis=1, keepdims=True), 0.0
                )
                both.append(dot(weight.astype(bf16), dy_low[:, pair], NN))
            dw_parts.append(pair_lanes(both[0], both[1], CHUNK))
        daff_ref[c] = daff
        state = states_ref[c]
        state_low = state.astype(bf16)
        dstate_low = dstate.astype(bf16)
        grown = spread_heads(jnp.exp(cumc), 0, GROUP, CHUNK)
        to_end = spread_heads(jnp.exp(last - cumc), 0, GROUP, CHUNK)
        fall = spread_heads(jnp.exp(last), 0, GROUP, 1)
        dy_grown = (dy * grown).astype(bf16)
        carried = dot(c_now, state_low, NN) * grown
        from_end = dot(b_now, dstate_low, NN) * to_end
        dbc_ref[sl, NS:] += dot(dy_grown, state_low, NT)
        dbc_ref[sl, :NS] += dot((w * to_end).astype(bf16), dstate_low, NT)
        dw = jnp.concatenate(dw_parts, axis=1) + from_end
        ended = w * from_end
        cols_ref[0, sl, :] = (
            dcum + split_sum(dw * x, ones_dt) + split_sum(dy * carried - ended, ones_cum)
        )
        dlast_ref[c : c + 1, :] = jnp.sum(ended, axis=0, keepdims=True) + fall * jnp.sum(
            state * dstate, axis=0, keepdims=True
        )
        dstate = fall * dstate + dot(c_now, dy_grown, TN)
        dskip = dskip + jnp.sum(dy * x, axis=0, keepdims=True)
        dx_ref[sl, :] = dw * dt + skip * dy
    dskip_ref[...] = dskip
    unconv(val_ref, tapv_ref[...], dx_ref[...], pad_ref, dval_ref, dtapv_ref, rows)

    @pl.when(step == pl.num_programs(0) - 1)
    def _():
        for c in range(chunks):
            sl = pl.ds(c * CHUNK, CHUNK)
            daff_low = daff_ref[c].astype(bf16)
            dbc_ref[sl, :NS] += dot(daff_low, bc_ref[sl, NS:], NN)
            dbc_ref[sl, NS:] += dot(daff_low, bc_ref[sl, :NS], TN)
        unconv(shr_ref, taps_ref[...], dbc_ref[...], pad_ref, dshr_ref, dtaps_ref, rows)


def settle_kernel(
    low_in_ref, dshr_ref, cols_ref, rows_ref, dlast_ref, step_ref, rate_ref,
    low_ref, ddecay_ref, dbias_ref, dstep_ref,
):
    rows = step_ref.shape[0]
    t = pl.program_id(0)
    lane = lax.broadcasted_iota(jnp.int32, (rows, 128), 1)

    @pl.when(t == 0)
    def _():
        ddt = jnp.zeros((rows, 128), f32)
        dcum = jnp.zeros((rows, 128), f32)
        for i in range(4):
            own = lane // GROUP == i
            cols = cols_ref[i]
            ddt = jnp.where(own, pltpu.roll(cols, GROUP * i, 1) if i else cols, ddt)
            dcum = jnp.where(own, pltpu.roll(cols, (GROUP * i - SLOT) % 128, 1), dcum)
        filled = jnp.concatenate(
            [rows_ref[i] for i in range(4)] + [jnp.zeros((128 - 4 * SLOT, rows), f32)], axis=0
        )
        turned = jnp.transpose(filled)
        for i in range(4):
            moved = pltpu.roll(turned, ((GROUP - SLOT) * i) % 128, 1) if i else turned
            dcum = dcum + jnp.where(lane // GROUP == i, moved, 0.0)
        width = dlast_ref.shape[1]
        head = lax.broadcasted_iota(jnp.int32, (width, 128), 0) // PH
        place = lax.broadcasted_iota(jnp.int32, (width, 128), 1)
        at_end = exact(dlast_ref[...], jnp.where(head == place, 1.0, 0.0), NN)
        lower = lower_ones()
        steps = step_ref[...]
        rate = rate_ref[...]
        decay = -rate * softplus(steps)
        ddecay = jnp.zeros((1, 128), f32)
        dbias = jnp.zeros((1, 128), f32)
        for c in range(rows // CHUNK):
            sl = slice(c * CHUNK, (c + 1) * CHUNK)
            dlog = exact(lower, dcum[sl], TN) + at_end[c : c + 1]
            ddecay = ddecay + jnp.sum(dlog * decay[sl], axis=0, keepdims=True)
            dstep = (ddt[sl] - rate * dlog) * sigmoid(steps[sl])
            dbias = dbias + jnp.sum(dstep, axis=0, keepdims=True)
            dstep_ref[sl, :] = dstep
        ddecay_ref[...] = ddecay
        dbias_ref[...] = dbias

    for i in range(4):

        @pl.when(t == i)
        def _(i=i):
            shared = dshr_ref[:, (i // 2) * 2 * PH : (i // 2 + 1) * 2 * PH]
            if i % 2:
                shared = pltpu.roll(shared, PH, 1)
            steps = pltpu.roll(dstep_ref[...], (PH - GROUP * i) % 128, 1)
            steps = jnp.where((lane >= PH) & (lane < PH + GROUP), steps, 0.0)
            low_ref[pl.ds(0, HALO), :] = jnp.where(lane < PH, 1.0, 0.0)[:HALO].astype(bf16) * (
                shared[:HALO].astype(bf16)
            )
            low_ref[pl.ds(HALO, rows), :] = jnp.where(lane < PH, shared[HALO:], steps).astype(bf16)


def first_back_kernel(
    a_ref, b_ref, late_ref, rows_ref, middle_ref, gain_ref, more_ref, out_ref, gains_ref
):
    rows = a_ref.shape[0]
    out_ref[...] = a_ref[...] + b_ref[pl.ds(HALO, rows), :]
    out_ref[pl.ds(rows - HALO, HALO), :] += late_ref[...]
    grad = out_ref[...]
    values = rows_ref[...].astype(f32)
    inv = lax.rsqrt(jnp.mean(values * values, axis=1, keepdims=True) + epsilon)
    normed = values * inv
    gains_ref[...] = jnp.zeros(gains_ref.shape, f32)
    gains_ref[0:1, :] = jnp.sum(grad * normed, axis=0, keepdims=True)
    gains_ref[1:2, :] = more_ref[...]
    scaled = grad * gain_ref[...]
    cross = jnp.mean(scaled * normed, axis=1, keepdims=True)
    out_ref[...] = middle_ref[...] + inv * (scaled - normed * cross)


def swap_halves(value):
    half = HD // 2
    width = value.shape[1]
    lane = lax.broadcasted_iota(jnp.int32, value.shape, 1) % HD
    return jnp.where(
        lane < half, pltpu.roll(value, width - half, 1), pltpu.roll(value, half, 1)
    )


def rotate_kernel(t0_ref, t1_ref, t2_ref, t3_ref, cos_ref, sin_ref, out_ref):
    rows = cos_ref.shape[0]
    for head, (key, value) in enumerate(((t0_ref, t1_ref), (t2_ref, t3_ref))):
        both = pair_lanes(key[...], pltpu.roll(value[...], HD, 1), rows)
        out = both * cos_ref[...] + swap_halves(both) * sin_ref[...]
        out_ref[:, head * 2 * HD : (head + 1) * 2 * HD] = out.astype(bf16)


def unrotate_kernel(low_in_ref, own_ref, late_ref, cos_ref, sin_ref, out_ref):
    value = own_ref[...] + late_ref[...].astype(f32)
    value = value * cos_ref[...] + swap_halves(value * sin_ref[...])
    odd = lax.rem(pl.program_id(0), 2) == 1
    value = jnp.where(odd, pltpu.roll(value, HD, 1), value)
    lane = lax.broadcasted_iota(jnp.int32, value.shape, 1)
    out_ref[...] = jnp.where(lane < HD, value, 0.0).astype(bf16)


def head_queries(query, which):
    lane = lax.broadcasted_iota(jnp.int32, query.shape, 1)
    moved = pltpu.roll(query, HD, 1) if which else query
    return jnp.where(lane < HD, moved, 0.0)


def score_weights(query, before, own, allowed):
    early = jnp.where(allowed, dot(query, before, NT), masked_fill)
    late = dot(query, own, NT)
    row = lax.broadcasted_iota(jnp.int32, late.shape, 0)
    col = lax.broadcasted_iota(jnp.int32, late.shape, 1)
    late = jnp.where(row >= col, late, masked_fill)
    top = jnp.maximum(
        jnp.max(early, axis=1, keepdims=True), jnp.max(late, axis=1, keepdims=True)
    )
    early = jnp.exp(early - top)
    late = jnp.exp(late - top)
    total = jnp.sum(early, axis=1, keepdims=True) + jnp.sum(late, axis=1, keepdims=True)
    return early, late, 1.0 / total


def rotated_queries(q_ref, cos_ref, sin_ref):
    query = q_ref[...]
    return (query * cos_ref[...] + swap_halves(query) * sin_ref[...]) * (HD**-0.5)


def attend_kernel(part_ref, q_ref, cos_ref, sin_ref, before_ref, own_ref, out_ref):
    allowed = part_ref[0] > 0
    query = rotated_queries(q_ref, cos_ref, sin_ref)
    before = before_ref[...]
    own = own_ref[...]
    results = []
    for which in range(2):
        q_low = head_queries(query, which).astype(bf16)
        early, late, scale = score_weights(q_low, before, own, allowed)
        result = dot(early.astype(bf16), before, NN) + dot(late.astype(bf16), own, NN)
        results.append(result * scale)
    out_ref[...] = pair_lanes(pltpu.roll(results[0], HD, 1), results[1], query.shape[0]).astype(
        bf16
    )


def unattend_kernel(
    part_ref, q_ref, cos_ref, sin_ref, before_ref, own_ref, dout_ref,
    dq_ref, dbefore_ref, down_ref,
):
    allowed = part_ref[0] > 0
    query = rotated_queries(q_ref, cos_ref, sin_ref)
    before = before_ref[...]
    own = own_ref[...]
    dout = dout_ref[...]
    lane = lax.broadcasted_iota(jnp.int32, dout.shape, 1)
    dqs = []
    dbefore = None
    down = None
    for which in range(2):
        q_low = head_queries(query, which).astype(bf16)
        early, late, scale = score_weights(q_low, before, own, allowed)
        early = early * scale
        late = late * scale
        dout_own = dout if which else pltpu.roll(dout, HD, 1)
        dout_low = jnp.where(lane >= HD, dout_own, 0.0).astype(bf16)
        dearly = dot(dout_low, before, NT)
        dlate = dot(dout_low, own, NT)
        cross = jnp.sum(early * dearly, axis=1, keepdims=True) + jnp.sum(
            late * dlate, axis=1, keepdims=True
        )
        dearly = (early * (dearly - cross)).astype(bf16)
        dlate = (late * (dlate - cross)).astype(bf16)
        dqs.append(dot(dearly, before, NN) + dot(dlate, own, NN))
        part_before = dot(dearly, q_low, TN) + dot(early.astype(bf16), dout_low, TN)
        part_own = dot(dlate, q_low, TN) + dot(late.astype(bf16), dout_low, TN)
        dbefore = part_before if dbefore is None else dbefore + part_before
        down = part_own if down is None else down + part_own
    dq = pair_lanes(dqs[0], pltpu.roll(dqs[1], HD, 1), dout.shape[0]) * (HD**-0.5)
    dq_ref[...] = (dq * cos_ref[...] + swap_halves(dq * sin_ref[...])).astype(bf16)
    first = lax.rem(pl.program_id(0), AH // KVH // 2) == 0

    @pl.when(first)
    def _():
        dbefore_ref[...] = dbefore
        down_ref[...] = down

    @pl.when(jnp.logical_not(first))
    def _():
        dbefore_ref[...] += dbefore
        down_ref[...] += down


def times(rows_in, blocks, outs, finish, extras=(), specs=(), out_specs=None, deps=()):
    rows, depth = rows_in.shape
    groups, _, width = blocks[0].shape
    tile = width
    count = len(blocks)
    tile_spec = spec((rows, tile), lambda i: (0, i))

    def kernel(rows_ref, *refs):
        weight = jnp.concatenate([ref[0] for ref in refs[:count]], axis=0)
        finish(dot(rows_ref[...], weight, NN), *refs[count:])

    return call(
        kernel,
        (groups,),
        [spec((rows, depth), lambda i: (0, 0))]
        + [spec((1, b.shape[1], tile), lambda i: (i, 0, 0)) for b in blocks]
        + list(specs),
        out_specs or [tile_spec] * len(outs),
        outs,
        flops=2 * rows * depth * width * groups,
        moved=depth * width * groups * 2 + rows * width * groups * 4,
        deps=deps,
    )(rows_in, *blocks, *extras)


def times_transposed(lefts, blocks, outs, finish, extras=(), deps=()):
    rows = lefts[0].shape[0]
    groups, _, width = blocks[0].shape
    count = len(blocks)
    depth = sum(b.shape[1] for b in blocks)
    whole = lambda item: spec(item.shape, lambda i: (0, 0))

    def kernel(*refs):
        left = [ref[...] for ref in refs[: len(lefts)]]
        left = jnp.concatenate(left, axis=1) if len(left) > 1 else left[0]
        refs = refs[len(lefts) :]
        weight = jnp.concatenate([ref[0] for ref in refs[:count]], axis=0)
        part = dot(left, weight, NT)
        total = refs[-1]
        step = pl.program_id(0)

        @pl.when(step == 0)
        def _():
            total[...] = part

        @pl.when(step > 0)
        def _():
            total[...] += part

        @pl.when(step == pl.num_programs(0) - 1)
        def _():
            finish(total[...], *refs[count:-1])

    return call(
        kernel,
        (groups,),
        [spec((rows, item.shape[1] // groups), lambda i: (0, i)) for item in lefts]
        + [spec((1, b.shape[1], width), lambda i: (i, 0, 0)) for b in blocks]
        + [whole(e) for e in extras],
        [whole(o) for o in outs],
        outs,
        [pltpu.VMEM((rows, depth), f32)],
        flops=2 * rows * depth * width * groups,
        moved=depth * width * groups * 2 + rows * depth * 8,
        deps=deps,
    )(*lefts, *blocks, *extras)


def store(value, out_ref):
    out_ref[...] = value.astype(out_ref.dtype)


def add_store(value, other_ref, out_ref):
    out_ref[...] = value + other_ref[...]


def middle_finish(value, rows_ref, gain_ref, middle_ref, low_ref):
    middle = rows_ref[...] + value
    middle_ref[...] = middle
    inv = lax.rsqrt(jnp.mean(middle * middle, axis=1, keepdims=True) + epsilon)
    low_ref[...] = (middle * inv * gain_ref[...]).astype(bf16)


def unit_finish(value, hidden_ref, by_gate_ref, by_up_ref):
    half = value.shape[1] // 2
    gate = value[:, :half]
    up = value[:, half:]
    sig = sigmoid(gate)
    silu = gate * sig
    hidden_ref[...] = (silu * up).astype(bf16)
    by_gate_ref[...] = (up * sig * (1.0 + gate * (1.0 - sig))).astype(bf16)
    by_up_ref[...] = silu.astype(bf16)


def unit_back_finish(value, by_gate_ref, by_up_ref, out_ref):
    half = value.shape[1]
    out_ref[:, :half] = (value * by_gate_ref[...].astype(f32)).astype(bf16)
    out_ref[:, half:] = (value * by_up_ref[...].astype(f32)).astype(bf16)


def middle_back_finish(value, middle_ref, cot_ref, gain_ref, grad_ref, low_ref, dgain_ref):
    middle = middle_ref[...]
    inv = lax.rsqrt(jnp.mean(middle * middle, axis=1, keepdims=True) + epsilon)
    normed = middle * inv
    dgain_ref[...] = jnp.sum(value * normed, axis=0, keepdims=True)
    scaled = value * gain_ref[...]
    cross = jnp.mean(scaled * normed, axis=1, keepdims=True)
    grad = cot_ref[...].astype(f32) + inv * (scaled - normed * cross)
    grad_ref[...] = grad
    low_ref[...] = grad.astype(bf16)


def partner(value, bit):
    count = lax.axis_size("dp")
    return lax.ppermute(value, "dp", [(i, i ^ (1 << bit)) for i in range(count)])


def high_bits():
    return list(range(1, lax.axis_size("dp").bit_length() - 1))


def put_rows(out_ref, parts):
    if parts[0].shape[0] % 16:
        parts = [jnp.concatenate([p.astype(f32) for p in parts], axis=0).astype(bf16)]
    at = 0
    for p in parts:
        out_ref[0, at : at + p.shape[0], :] = p
        at += p.shape[0]


def cut_pieces(gathered, ranges, deps=()):
    groups, rows, width = gathered.shape
    half = rows // 2

    def kernel(in_ref, *out_refs):
        for i, (start, stop) in enumerate(ranges):
            part = in_ref[0, :, start:stop]
            if half % 16:
                part = part.astype(f32)
            out_refs[2 * i][0] = part[:half].astype(bf16)
            out_refs[2 * i + 1][0] = part[half:].astype(bf16)

    sizes = [stop - start for start, stop in ranges for _ in range(2)]
    outs = call(
        kernel,
        (groups,),
        [spec((1, rows, width), lambda t: (t, 0, 0))],
        [spec((1, half, w), lambda t: (t, 0, 0)) for w in sizes],
        [shape((groups, half, w), bf16) for w in sizes],
        moved=groups * rows * width * 4,
        deps=deps,
    )(gathered)
    return [(outs[2 * i], outs[2 * i + 1]) for i in range(len(ranges))]


def spread_send(held, step):
    bits = high_bits()
    return partner(held[0], bits[step]), partner(held[1], bits[-1 - step])


def join_all(items, deps=()):
    groups = items[0][0][0].shape[0]
    args, in_specs, out_specs, outs, moved = [], [], [], [], 0
    for held, got, last in items:
        _, rows, width = held[0].shape
        args += [held[0], got[0], held[1], got[1]]
        in_specs += [spec((1, rows, width), lambda t: (t, 0, 0))] * 4
        size = 4 if last else 2
        number = 1 if last else 2
        out_specs += [spec((1, size * rows, width), lambda t: (t, 0, 0))] * number
        outs += [shape((groups, size * rows, width), bf16)] * number
        moved += groups * rows * width * 16

    def kernel(*refs):
        out_refs = list(refs[len(args) :])
        for i, (_, _, last) in enumerate(items):
            a_ref, b_ref, c_ref, d_ref = refs[4 * i : 4 * i + 4]
            upper = [a_ref[0], b_ref[0]]
            lower = [c_ref[0], d_ref[0]]
            if last:
                put_rows(out_refs.pop(0), upper + lower)
            else:
                put_rows(out_refs.pop(0), upper)
                put_rows(out_refs.pop(0), lower)

    out = list(
        call(kernel, (groups,), in_specs, out_specs, outs, moved=moved, deps=deps)(*args)
    )
    return [[out.pop(0)] if last else [out.pop(0), out.pop(0)] for _, _, last in items]


def join(held, got, deps=(), last=False):
    return join_all([(held, got, last)], deps)[0]


def spread_rest(held, got, first, deps=()):
    steps = len(high_bits())
    for i in range(first, steps):
        held = join(held, got, deps, i + 1 == steps)
        if i + 1 < steps:
            got = spread_send(held, i + 1)
    return held


def spread_end(held):
    return held[0], partner(held[0], 0)


def route_bits(route):
    return high_bits()[::-1] if route else high_bits()


def send_one(held, route, step):
    return partner(held, route_bits(route)[step])


def join_one(held, got, route, step, deps=()):
    groups, rows, width = held.shape
    bits = route_bits(route)
    masks = [(0, 0), (0, 1)]
    for bit in bits[: step + 1]:
        masks = masks + [(m | (1 << bit), p) for m, p in masks]
    places = list(range(len(masks)))
    if step + 1 == len(bits):
        goal = block_masks()[: len(masks)]
        places = [masks.index(m) for m in goal]
    size = 2 * rows // len(masks)

    def kernel(a_ref, b_ref, out_ref):
        if step + 1 < len(bits):
            put_rows(out_ref, [a_ref[0], b_ref[0]])
            return
        parts = []
        for place in places:
            ref, at = (a_ref, place * size) if place * size < rows else (b_ref, place * size - rows)
            parts.append(ref[0, at : at + size, :])
        put_rows(out_ref, parts)

    one = spec((1, rows, width), lambda t: (t, 0, 0))
    return call(
        kernel,
        (groups,),
        [one] * 2,
        spec((1, 2 * rows, width), lambda t: (t, 0, 0)),
        shape((groups, 2 * rows, width), bf16),
        moved=groups * rows * width * 8,
        deps=deps,
    )(held, got)


def rest_one(held, got, route, first, deps=()):
    steps = len(high_bits())
    for i in range(first, steps):
        held = join_one(held, got, route, i, deps)
        if i + 1 < steps:
            got = send_one(held, route, i + 1)
    return held


def slice_one(gathered, start, stop, deps=()):
    groups, rows, width = gathered.shape

    def kernel(in_ref, out_ref):
        out_ref[0] = in_ref[0, :, start:stop]

    return call(
        kernel,
        (groups,),
        [spec((1, rows, width), lambda t: (t, 0, 0))],
        spec((1, rows, stop - start), lambda t: (t, 0, 0)),
        shape((groups, rows, stop - start), bf16),
        moved=groups * rows * width * 4,
        deps=deps,
    )(gathered)


def tile_of(width):
    return next(t for t in (1024, 768, 512, 256, 128) if width % t == 0)


def collect_send(left, right, deps=()):
    rows, depth = left.shape
    near = depth // 2
    width = right.shape[1]
    tile = tile_of(width)

    def kernel(left_ref, right_ref, out_ref):
        out_ref[...] = dot(left_ref[...], right_ref[...], TN).astype(bf16)

    send = call(
        kernel,
        (width // tile,),
        [spec((rows, near), lambda i: (0, 1)), spec((rows, tile), lambda i: (0, i))],
        spec((near, tile), lambda i: (0, i)),
        shape((near, width), bf16),
        flops=2 * rows * near * width,
        moved=(rows + near) * width * 2,
        deps=deps,
    )(left, right)
    return send, partner(send, 0)


def collect_keep(left, right, got, deps=(), route=None):
    rows, depth = left.shape
    near = depth // 2
    quarter = near // 4
    if route is not None:
        masks, bit = route_masks(route, 0)
        lists = split_masks(masks, bit)
    else:
        lists = [[2 * i, 2 * i + 1] for i in range(4)]
    size = near // sum(len(x) for x in lists) if route is not None else quarter // 2
    width = right.shape[1]
    tile = tile_of(width)

    def kernel(left_ref, right_ref, got_ref, *out_refs):
        total = dot(left_ref[...], right_ref[...], TN) + got_ref[...].astype(f32)
        for places, out_ref in zip(lists, out_refs):
            out_ref[...] = pick_rows(total, places, size).astype(bf16)

    high = near // len(lists)
    out = spec((high, tile), lambda i: (0, i))
    return call(
        kernel,
        (width // tile,),
        [
            spec((rows, near), lambda i: (0, 0)),
            spec((rows, tile), lambda i: (0, i)),
            spec((near, tile), lambda i: (0, i)),
        ],
        [out] * len(lists),
        [shape((high, width), bf16)] * len(lists),
        flops=2 * rows * near * width,
        moved=(rows + 2 * near) * width * 2,
        deps=deps,
    )(left, right, got)


def pick_rows(value, places, size):
    parts, at = [], 0
    while at < len(places):
        end = at + 1
        while end < len(places) and places[end] == places[end - 1] + 1:
            end += 1
        parts.append(value[places[at] * size : (places[end - 1] + 1) * size])
        at = end
    return jnp.concatenate(parts, axis=0) if len(parts) > 1 else parts[0]


def route_masks(route, step):
    bits = route_bits(route)[::-1]
    masks = block_masks()[: 2 << len(bits)]
    for bit in bits[:step]:
        masks = [m for m in masks if not m[0] >> bit & 1]
    return masks, bits[step] if step < len(bits) else None


def split_masks(masks, bit):
    return [
        [i for i, m in enumerate(masks) if (m[0] >> bit & 1) == side] for side in range(2)
    ]


def move_one(parts, route, step):
    return partner(parts[1], route_bits(route)[::-1][step])


def add_one(parts, got, route, step, deps=()):
    rows, width = parts[0].shape
    half = rows // 2
    tile = tile_of(width)
    masks, bit = route_masks(route, step + 1)
    lists = split_masks(masks, bit)
    size = rows // len(masks)

    def kernel(a_ref, b_ref, *out_refs):
        total = a_ref[...].astype(f32) + b_ref[...].astype(f32)
        for places, out_ref in zip(lists, out_refs):
            out_ref[...] = pick_rows(total, places, size).astype(bf16)

    block = spec((rows, tile), lambda i: (0, i))
    return call(
        kernel,
        (width // tile,),
        [block] * 2,
        [spec((half, tile), lambda i: (0, i))] * 2,
        [shape((half, width), bf16)] * 2,
        moved=rows * width * 6,
        deps=deps,
    )(parts[0], got)


def collect_move(parts, step):
    bits = high_bits()
    return partner(parts[1], bits[-1 - step]), partner(parts[3], bits[step])


def collect_add(parts, got, deps=()):
    rows, width = parts[0].shape
    half = rows // 2
    tile = tile_of(width)

    def kernel(a_ref, b_ref, c_ref, d_ref, *out_refs):
        for i, (own, other) in enumerate(((a_ref, b_ref), (c_ref, d_ref))):
            total = own[...].astype(f32) + other[...].astype(f32)
            out_refs[2 * i][...] = total[:half].astype(bf16)
            out_refs[2 * i + 1][...] = total[half:].astype(bf16)

    block = spec((rows, tile), lambda i: (0, i))
    return call(
        kernel,
        (width // tile,),
        [block] * 4,
        [spec((half, tile), lambda i: (0, i))] * 4,
        [shape((half, width), bf16)] * 4,
        moved=rows * width * 12,
        deps=deps,
    )(parts[0], got[0], parts[2], got[1])


def collect_end(pairs, deps=()):
    groups = lax.axis_size("tensor")
    args, in_specs, widths, counts = [], [], [], []
    for parts, got in pairs:
        width = parts[0].shape[1] // groups
        widths.append(width)
        both = len(parts) == 4
        add = [parts[0], got[0], parts[2], got[1]] if both else [parts[0], got]
        counts.append(len(add))
        args += add
        in_specs += [spec((parts[0].shape[0], width), lambda t: (0, t))] * len(add)
        rows = parts[0].shape[0] // (1 if both else 2)

    def kernel(*refs):
        at = first = 0
        for width, count in zip(widths, counts):
            values = [ref[...].astype(f32) for ref in refs[first : first + count]]
            sums = [values[i] + values[i + 1] for i in range(0, count, 2)]
            out = jnp.concatenate(sums, axis=0) if len(sums) > 1 else sums[0]
            refs[-1][0, :, at : at + width] = out.astype(bf16)
            at += width
            first += count

    total = sum(widths)
    return call(
        kernel,
        (groups,),
        in_specs,
        spec((1, 2 * rows, total), lambda t: (t, 0, 0)),
        shape((groups, 2 * rows, total), bf16),
        moved=groups * rows * total * 12,
        deps=deps,
    )(*args)


def block_masks():
    bits = high_bits()
    count = 1 << len(bits)
    masks = []
    for core in range(2):
        for part in range(2):
            for j in range(count):
                order = bits[::-1] if part else bits
                mask = sum(((j >> i) & 1) << bit for i, bit in enumerate(order))
                masks.append((mask | core, part))
    return masks


def take_blocks(value, sources):
    width = value.shape[-1] // len(sources)
    axis = value.ndim - 1
    return jnp.concatenate(
        [lax.dynamic_slice_in_dim(value, s * width, width, axis) for s in sources], axis=axis
    )


def permute_features(value):
    me = lax.axis_index("dp")
    return take_blocks(value, [(me ^ mask) * 2 + part for mask, part in block_masks()])


def restore_features(value):
    me = lax.axis_index("dp")
    masks = block_masks()
    count = lax.axis_size("dp")
    table = jnp.array(
        [[masks.index((m, part)) for part in range(2)] for m in range(count)], jnp.int32
    )
    return take_blocks(
        value, [table[me ^ block, part] for block in range(count) for part in range(2)]
    )


def restore_all(values, deps=()):
    count = lax.axis_size("dp")
    if values[0].shape[1] // count != 128:
        return [restore_features(v) for v in values]
    masks = block_masks()
    places = [[masks.index((m, part)) for part in range(2)] for m in range(count)]
    rows = jnp.array([[p[0] // 2, p[0] % 2, p[1] // 2, p[1] % 2] for p in places], jnp.int32)
    table = rows[lax.axis_index("dp") ^ jnp.arange(count, dtype=jnp.int32)].reshape(-1)
    late = jax.tree.leaves(deps)
    number = len(values)

    def kernel(table_ref, *refs):
        i = pl.program_id(0)
        out_refs = refs[2 * number + len(late) :]
        for n in range(number):
            front, back = refs[2 * n][...], refs[2 * n + 1][...]
            front = jnp.where(table_ref[4 * i + 1] > 0, pltpu.roll(front, 64, 1), front)
            back = jnp.where(table_ref[4 * i + 3] > 0, back, pltpu.roll(back, 64, 1))
            lane = lax.broadcasted_iota(jnp.int32, front.shape, 1)
            out_refs[n][...] = jnp.where(lane < 64, front, back)

    in_specs = []
    for v in values:
        for at in (0, 2):
            in_specs.append(spec((v.shape[0], 128), lambda i, t, at=at: (0, t[4 * i + at])))
    in_specs += [pl.BlockSpec(memory_space=pl.ANY)] * len(late)
    return pl.pallas_call(
        kernel,
        grid_spec=pltpu.PrefetchScalarGridSpec(
            num_scalar_prefetch=1,
            grid=(count,),
            in_specs=in_specs,
            out_specs=[spec((v.shape[0], 128), lambda i, t: (0, i)) for v in values],
        ),
        out_shape=[shape(v.shape, v.dtype) for v in values],
        compiler_params=pltpu.CompilerParams(vmem_limit_bytes=VMEM_BYTES),
        cost_estimate=pl.CostEstimate(flops=1, bytes_accessed=1, transcendentals=0),
    )(table, *[v for v in values for _ in range(2)], *late)


def sum_all(value):
    for axis in ("dp", "tensor"):
        count = lax.axis_size(axis)
        for bit in range(count.bit_length() - 1):
            value = value + lax.ppermute(value, axis, [(i, i ^ (1 << bit)) for i in range(count)])
    return value


def norm_of(rows):
    inv = lax.rsqrt(jnp.mean(rows * rows, axis=-1, keepdims=True) + epsilon)
    return rows * inv, inv


def norm_back(grad, gain, normed, inv):
    scaled = grad * gain
    return inv * (scaled - normed * jnp.mean(scaled * normed, axis=-1, keepdims=True))


def over_tensor(piece):
    return lax.all_gather(piece, "tensor", axis=0)


def shards(
    residual,
    mixer_in,
    step_in,
    shared_in,
    query_in,
    keyval_in,
    mixer_proj,
    attn_proj,
    gate_up,
    down_proj,
    norm_gain,
    mlp_gain,
    conv_filter,
    decay_log,
    skip_gain,
    step_bias,
    gated_gain,
    cotangent,
):
    tensor_count = lax.axis_size("tensor")
    rows, model = residual.shape
    depth = mixer_in.shape[0]
    ssm = conv_filter.shape[1] - 2 * NS
    heads = ssm // PH
    groups = heads // GROUP
    chunks = rows // CHUNK
    span = LEN // rows
    part = lax.axis_index("tensor") % span
    onward = [(i, i + 1) for i in range(tensor_count) if i % span != span - 1]
    backward = [(j, i) for i, j in onward]
    hidden_w = gate_up.shape[2]
    gate_w = mixer_in.shape[2]
    query_w = query_in.shape[1]
    shared_w = shared_in.shape[1]
    attn_w = AH * HD
    ff = hidden_w * tensor_count
    steps = len(high_bits())

    def finish_dp(parts, got, deps):
        for i in range(2, steps):
            parts = collect_add(parts, got, deps)
            got = collect_move(parts, i)
        return collect_end([(parts, got)], deps)

    def finish_tensor(joined):
        total = lax.psum_scatter(joined, "tensor", scatter_dimension=0, tiled=False)
        return total.astype(f32)

    before_rows = lax.ppermute(residual[rows - HALO :], "tensor", onward)
    ext_low = permute_features(jnp.concatenate([before_rows, residual], axis=0))
    cot = permute_features(cotangent)
    gain_first = permute_features(norm_gain)
    gain_second = permute_features(mlp_gain)
    ext_normed, ext_inv = norm_of(ext_low.astype(f32))
    ext_in = (ext_normed * gain_first).astype(bf16)
    normed_first = ext_normed[HALO:]
    inv_first = ext_inv[HALO:]
    normed_in = ext_in[HALO:]
    group_rows = ext_low[HALO:].astype(f32)
    wide_f32 = shape((rows, model), f32)
    wide_low = shape((rows, model), bf16)
    second_row = gain_second[None, :]

    half = HD // 2
    frequency = rope_base ** (-2.0 * jnp.arange(half, dtype=f32) / HD)
    place = (part * rows + jnp.arange(rows, dtype=jnp.int32)).astype(f32)
    angles = place[:, None] * frequency[None, :]
    cosine = jnp.cos(angles)
    sine = jnp.sin(angles)
    ones = jnp.ones((rows, HD), f32)
    cos_q = jnp.concatenate([cosine] * 4, axis=1)
    sin_q = jnp.concatenate([-sine, sine] * 2, axis=1)
    cos_kv = jnp.concatenate([cosine, cosine, ones], axis=1)
    sin_kv = jnp.concatenate([-sine, sine, 0.0 * ones], axis=1)

    def padded(parts):
        width = sum(p.shape[1] for p in parts)
        return jnp.concatenate(parts + [jnp.zeros((depth, -width % 128), bf16)], axis=1)

    val_in = padded([mixer_in[:, 1], shared_in, step_in])
    gate_in = padded([mixer_in[:, 0], query_in, keyval_in])
    val_w = val_in.shape[1]
    out_in = jnp.concatenate([mixer_proj, attn_proj], axis=0).T
    out_w = out_in.shape[1]
    in_z = over_tensor(jnp.concatenate([val_in, gate_in], axis=1))
    back_z = over_tensor(jnp.concatenate([out_in, down_proj.T], axis=1))
    tables = (cos_q, sin_q, cos_kv, sin_kv)
    (val_held,) = cut_pieces(in_z, [(0, val_w)], (ext_in, tables, cot, group_rows))
    val_got = spread_send(val_held, 0)
    val_held = join(val_held, val_got)
    val_got = spread_send(val_held, 1)
    (gate_held,) = cut_pieces(in_z, [(val_w, in_z.shape[2])], val_held)
    gate_got = spread_send(gate_held, 0)
    for i in range(1, steps - 1):
        val_held = join(val_held, val_got, gate_held)
        val_got = spread_send(val_held, i + 1)
    val_held, gate_held = join_all(
        [(val_held, val_got, True), (gate_held, gate_got, False)], gate_held
    )
    in_b = spread_end(val_held)
    gate_got = spread_send(gate_held, 1)
    ff_in = slice_one(gate_up.reshape(1, depth, 2 * hidden_w), 0, 2 * hidden_w, val_held)
    ff_z = over_tensor(ff_in[0])

    (out_held,) = cut_pieces(back_z, [(0, out_w)], gate_held)
    out_got = spread_send(out_held, 0)
    (proj_b,) = times(
        ext_in,
        in_b,
        [shape((rows + HALO, val_w * tensor_count), f32)],
        store,
        deps=(gate_held, out_held),
    )
    for i in range(1, steps - 1):
        gate_held = join(gate_held, gate_got, proj_b)
        gate_got = spread_send(gate_held, i + 1)
    gate_held, out_held = join_all(
        [(gate_held, gate_got, True), (out_held, out_got, False)], proj_b
    )
    in_a = spread_end(gate_held)
    out_got = spread_send(out_held, 1)

    ext = rows + HALO
    whole = lambda *dims: spec(dims, lambda i: (0,) * len(dims))
    tail = lambda count, t: (lambda i: (0, count * t + count - 1))
    per_val = val_w // 128
    bias_row = jnp.pad(step_bias, (0, 128 - heads))[None, :]
    rate_row = jnp.pad(jnp.exp(decay_log), (0, 128 - heads))[None, :]
    shr, step_lin, cols, cum_rows, grow = call(
        prepare_kernel,
        (1,),
        [spec((ext, 128), tail(per_val, t)) for t in range(4)] + [whole(1, 128)] * 2,
        [
            whole(ext, 2 * NS),
            whole(rows, 128),
            whole(groups, rows, 2 * SLOT),
            whole(groups, SLOT, rows),
            whole(rows, 128),
        ],
        [
            shape((ext, 2 * NS), f32),
            shape((rows, 128), f32),
            shape((groups, rows, 2 * SLOT), f32),
            shape((groups, SLOT, rows), f32),
            shape((rows, 128), f32),
        ],
        moved=rows * 128 * 40,
    )(proj_b, proj_b, proj_b, proj_b, bias_row, rate_row)
    skip_lanes = jnp.repeat(skip_gain, PH)[None, :]

    val_spec = spec((ext, val_w), lambda g: (0, g))
    shr_spec = whole(ext, 2 * NS)
    tapv_spec = spec((KC, GW), lambda g: (0, g))
    taps_spec = spec((KC, 2 * NS), lambda g: (0, ssm // (2 * NS)))
    col_spec = spec((1, rows, 2 * SLOT), lambda g: (g, 0, 0))
    row_spec = spec((1, SLOT, rows), lambda g: (g, 0, 0))
    lane_spec = spec((1, GW), lambda g: (0, g))
    bc_spec = whole(rows, 2 * NS)
    grp_spec = spec((rows, GW), lambda g: (0, g))
    state_spec = spec((NS, GW), lambda g: (0, g))
    y_local, state_local, bc_act = call(
        mixer_kernel,
        (groups,),
        [val_spec, shr_spec, tapv_spec, taps_spec, col_spec, row_spec, lane_spec],
        [grp_spec, state_spec, bc_spec],
        [shape((rows, ssm), f32), shape((NS, ssm), bf16), shape((rows, 2 * NS), bf16)],
        [pltpu.VMEM((chunks, CHUNK, CHUNK), f32)],
        flops=2 * rows * ssm * 512,
        moved=rows * ssm * 8,
        deps=(gate_held, out_held),
    )(proj_b, shr, conv_filter, conv_filter, cols, cum_rows, skip_lanes)
    entering = lax.ppermute(state_local, "tensor", onward)
    per_gate = gate_held[0].shape[2] // 128
    out_held = spread_rest(out_held, out_got, 1, y_local)
    out_full = spread_end(out_held)
    (ff_held,) = cut_pieces(ff_z, [(0, 2 * hidden_w)], out_held)
    ff_got = spread_send(ff_held, 0)
    (proj_a,) = times(
        normed_in,
        in_a,
        [shape((rows, per_gate * 128 * tensor_count), f32)],
        store,
        deps=(out_held, ff_held),
    )
    ff_held = join(ff_held, ff_got, (proj_a, entering))
    ff_got = spread_send(ff_held, 1)

    kv_w = 2 * KVH * HD
    own_kv = call(
        rotate_kernel,
        (1,),
        [spec((rows, 128), tail(per_gate, t)) for t in range(4)] + [whole(rows, 2 * HD)] * 2,
        whole(rows, kv_w),
        shape((rows, kv_w), bf16),
        moved=rows * kv_w * 12,
    )(proj_a, proj_a, proj_a, proj_a, cos_kv, sin_kv)
    before_kv = lax.ppermute(own_kv, "tensor", onward)
    part_arg = part.astype(jnp.int32).reshape(1)
    pairs = AH // 2
    per_kv = AH // KVH // 2
    smem = pl.BlockSpec(memory_space=pltpu.SMEM)
    q_spec = spec((rows, 2 * HD), lambda i: (0, per_gate * i + GW // 128))
    table_spec = spec((rows, 2 * HD), lambda i: (0, 0))
    kv_spec = spec((rows, 2 * HD), lambda i: (0, i // per_kv))
    pair_spec = spec((rows, 2 * HD), lambda i: (0, i))
    attn_heads = call(
        attend_kernel,
        (pairs,),
        [smem, q_spec, table_spec, table_spec, kv_spec, kv_spec],
        pair_spec,
        shape((rows, attn_w), bf16),
        flops=2 * AH * rows * LEN * 256,
        moved=rows * attn_w * 8,
        deps=ff_held,
    )(part_arg, proj_a, cos_q, sin_q, before_kv, own_kv)

    (down_held,) = cut_pieces(back_z, [(out_w, back_z.shape[2])], (attn_heads, out_full))
    down_got = spread_send(down_held, 0)
    block_rows = CHUNK
    wide = spec((block_rows, ssm), lambda i: (i, 0))
    gate_block = spec((block_rows, proj_a.shape[1]), lambda i: (i, 0))
    heads_block = spec((block_rows, ssm + attn_w), lambda i: (i, 0))
    attn_block = spec((block_rows, attn_w), lambda i: (i, 0))
    bc_block = spec((block_rows, 2 * NS), lambda i: (i, 0))
    grow_block = spec((block_rows, 128), lambda i: (i, 0))
    state_whole = whole(NS, ssm)
    gain_whole = whole(1, ssm)
    gated_row = gated_gain[None, :]
    scanned, heads_all = call(
        finish_kernel,
        (rows // block_rows,),
        [wide, gate_block, bc_block, grow_block, state_whole, gain_whole, attn_block],
        [wide, heads_block],
        [shape((rows, ssm), f32), shape((rows, ssm + attn_w), bf16)],
        flops=2 * rows * ssm * NS,
        moved=rows * ssm * 14,
        deps=down_held,
    )(y_local, proj_a, bc_act, grow, entering, gated_row, attn_heads)

    ff_held = spread_rest(ff_held, ff_got, 1, heads_all)
    ff_full = spread_end(ff_held)
    middle, mlp_rows = times_transposed(
        [heads_all],
        out_full,
        [wide_f32, wide_low],
        middle_finish,
        (group_rows, second_row),
        deps=ff_held,
    )
    down_held = join(down_held, down_got, middle)
    down_got = spread_send(down_held, 1)
    unit = spec((rows, hidden_w), lambda i: (0, i))
    ff_low = shape((rows, ff), bf16)
    hidden, by_gate, by_up = times(
        mlp_rows, ff_full, [ff_low] * 3, unit_finish, out_specs=[unit] * 3, deps=down_held
    )
    down_held = spread_rest(down_held, down_got, 1, hidden)
    down_full = spread_end(down_held)
    down_send, down_got = collect_send(cot, hidden, down_held)
    (both_grad,) = times(
        cot,
        down_full,
        [shape((rows, 2 * ff), bf16)],
        unit_back_finish,
        (by_gate, by_up),
        (unit, unit),
        [spec((rows, 2 * hidden_w), lambda i: (0, i))],
        deps=down_send,
    )
    down_sum = collect_keep(cot, hidden, down_got, both_grad)
    down_got = collect_move(down_sum, 0)
    ff_send, ff_got = collect_send(mlp_rows, both_grad, down_sum)
    middle_grad, branch_grad, mlp_gain_part = times_transposed(
        [both_grad],
        ff_full,
        [wide_f32, wide_low, shape((1, model), f32)],
        middle_back_finish,
        (middle, cot, second_row),
        deps=(ff_send, down_sum),
    )

    down_sum = collect_add(down_sum, down_got, branch_grad)
    down_got = collect_move(down_sum, 1)
    (heads_grad,) = times(
        branch_grad, out_full, [shape((rows, ssm + attn_w), f32)], store, deps=down_sum
    )
    out_send, out_got = collect_send(branch_grad, heads_all, heads_grad)
    ff_sum = collect_keep(mlp_rows, both_grad, ff_got, out_send)
    ff_got = collect_move(ff_sum, 0)
    dgate, dscan, gated_gain_part, dstate_local = call(
        ungate_kernel,
        (rows // block_rows,),
        [heads_block, wide, gate_block, bc_block, grow_block, gain_whole],
        [wide, wide, gain_whole, state_whole],
        [
            shape((rows, ssm), bf16),
            shape((rows, ssm), f32),
            shape((1, ssm), f32),
            shape((NS, ssm), f32),
        ],
        flops=2 * rows * ssm * NS,
        moved=rows * ssm * 18,
        deps=(out_send, ff_sum),
    )(heads_grad, scanned, proj_a, bc_act, grow, gated_row)
    leaving_grad = lax.ppermute(dstate_local.astype(bf16), "tensor", backward)
    down_z = finish_dp(down_sum, down_got, dgate)
    down_t = finish_tensor(down_z)
    gate_send, gate_got = collect_send(normed_in, dgate, down_z)
    out_sum = collect_keep(branch_grad, heads_all, out_got, gate_send, 0)
    out_got = move_one(out_sum, 0, 0)
    (output,) = times_transposed(
        [hidden], down_full, [wide_f32], add_store, (middle,), deps=out_sum
    )
    gate_sum = collect_keep(normed_in, dgate, gate_got, (output, leaving_grad), 1)
    gate_got = move_one(gate_sum, 1, 0)
    (output,) = restore_all([output], gate_sum)

    dout_spec = spec((rows, 2 * HD), lambda i: (0, 4 * i + 3))
    qk_low, before_grad, own_grad = call(
        unattend_kernel,
        (pairs,),
        [smem, q_spec, table_spec, table_spec, kv_spec, kv_spec, dout_spec],
        [spec((rows, 2 * HD), lambda i: (0, 2 * i)), kv_spec, kv_spec],
        [shape((rows, 4 * HD * pairs), bf16), shape((rows, kv_w), f32), shape((rows, kv_w), f32)],
        flops=2 * AH * rows * LEN * 640,
        moved=rows * attn_w * 16,
        deps=(out_sum, gate_sum, output),
    )(part_arg, proj_a, cos_q, sin_q, before_kv, own_kv, heads_grad)
    late_grad = lax.ppermute(before_grad.astype(bf16), "tensor", backward)

    ff_sum = collect_add(ff_sum, ff_got, before_grad)
    ff_got = collect_move(ff_sum, 1)
    out_sum = add_one(out_sum, out_got, 0, 0, ff_sum)
    out_got = move_one(out_sum, 0, 1)
    gate_sum = add_one(gate_sum, gate_got, 1, 0, out_sum)
    gate_got = move_one(gate_sum, 1, 1)
    half_spec = spec((rows, 2 * HD), lambda t: (0, t // 2))
    qk_low = call(
        unrotate_kernel,
        (tensor_count,),
        [pl.BlockSpec(memory_space=pl.ANY), half_spec, half_spec] + [whole(rows, 2 * HD)] * 2,
        spec((rows, 2 * HD), lambda t: (0, 2 * t + 1)),
        shape(qk_low.shape, bf16),
        moved=rows * kv_w * 16,
        aliases={0: 0},
        deps=(ff_sum, out_sum, gate_sum),
    )(qk_low, own_grad, late_grad, cos_kv, sin_kv)

    qk_send, qk_got = collect_send(normed_in, qk_low)

    low_v, dshr, dcols, drows, dlast, dtapv, dtaps, dskip = call(
        unmix_kernel,
        (groups,),
        [
            val_spec, shr_spec, tapv_spec, taps_spec, col_spec, row_spec, lane_spec,
            bc_spec, grp_spec, state_spec, state_spec,
        ],
        [
            val_spec,
            shr_spec,
            spec((1, rows, 128), lambda g: (g, 0, 0)),
            row_spec,
            spec((chunks, GW), lambda g: (0, g)),
            tapv_spec,
            whole(KC, 2 * NS),
            lane_spec,
        ],
        [
            shape((ext, val_w * tensor_count), bf16),
            shape((ext, 2 * NS), f32),
            shape((groups, rows, 128), f32),
            shape((groups, SLOT, rows), f32),
            shape((chunks, ssm), f32),
            shape((KC, ssm), f32),
            shape((KC, 2 * NS), f32),
            shape((1, ssm), f32),
        ],
        [
            pltpu.VMEM((chunks, CHUNK, CHUNK), f32),
            pltpu.VMEM((rows, 2 * NS), f32),
            pltpu.VMEM((chunks, CHUNK, CHUNK), f32),
            pltpu.VMEM((rows, GW), f32),
            pltpu.VMEM((chunks, NS, GW), f32),
            pltpu.VMEM((rows + HALO + 16, GW), f32),
        ],
        flops=2 * rows * ssm * 1280,
        moved=rows * ssm * 12,
        deps=(ff_sum, out_sum, gate_sum, qk_send),
    )(
        proj_b, shr, conv_filter, conv_filter, cols, cum_rows, skip_lanes,
        bc_act, dscan, entering, leaving_grad,
    )
    def rest_dp(parts, got, deps=()):
        for i in range(2, steps):
            parts = collect_add(parts, got, deps)
            got = collect_move(parts, i)
        return parts, got

    def rest_one_way(parts, got, route, deps):
        for i in range(2, steps):
            parts = add_one(parts, got, route, i - 1, deps)
            got = move_one(parts, route, i)
        return parts, got

    ends = collect_end(
        [
            rest_dp(ff_sum, ff_got, low_v),
            rest_one_way(out_sum, out_got, 0, low_v),
            rest_one_way(gate_sum, gate_got, 1, low_v),
        ],
        low_v,
    )
    ends_t = finish_tensor(ends)
    ff_t = ends_t[:, : 2 * hidden_w]
    out_t = ends_t[:, 2 * hidden_w : 2 * hidden_w + out_w]
    gate_t = ends_t[:, 2 * hidden_w + out_w :]
    low_v, decay_part, bias_part = call(
        settle_kernel,
        (tensor_count,),
        [
            pl.BlockSpec(memory_space=pl.ANY),
            shr_spec,
            whole(groups, rows, 128),
            whole(groups, SLOT, rows),
            whole(chunks, ssm),
            whole(rows, 128),
            whole(1, 128),
        ],
        [
            spec((ext, 128), lambda t: (0, per_val * t + per_val - 1)),
            whole(1, 128),
            whole(1, 128),
        ],
        [shape(low_v.shape, bf16), shape((1, 128), f32), shape((1, 128), f32)],
        [pltpu.VMEM((rows, 128), f32)],
        moved=rows * 128 * 60,
        aliases={0: 0},
        deps=ends,
    )(low_v, dshr, dcols, drows, dlast, step_lin, rate_row)
    qk_sum = collect_keep(normed_in, qk_low, qk_got, ends)
    qk_got = collect_move(qk_sum, 0)
    val_send, val_got = collect_send(ext_in, low_v, qk_sum)
    (grad_a,) = times_transposed([dgate, qk_low], in_a, [wide_f32], store, deps=val_send)
    val_sum = collect_keep(ext_in, low_v, val_got, grad_a)
    val_got = collect_move(val_sum, 0)
    qk_sum = collect_add(qk_sum, qk_got, val_sum)
    qk_got = collect_move(qk_sum, 1)
    (grad_b,) = times_transposed(
        [low_v], in_b, [shape((ext, model), f32)], store, deps=(val_sum, qk_sum)
    )
    val_sum = collect_add(val_sum, val_got, grad_b)
    val_got = collect_move(val_sum, 1)
    late_rows = lax.ppermute(grad_b[:HALO], "tensor", backward)
    residual_grad, gain_sums = call(
        first_back_kernel,
        (1,),
        [
            whole(rows, model), whole(ext, model), whole(HALO, model), whole(rows, model),
            whole(rows, model), whole(1, model), whole(1, model),
        ],
        [whole(rows, model), whole(8, model)],
        [wide_f32, shape((8, model), f32)],
        deps=val_sum,
    )(
        grad_a, grad_b, late_rows, ext_low[HALO:], middle_grad, gain_first[None, :], mlp_gain_part
    )
    residual_grad, gain_sums = restore_all([residual_grad, gain_sums])
    last_t = finish_tensor(collect_end([rest_dp(val_sum, val_got), rest_dp(qk_sum, qk_got)]))
    gate_up_sum = ff_t.reshape(depth, 2, hidden_w)
    val_t = last_t[:, :val_w]
    qk_t = last_t[:, val_w:]
    skip_part = dskip.reshape(heads, PH).sum(axis=-1)

    small = [
        gain_sums[0],
        gain_sums[1],
        jnp.concatenate([dtapv, dtaps], axis=1).reshape(-1),
        decay_part[0, :heads],
        skip_part,
        bias_part[0, :heads],
        gated_gain_part[0],
    ]
    sizes = [item.shape[0] for item in small]
    total = sum_all(jnp.concatenate(small))
    marks = [sum(sizes[:i]) for i in range(len(sizes) + 1)]
    sums = [total[marks[i] : marks[i + 1]] for i in range(len(sizes))]
    return (
        output,
        residual_grad,
        jnp.stack([gate_t, val_t[:, :gate_w]], axis=1),
        val_t[:, gate_w + shared_w : gate_w + shared_w + step_in.shape[1]],
        val_t[:, gate_w : gate_w + shared_w],
        qk_t[:, :query_w],
        qk_t[:, query_w : query_w + keyval_in.shape[1]],
        out_t[:, :gate_w].T,
        out_t[:, gate_w:].T,
        gate_up_sum,
        down_t.T,
        sums[0],
        sums[1],
        sums[2].reshape(conv_filter.shape),
        sums[3],
        sums[4],
        sums[5],
        sums[6],
    )


def solution(mesh):
    rows_spec = P(("dp", "tensor"), None)
    into = P("dp", "tensor")
    out_of = P("tensor", "dp")
    double = P("dp", None, "tensor")
    weights = (double, into, into, into, into, out_of, out_of, double, out_of)
    return jax.shard_map(
        shards,
        mesh=mesh,
        in_specs=(rows_spec,) + weights + (P(),) * 7 + (rows_spec,),
        out_specs=(rows_spec, rows_spec) + weights + (P(),) * 7,
        check_vma=False,
    )
```

```python
import functools

import jax
import jax.numpy as jnp
from jax import lax
from jax.experimental import pallas as pl
from jax.experimental.pallas import tpu as pltpu
from jax.sharding import PartitionSpec as P

PH = 64
NS = 128
KC = 4
AH = 8
KVH = 2
HD = 64
LEN = 1024
CHUNK = 128
HALO = 16
GROUP = 6
SLOT = 8
GW = GROUP * PH

epsilon = 1e-05
rope_base = 100000000000.0
masked_fill = -1e30
highest = lax.Precision.HIGHEST
f32 = jnp.float32
bf16 = jnp.bfloat16
VMEM_BYTES = 52 * 1024 * 1024


def call(
    kernel, grid, in_specs, out_specs, out_shape, scratch=(), flops=0, moved=0, aliases=None, deps=()
):
    late = jax.tree.leaves(deps)
    count = len(in_specs)

    def body(*refs):
        kernel(*refs[:count], *refs[count + len(late) :])

    run = pl.pallas_call(
        body,
        grid=grid,
        in_specs=list(in_specs) + [pl.BlockSpec(memory_space=pl.ANY)] * len(late),
        out_specs=out_specs,
        out_shape=out_shape,
        scratch_shapes=list(scratch),
        input_output_aliases=aliases or {},
        compiler_params=pltpu.CompilerParams(
            vmem_limit_bytes=VMEM_BYTES, dimension_semantics=("arbitrary",) * len(grid)
        ),
        cost_estimate=pl.CostEstimate(flops=1, bytes_accessed=1, transcendentals=0),
    )
    return lambda *args: run(*args, *late)


def spec(block, index):
    return pl.BlockSpec(block, index)


def shape(dims, kind):
    return jax.ShapeDtypeStruct(dims, kind)


def dot(left, right, dims):
    return lax.dot_general(left, right, ((dims[:1], dims[1:]), ((), ())), preferred_element_type=f32)


NN = (1, 0)
NT = (1, 1)
TN = (0, 0)


def sigmoid(value):
    return 1.0 / (1.0 + jnp.exp(-value))


def pair_lanes(left, right, rows):
    lane = lax.broadcasted_iota(jnp.int32, (rows, 2 * PH), 1)
    return jnp.where(lane < PH, left, right)


def spread_heads(columns, first, count, rows):
    parts = [
        pair_lanes(
            columns[:, first + 2 * p : first + 2 * p + 1],
            columns[:, first + 2 * p + 1 : first + 2 * p + 2],
            rows,
        )
        for p in range(count // 2)
    ]
    return jnp.concatenate(parts, axis=1) if len(parts) > 1 else parts[0]


def conv_of(ref, taps, rows):
    width = taps.shape[1]
    total = ref[pl.ds(HALO - KC + 1, rows), :width] * taps[0:1, :]
    for offset in range(1, KC):
        moved = ref[pl.ds(HALO - KC + 1 + offset, rows), :width]
        total = total + moved * taps[offset : offset + 1, :]
    return total


def causal_mask(transposed):
    row = lax.broadcasted_iota(jnp.int32, (CHUNK, CHUNK), 0)
    col = lax.broadcasted_iota(jnp.int32, (CHUNK, CHUNK), 1)
    return col >= row if transposed else row >= col


def exact(left, right, dims):
    return lax.dot_general(
        left,
        right,
        ((dims[:1], dims[1:]), ((), ())),
        precision=highest,
        preferred_element_type=f32,
    )


def lower_ones():
    return jnp.where(causal_mask(False), 1.0, 0.0)


def softplus(value):
    return jnp.maximum(value, 0.0) + jnp.log1p(jnp.exp(-jnp.abs(value)))


def prepare_kernel(
    t0_ref, t1_ref, t2_ref, t3_ref, bias_ref, rate_ref,
    shr_ref, step_ref, cols_ref, rows_ref, grow_ref,
):
    tails = [t0_ref[...], t1_ref[...], t2_ref[...], t3_ref[...]]
    ext = tails[0].shape[0]
    shr_ref[:, :NS] = pair_lanes(tails[0], pltpu.roll(tails[1], PH, 1), ext)
    shr_ref[:, NS:] = pair_lanes(tails[2], pltpu.roll(tails[3], PH, 1), ext)
    rows = ext - HALO
    lane = lax.broadcasted_iota(jnp.int32, (rows, 128), 1)
    steps = jnp.zeros((rows, 128), f32)
    for t in range(4):
        moved = pltpu.roll(tails[t][HALO:], (GROUP * t - PH) % 128, 1)
        steps = jnp.where(lane // GROUP == t, moved, steps)
    steps = steps + bias_ref[...]
    step_ref[...] = steps
    dt = softplus(steps)
    decay = -rate_ref[...] * dt
    lower = lower_ones()
    prefix = jnp.zeros((1, 128), f32)
    parts = []
    for c in range(rows // CHUNK):
        sl = slice(c * CHUNK, (c + 1) * CHUNK)
        cum = exact(lower, decay[sl], NN)
        parts.append(cum)
        grow_ref[sl, :] = jnp.exp(cum + prefix)
        prefix = prefix + cum[CHUNK - 1 : CHUNK]
    cum = jnp.concatenate(parts, axis=0)
    for t in range(4):
        shift = (-GROUP * t) % 128
        dt_own = pltpu.roll(dt, shift, 1) if t else dt
        cum_own = pltpu.roll(cum, shift, 1) if t else cum
        both = jnp.where(lane < SLOT, dt_own, pltpu.roll(cum_own, SLOT, 1))
        cols_ref[t] = both[:, : 2 * SLOT]
        rows_ref[t] = jnp.transpose(cum_own)[:SLOT]


def mixer_kernel(
    val_ref, shr_ref, tapv_ref, taps_ref, cols_ref, cumr_ref, skip_ref,
    y_ref, state_ref, bc_ref, aff_ref,
):
    rows = y_ref.shape[0]
    chunks = rows // CHUNK

    @pl.when(pl.program_id(0) == 0)
    def _():
        pre = conv_of(shr_ref, taps_ref[...], rows)
        bc_ref[...] = (pre * sigmoid(pre)).astype(bf16)
        for c in range(chunks):
            sl = pl.ds(c * CHUNK, CHUNK)
            aff_ref[c] = dot(bc_ref[sl, NS:], bc_ref[sl, :NS], NT)

    pre = conv_of(val_ref, tapv_ref[...], rows)
    head_in = pre * sigmoid(pre)
    mask = causal_mask(False)
    skip = skip_ref[...]
    state = jnp.zeros((NS, GW), f32)
    for c in range(chunks):
        sl = pl.ds(c * CHUNK, CHUNK)
        x = head_in[c * CHUNK : (c + 1) * CHUNK]
        cols = cols_ref[0, sl, :]
        cumc = cols[:, SLOT:]
        cumr = cumr_ref[0, :, sl]
        w = x * spread_heads(cols, 0, GROUP, CHUNK)
        w_low = w.astype(bf16)
        inner = []
        for p in range(GROUP // 2):
            both = []
            for h in (2 * p, 2 * p + 1):
                gap = cumc[:, h : h + 1] - cumr[h : h + 1, :]
                decay = jnp.exp(jnp.where(mask, gap, masked_fill))
                weight = (aff_ref[c] * decay).astype(bf16)
                both.append(dot(weight, w_low[:, p * 2 * PH : (p + 1) * 2 * PH], NN))
            inner.append(pair_lanes(both[0], both[1], CHUNK))
        out = jnp.concatenate(inner, axis=1) + skip * x
        b_now = bc_ref[sl, :NS]
        c_now = bc_ref[sl, NS:]
        last = cumc[CHUNK - 1 : CHUNK, :]
        if c > 0:
            grown = spread_heads(jnp.exp(cumc), 0, GROUP, CHUNK)
            out = out + dot(c_now, state.astype(bf16), NN) * grown
        y_ref[sl, :] = out
        to_end = spread_heads(jnp.exp(last - cumc), 0, GROUP, CHUNK)
        added = dot(b_now, (w * to_end).astype(bf16), TN)
        fall = spread_heads(jnp.exp(last), 0, GROUP, 1)
        state = state * fall + added
    state_ref[...] = state.astype(bf16)


def gate_lanes(ref, width):
    count = ref.shape[1] // (width + 2 * PH * 2)
    step = ref.shape[1] // count
    return jnp.concatenate([ref[:, t * step : t * step + width] for t in range(count)], axis=1)


def finish_kernel(
    y_ref, gate_ref, bc_ref, grow_ref, state_ref, gain_ref, attn_ref, scan_ref, heads_ref
):
    rows, width = y_ref.shape
    grown = spread_heads(grow_ref[...], 0, width // PH, rows)
    scan = y_ref[...] + dot(bc_ref[:, NS:], state_ref[...], NN) * grown
    scan_ref[...] = scan
    gate = gate_lanes(gate_ref, GW)
    pre = scan * gate * sigmoid(gate)
    inv = lax.rsqrt(jnp.mean(pre * pre, axis=1, keepdims=True) + epsilon)
    low = (pre * inv * gain_ref[...]).astype(bf16)
    step = GW + 2 * HD
    for t in range(width // GW):
        heads_ref[:, t * step : t * step + GW] = low[:, t * GW : (t + 1) * GW]
        heads_ref[:, t * step + GW : (t + 1) * step] = attn_ref[:, t * 2 * HD : (t + 1) * 2 * HD]


def ungate_kernel(
    grad_ref, scan_ref, gate_ref, bc_ref, grow_ref, gain_ref,
    dgate_ref, dscan_ref, dgain_ref, dstate_ref,
):
    rows, width = scan_ref.shape
    scan = scan_ref[...]
    gate = gate_lanes(gate_ref, GW)
    sig = sigmoid(gate)
    silu = gate * sig
    pre = scan * silu
    inv = lax.rsqrt(jnp.mean(pre * pre, axis=1, keepdims=True) + epsilon)
    normed = pre * inv
    step = GW + 2 * HD
    grad = jnp.concatenate(
        [grad_ref[:, t * step : t * step + GW] for t in range(width // GW)], axis=1
    )
    u = grad * gain_ref[...]
    cross = jnp.mean(u * normed, axis=1, keepdims=True)
    dpre = inv * (u - normed * cross)
    dscan = dpre * silu
    dgate_ref[...] = (dpre * scan * sig * (1.0 + gate * (1.0 - sig))).astype(bf16)
    dscan_ref[...] = dscan
    grown = spread_heads(grow_ref[...], 0, width // PH, rows)
    dstate = dot(bc_ref[:, NS:], (dscan * grown).astype(bf16), TN)
    dgain = jnp.sum(grad * normed, axis=0, keepdims=True)
    first = pl.program_id(0) == 0

    @pl.when(first)
    def _():
        dgain_ref[...] = dgain
        dstate_ref[...] = dstate

    @pl.when(jnp.logical_not(first))
    def _():
        dgain_ref[...] += dgain
        dstate_ref[...] += dstate


def split_sum(value, ones_at):
    high = value.astype(bf16)
    low = (value - high.astype(f32)).astype(bf16)
    return dot(high, ones_at, NN) + dot(low, ones_at, NN)


def unconv(ref, taps, dact, pad_ref, out_ref, dtaps_ref, rows):
    pre = conv_of(ref, taps, rows)
    sig = sigmoid(pre)
    dpre = dact * sig * (1.0 + pre * (1.0 - sig))
    lead = HALO + 8
    width = dact.shape[1]
    pad_ref[pl.ds(0, lead), :width] = jnp.zeros((lead, width), f32)
    pad_ref[pl.ds(lead + rows, 8), :width] = jnp.zeros((8, width), f32)
    pad_ref[pl.ds(lead, rows), :width] = dpre
    total = None
    dtaps = []
    for offset in range(KC):
        part = pad_ref[pl.ds(8 + KC - 1 - offset, rows + HALO), :width]
        part = part * taps[offset : offset + 1, :]
        total = part if total is None else total + part
        moved = ref[pl.ds(HALO - KC + 1 + offset, rows), :width]
        dtaps.append(jnp.sum(dpre * moved, axis=0, keepdims=True))
    out_ref[:, :width] = total.astype(out_ref.dtype)
    dtaps_ref[...] = jnp.concatenate(dtaps, axis=0)


def unmix_kernel(
    val_ref, shr_ref, tapv_ref, taps_ref, in_ref, cumr_ref, skip_ref, bc_ref,
    dscan_ref, enter_ref, dleave_ref,
    dval_ref, dshr_ref, cols_ref, rows_ref, dlast_ref, dtapv_ref, dtaps_ref, dskip_ref,
    daff_ref, dbc_ref, aff_ref, dx_ref, states_ref, pad_ref,
):
    rows = dscan_ref.shape[0]
    chunks = rows // CHUNK
    step = pl.program_id(0)

    @pl.when(step == 0)
    def _():
        for c in range(chunks):
            sl = pl.ds(c * CHUNK, CHUNK)
            aff_ref[c] = dot(bc_ref[sl, :NS], bc_ref[sl, NS:], NT)
        daff_ref[...] = jnp.zeros(daff_ref.shape, f32)
        dbc_ref[...] = jnp.zeros(dbc_ref.shape, f32)

    pre = conv_of(val_ref, tapv_ref[...], rows)
    dx_ref[...] = pre * sigmoid(pre)
    mask = causal_mask(True)
    skip = skip_ref[...]
    lane = lax.broadcasted_iota(jnp.int32, (GW, 128), 0) // PH
    slot = lax.broadcasted_iota(jnp.int32, (GW, 128), 1)
    ones_dt = jnp.where(lane == slot, 1.0, 0.0).astype(bf16)
    ones_cum = jnp.where(lane + SLOT == slot, 1.0, 0.0).astype(bf16)
    half_lane = lax.broadcasted_iota(jnp.int32, (CHUNK, 2 * PH), 1) // PH
    slot_lane = lax.broadcasted_iota(jnp.int32, (CHUNK, 128), 1)

    state = enter_ref[...].astype(f32)
    states_ref[0] = state
    for c in range(chunks - 1):
        sl = pl.ds(c * CHUNK, CHUNK)
        cumc = in_ref[0, sl, SLOT:]
        last = cumc[CHUNK - 1 : CHUNK, :]
        scale = spread_heads(in_ref[0, sl, :SLOT] * jnp.exp(last - cumc), 0, GROUP, CHUNK)
        added = dot(bc_ref[sl, :NS], (dx_ref[sl, :] * scale).astype(bf16), TN)
        state = state * spread_heads(jnp.exp(last), 0, GROUP, 1) + added
        states_ref[c + 1] = state

    dstate = dleave_ref[...].astype(f32)
    dskip = jnp.zeros((1, GW), f32)
    for c in reversed(range(chunks)):
        sl = pl.ds(c * CHUNK, CHUNK)
        x = dx_ref[sl, :]
        dy = dscan_ref[sl, :]
        dy_low = dy.astype(bf16)
        cumc = in_ref[0, sl, SLOT:]
        cumr = cumr_ref[0, :, sl]
        last = cumc[CHUNK - 1 : CHUNK, :]
        dt = spread_heads(in_ref[0, sl, :SLOT], 0, GROUP, CHUNK)
        w = x * dt
        w_low = w.astype(bf16)
        b_now = bc_ref[sl, :NS]
        c_now = bc_ref[sl, NS:]
        affinity = aff_ref[c]
        dcum = jnp.zeros((CHUNK, 128), f32)
        daff = daff_ref[c]
        dw_parts = []
        for p in range(GROUP // 2):
            pair = slice(p * 2 * PH, (p + 1) * 2 * PH)
            both = []
            for h in (2 * p, 2 * p + 1):
                gap = cumr[h : h + 1, :] - cumc[:, h : h + 1]
                decay = jnp.exp(jnp.where(mask, gap, masked_fill))
                weight = affinity * decay
                w_own = jnp.where(half_lane == h - 2 * p, w[:, pair], 0.0).astype(bf16)
                dweight = dot(w_own, dy_low[:, pair], NT)
                daff = daff + dweight * decay
                moved = dweight * weight
                rows_ref[0, h : h + 1, sl] = jnp.sum(moved, axis=0, keepdims=True)
                dcum = dcum - jnp.where(
                    slot_lane == SLOT + h, jnp.sum(moved, axis=1, keepdims=True), 0.0
                )
                both.append(dot(weight.astype(bf16), dy_low[:, pair], NN))
            dw_parts.append(pair_lanes(both[0], both[1], CHUNK))
        daff_ref[c] = daff
        state = states_ref[c]
        state_low = state.astype(bf16)
        dstate_low = dstate.astype(bf16)
        grown = spread_heads(jnp.exp(cumc), 0, GROUP, CHUNK)
        to_end = spread_heads(jnp.exp(last - cumc), 0, GROUP, CHUNK)
        fall = spread_heads(jnp.exp(last), 0, GROUP, 1)
        dy_grown = (dy * grown).astype(bf16)
        carried = dot(c_now, state_low, NN) * grown
        from_end = dot(b_now, dstate_low, NN) * to_end
        dbc_ref[sl, NS:] += dot(dy_grown, state_low, NT)
        dbc_ref[sl, :NS] += dot((w * to_end).astype(bf16), dstate_low, NT)
        dw = jnp.concatenate(dw_parts, axis=1) + from_end
        ended = w * from_end
        cols_ref[0, sl, :] = (
            dcum + split_sum(dw * x, ones_dt) + split_sum(dy * carried - ended, ones_cum)
        )
        dlast_ref[c : c + 1, :] = jnp.sum(ended, axis=0, keepdims=True) + fall * jnp.sum(
            state * dstate, axis=0, keepdims=True
        )
        dstate = fall * dstate + dot(c_now, dy_grown, TN)
        dskip = dskip + jnp.sum(dy * x, axis=0, keepdims=True)
        dx_ref[sl, :] = dw * dt + skip * dy
    dskip_ref[...] = dskip
    unconv(val_ref, tapv_ref[...], dx_ref[...], pad_ref, dval_ref, dtapv_ref, rows)

    @pl.when(step == pl.num_programs(0) - 1)
    def _():
        for c in range(chunks):
            sl = pl.ds(c * CHUNK, CHUNK)
            daff_low = daff_ref[c].astype(bf16)
            dbc_ref[sl, :NS] += dot(daff_low, bc_ref[sl, NS:], NN)
            dbc_ref[sl, NS:] += dot(daff_low, bc_ref[sl, :NS], TN)
        unconv(shr_ref, taps_ref[...], dbc_ref[...], pad_ref, dshr_ref, dtaps_ref, rows)


def settle_kernel(
    low_in_ref, dshr_ref, cols_ref, rows_ref, dlast_ref, step_ref, rate_ref,
    low_ref, ddecay_ref, dbias_ref, dstep_ref,
):
    rows = step_ref.shape[0]
    t = pl.program_id(0)
    lane = lax.broadcasted_iota(jnp.int32, (rows, 128), 1)

    @pl.when(t == 0)
    def _():
        ddt = jnp.zeros((rows, 128), f32)
        dcum = jnp.zeros((rows, 128), f32)
        for i in range(4):
            own = lane // GROUP == i
            cols = cols_ref[i]
            ddt = jnp.where(own, pltpu.roll(cols, GROUP * i, 1) if i else cols, ddt)
            dcum = jnp.where(own, pltpu.roll(cols, (GROUP * i - SLOT) % 128, 1), dcum)
        filled = jnp.concatenate(
            [rows_ref[i] for i in range(4)] + [jnp.zeros((128 - 4 * SLOT, rows), f32)], axis=0
        )
        turned = jnp.transpose(filled)
        for i in range(4):
            moved = pltpu.roll(turned, ((GROUP - SLOT) * i) % 128, 1) if i else turned
            dcum = dcum + jnp.where(lane // GROUP == i, moved, 0.0)
        width = dlast_ref.shape[1]
        head = lax.broadcasted_iota(jnp.int32, (width, 128), 0) // PH
        place = lax.broadcasted_iota(jnp.int32, (width, 128), 1)
        at_end = exact(dlast_ref[...], jnp.where(head == place, 1.0, 0.0), NN)
        lower = lower_ones()
        steps = step_ref[...]
        rate = rate_ref[...]
        decay = -rate * softplus(steps)
        ddecay = jnp.zeros((1, 128), f32)
        dbias = jnp.zeros((1, 128), f32)
        for c in range(rows // CHUNK):
            sl = slice(c * CHUNK, (c + 1) * CHUNK)
            dlog = exact(lower, dcum[sl], TN) + at_end[c : c + 1]
            ddecay = ddecay + jnp.sum(dlog * decay[sl], axis=0, keepdims=True)
            dstep = (ddt[sl] - rate * dlog) * sigmoid(steps[sl])
            dbias = dbias + jnp.sum(dstep, axis=0, keepdims=True)
            dstep_ref[sl, :] = dstep
        ddecay_ref[...] = ddecay
        dbias_ref[...] = dbias

    for i in range(4):

        @pl.when(t == i)
        def _(i=i):
            shared = dshr_ref[:, (i // 2) * 2 * PH : (i // 2 + 1) * 2 * PH]
            if i % 2:
                shared = pltpu.roll(shared, PH, 1)
            steps = pltpu.roll(dstep_ref[...], (PH - GROUP * i) % 128, 1)
            steps = jnp.where((lane >= PH) & (lane < PH + GROUP), steps, 0.0)
            low_ref[pl.ds(0, HALO), :] = jnp.where(lane < PH, 1.0, 0.0)[:HALO].astype(bf16) * (
                shared[:HALO].astype(bf16)
            )
            low_ref[pl.ds(HALO, rows), :] = jnp.where(lane < PH, shared[HALO:], steps).astype(bf16)


def first_back_kernel(
    a_ref, b_ref, late_ref, rows_ref, middle_ref, gain_ref, more_ref, out_ref, gains_ref
):
    rows = a_ref.shape[0]
    out_ref[...] = a_ref[...] + b_ref[pl.ds(HALO, rows), :]
    out_ref[pl.ds(rows - HALO, HALO), :] += late_ref[...]
    grad = out_ref[...]
    values = rows_ref[...].astype(f32)
    inv = lax.rsqrt(jnp.mean(values * values, axis=1, keepdims=True) + epsilon)
    normed = values * inv
    gains_ref[...] = jnp.zeros(gains_ref.shape, f32)
    gains_ref[0:1, :] = jnp.sum(grad * normed, axis=0, keepdims=True)
    gains_ref[1:2, :] = more_ref[...]
    scaled = grad * gain_ref[...]
    cross = jnp.mean(scaled * normed, axis=1, keepdims=True)
    out_ref[...] = middle_ref[...] + inv * (scaled - normed * cross)


def swap_halves(value):
    half = HD // 2
    width = value.shape[1]
    lane = lax.broadcasted_iota(jnp.int32, value.shape, 1) % HD
    return jnp.where(
        lane < half, pltpu.roll(value, width - half, 1), pltpu.roll(value, half, 1)
    )


def rotate_kernel(t0_ref, t1_ref, t2_ref, t3_ref, cos_ref, sin_ref, out_ref):
    rows = cos_ref.shape[0]
    for head, (key, value) in enumerate(((t0_ref, t1_ref), (t2_ref, t3_ref))):
        both = pair_lanes(key[...], pltpu.roll(value[...], HD, 1), rows)
        out = both * cos_ref[...] + swap_halves(both) * sin_ref[...]
        out_ref[:, head * 2 * HD : (head + 1) * 2 * HD] = out.astype(bf16)


def unrotate_kernel(low_in_ref, own_ref, late_ref, cos_ref, sin_ref, out_ref):
    value = own_ref[...] + late_ref[...].astype(f32)
    value = value * cos_ref[...] + swap_halves(value * sin_ref[...])
    odd = lax.rem(pl.program_id(0), 2) == 1
    value = jnp.where(odd, pltpu.roll(value, HD, 1), value)
    lane = lax.broadcasted_iota(jnp.int32, value.shape, 1)
    out_ref[...] = jnp.where(lane < HD, value, 0.0).astype(bf16)


def head_queries(query, which):
    lane = lax.broadcasted_iota(jnp.int32, query.shape, 1)
    moved = pltpu.roll(query, HD, 1) if which else query
    return jnp.where(lane < HD, moved, 0.0)


def score_weights(query, before, own, allowed):
    early = jnp.where(allowed, dot(query, before, NT), masked_fill)
    late = dot(query, own, NT)
    row = lax.broadcasted_iota(jnp.int32, late.shape, 0)
    col = lax.broadcasted_iota(jnp.int32, late.shape, 1)
    late = jnp.where(row >= col, late, masked_fill)
    top = jnp.maximum(
        jnp.max(early, axis=1, keepdims=True), jnp.max(late, axis=1, keepdims=True)
    )
    early = jnp.exp(early - top)
    late = jnp.exp(late - top)
    total = jnp.sum(early, axis=1, keepdims=True) + jnp.sum(late, axis=1, keepdims=True)
    return early, late, 1.0 / total


def rotated_queries(q_ref, cos_ref, sin_ref):
    query = q_ref[...]
    return (query * cos_ref[...] + swap_halves(query) * sin_ref[...]) * (HD**-0.5)


def attend_kernel(part_ref, q_ref, cos_ref, sin_ref, before_ref, own_ref, out_ref):
    allowed = part_ref[0] > 0
    query = rotated_queries(q_ref, cos_ref, sin_ref)
    before = before_ref[...]
    own = own_ref[...]
    results = []
    for which in range(2):
        q_low = head_queries(query, which).astype(bf16)
        early, late, scale = score_weights(q_low, before, own, allowed)
        result = dot(early.astype(bf16), before, NN) + dot(late.astype(bf16), own, NN)
        results.append(result * scale)
    out_ref[...] = pair_lanes(pltpu.roll(results[0], HD, 1), results[1], query.shape[0]).astype(
        bf16
    )


def unattend_kernel(
    part_ref, q_ref, cos_ref, sin_ref, before_ref, own_ref, dout_ref,
    dq_ref, dbefore_ref, down_ref,
):
    allowed = part_ref[0] > 0
    query = rotated_queries(q_ref, cos_ref, sin_ref)
    before = before_ref[...]
    own = own_ref[...]
    dout = dout_ref[...]
    lane = lax.broadcasted_iota(jnp.int32, dout.shape, 1)
    dqs = []
    dbefore = None
    down = None
    for which in range(2):
        q_low = head_queries(query, which).astype(bf16)
        early, late, scale = score_weights(q_low, before, own, allowed)
        early = early * scale
        late = late * scale
        dout_own = dout if which else pltpu.roll(dout, HD, 1)
        dout_low = jnp.where(lane >= HD, dout_own, 0.0).astype(bf16)
        dearly = dot(dout_low, before, NT)
        dlate = dot(dout_low, own, NT)
        cross = jnp.sum(early * dearly, axis=1, keepdims=True) + jnp.sum(
            late * dlate, axis=1, keepdims=True
        )
        dearly = (early * (dearly - cross)).astype(bf16)
        dlate = (late * (dlate - cross)).astype(bf16)
        dqs.append(dot(dearly, before, NN) + dot(dlate, own, NN))
        part_before = dot(dearly, q_low, TN) + dot(early.astype(bf16), dout_low, TN)
        part_own = dot(dlate, q_low, TN) + dot(late.astype(bf16), dout_low, TN)
        dbefore = part_before if dbefore is None else dbefore + part_before
        down = part_own if down is None else down + part_own
    dq = pair_lanes(dqs[0], pltpu.roll(dqs[1], HD, 1), dout.shape[0]) * (HD**-0.5)
    dq_ref[...] = (dq * cos_ref[...] + swap_halves(dq * sin_ref[...])).astype(bf16)
    first = lax.rem(pl.program_id(0), AH // KVH // 2) == 0

    @pl.when(first)
    def _():
        dbefore_ref[...] = dbefore
        down_ref[...] = down

    @pl.when(jnp.logical_not(first))
    def _():
        dbefore_ref[...] += dbefore
        down_ref[...] += down


def times(rows_in, blocks, outs, finish, extras=(), specs=(), out_specs=None, deps=()):
    rows, depth = rows_in.shape
    groups, _, width = blocks[0].shape
    tile = width
    count = len(blocks)
    tile_spec = spec((rows, tile), lambda i: (0, i))

    def kernel(rows_ref, *refs):
        weight = jnp.concatenate([ref[0] for ref in refs[:count]], axis=0)
        finish(dot(rows_ref[...], weight, NN), *refs[count:])

    return call(
        kernel,
        (groups,),
        [spec((rows, depth), lambda i: (0, 0))]
        + [spec((1, b.shape[1], tile), lambda i: (i, 0, 0)) for b in blocks]
        + list(specs),
        out_specs or [tile_spec] * len(outs),
        outs,
        flops=2 * rows * depth * width * groups,
        moved=depth * width * groups * 2 + rows * width * groups * 4,
        deps=deps,
    )(rows_in, *blocks, *extras)


def times_transposed(lefts, blocks, outs, finish, extras=(), deps=()):
    rows = lefts[0].shape[0]
    groups, _, width = blocks[0].shape
    count = len(blocks)
    depth = sum(b.shape[1] for b in blocks)
    whole = lambda item: spec(item.shape, lambda i: (0, 0))

    def kernel(*refs):
        left = [ref[...] for ref in refs[: len(lefts)]]
        left = jnp.concatenate(left, axis=1) if len(left) > 1 else left[0]
        refs = refs[len(lefts) :]
        weight = jnp.concatenate([ref[0] for ref in refs[:count]], axis=0)
        part = dot(left, weight, NT)
        total = refs[-1]
        step = pl.program_id(0)

        @pl.when(step == 0)
        def _():
            total[...] = part

        @pl.when(step > 0)
        def _():
            total[...] += part

        @pl.when(step == pl.num_programs(0) - 1)
        def _():
            finish(total[...], *refs[count:-1])

    return call(
        kernel,
        (groups,),
        [spec((rows, item.shape[1] // groups), lambda i: (0, i)) for item in lefts]
        + [spec((1, b.shape[1], width), lambda i: (i, 0, 0)) for b in blocks]
        + [whole(e) for e in extras],
        [whole(o) for o in outs],
        outs,
        [pltpu.VMEM((rows, depth), f32)],
        flops=2 * rows * depth * width * groups,
        moved=depth * width * groups * 2 + rows * depth * 8,
        deps=deps,
    )(*lefts, *blocks, *extras)


def store(value, out_ref):
    out_ref[...] = value.astype(out_ref.dtype)


def add_store(value, other_ref, out_ref):
    out_ref[...] = value + other_ref[...]


def middle_finish(value, rows_ref, gain_ref, middle_ref, low_ref):
    middle = rows_ref[...] + value
    middle_ref[...] = middle
    inv = lax.rsqrt(jnp.mean(middle * middle, axis=1, keepdims=True) + epsilon)
    low_ref[...] = (middle * inv * gain_ref[...]).astype(bf16)


def unit_finish(value, hidden_ref, by_gate_ref, by_up_ref):
    half = value.shape[1] // 2
    gate = value[:, :half]
    up = value[:, half:]
    sig = sigmoid(gate)
    silu = gate * sig
    hidden_ref[...] = (silu * up).astype(bf16)
    by_gate_ref[...] = (up * sig * (1.0 + gate * (1.0 - sig))).astype(bf16)
    by_up_ref[...] = silu.astype(bf16)


def unit_back_finish(value, by_gate_ref, by_up_ref, out_ref):
    half = value.shape[1]
    out_ref[:, :half] = (value * by_gate_ref[...].astype(f32)).astype(bf16)
    out_ref[:, half:] = (value * by_up_ref[...].astype(f32)).astype(bf16)


def middle_back_finish(value, middle_ref, cot_ref, gain_ref, grad_ref, low_ref, dgain_ref):
    middle = middle_ref[...]
    inv = lax.rsqrt(jnp.mean(middle * middle, axis=1, keepdims=True) + epsilon)
    normed = middle * inv
    dgain_ref[...] = jnp.sum(value * normed, axis=0, keepdims=True)
    scaled = value * gain_ref[...]
    cross = jnp.mean(scaled * normed, axis=1, keepdims=True)
    grad = cot_ref[...].astype(f32) + inv * (scaled - normed * cross)
    grad_ref[...] = grad
    low_ref[...] = grad.astype(bf16)


def partner(value, bit):
    count = lax.axis_size("dp")
    return lax.ppermute(value, "dp", [(i, i ^ (1 << bit)) for i in range(count)])


def high_bits():
    return list(range(1, lax.axis_size("dp").bit_length() - 1))


def put_rows(out_ref, parts):
    if parts[0].shape[0] % 16:
        parts = [jnp.concatenate([p.astype(f32) for p in parts], axis=0).astype(bf16)]
    at = 0
    for p in parts:
        out_ref[0, at : at + p.shape[0], :] = p
        at += p.shape[0]


def cut_pieces(gathered, ranges, deps=()):
    groups, rows, width = gathered.shape
    half = rows // 2

    def kernel(in_ref, *out_refs):
        for i, (start, stop) in enumerate(ranges):
            part = in_ref[0, :, start:stop]
            if half % 16:
                part = part.astype(f32)
            out_refs[2 * i][0] = part[:half].astype(bf16)
            out_refs[2 * i + 1][0] = part[half:].astype(bf16)

    sizes = [stop - start for start, stop in ranges for _ in range(2)]
    outs = call(
        kernel,
        (groups,),
        [spec((1, rows, width), lambda t: (t, 0, 0))],
        [spec((1, half, w), lambda t: (t, 0, 0)) for w in sizes],
        [shape((groups, half, w), bf16) for w in sizes],
        moved=groups * rows * width * 4,
        deps=deps,
    )(gathered)
    return [(outs[2 * i], outs[2 * i + 1]) for i in range(len(ranges))]


def cut_exchanged(own, deps=()):
    count = lax.axis_size("tensor")
    pieces = [own]
    for far in range(1, count):
        pieces.append(lax.ppermute(own, "tensor", [(i, i ^ far) for i in range(count)]))
    rows, width = own.shape
    half = rows // 2

    def kernel(me_ref, *refs):
        upper_ref, lower_ref = refs[-2:]
        source = jnp.bitwise_xor(pl.program_id(0), me_ref[0])
        for i in range(count):

            @pl.when(source == i)
            def _(i=i):
                part = refs[i][...]
                if half % 16:
                    part = part.astype(f32)
                upper_ref[0] = part[:half].astype(bf16)
                lower_ref[0] = part[half:].astype(bf16)

    return call(
        kernel,
        (count,),
        [pl.BlockSpec(memory_space=pltpu.SMEM)] + [spec((rows, width), lambda t: (0, 0))] * count,
        [spec((1, half, width), lambda t: (t, 0, 0))] * 2,
        [shape((count, half, width), bf16)] * 2,
        moved=count * rows * width * 4,
        deps=deps,
    )(lax.axis_index("tensor").astype(jnp.int32).reshape(1), *pieces)


def spread_send(held, step):
    bits = high_bits()
    return partner(held[0], bits[step]), partner(held[1], bits[-1 - step])


def join_all(items, deps=()):
    groups = items[0][0][0].shape[0]
    args, in_specs, out_specs, outs, moved = [], [], [], [], 0
    for held, got, last in items:
        _, rows, width = held[0].shape
        args += [held[0], got[0], held[1], got[1]]
        in_specs += [spec((1, rows, width), lambda t: (t, 0, 0))] * 4
        size = 4 if last else 2
        number = 1 if last else 2
        out_specs += [spec((1, size * rows, width), lambda t: (t, 0, 0))] * number
        outs += [shape((groups, size * rows, width), bf16)] * number
        moved += groups * rows * width * 16

    def kernel(*refs):
        out_refs = list(refs[len(args) :])
        for i, (_, _, last) in enumerate(items):
            a_ref, b_ref, c_ref, d_ref = refs[4 * i : 4 * i + 4]
            upper = [a_ref[0], b_ref[0]]
            lower = [c_ref[0], d_ref[0]]
            if last:
                put_rows(out_refs.pop(0), upper + lower)
            else:
                put_rows(out_refs.pop(0), upper)
                put_rows(out_refs.pop(0), lower)

    out = list(
        call(kernel, (groups,), in_specs, out_specs, outs, moved=moved, deps=deps)(*args)
    )
    return [[out.pop(0)] if last else [out.pop(0), out.pop(0)] for _, _, last in items]


def join(held, got, deps=(), last=False):
    return join_all([(held, got, last)], deps)[0]


def spread_rest(held, got, first, deps=()):
    steps = len(high_bits())
    for i in range(first, steps):
        held = join(held, got, deps, i + 1 == steps)
        if i + 1 < steps:
            got = spread_send(held, i + 1)
    return held


def spread_end(held):
    return held[0], partner(held[0], 0)


def route_bits(route):
    return high_bits()[::-1] if route else high_bits()


def send_one(held, route, step):
    return partner(held, route_bits(route)[step])


def join_one(held, got, route, step, deps=()):
    groups, rows, width = held.shape
    bits = route_bits(route)
    masks = [(0, 0), (0, 1)]
    for bit in bits[: step + 1]:
        masks = masks + [(m | (1 << bit), p) for m, p in masks]
    places = list(range(len(masks)))
    if step + 1 == len(bits):
        goal = block_masks()[: len(masks)]
        places = [masks.index(m) for m in goal]
    size = 2 * rows // len(masks)

    def kernel(a_ref, b_ref, out_ref):
        if step + 1 < len(bits):
            put_rows(out_ref, [a_ref[0], b_ref[0]])
            return
        parts = []
        for place in places:
            ref, at = (a_ref, place * size) if place * size < rows else (b_ref, place * size - rows)
            parts.append(ref[0, at : at + size, :])
        put_rows(out_ref, parts)

    one = spec((1, rows, width), lambda t: (t, 0, 0))
    return call(
        kernel,
        (groups,),
        [one] * 2,
        spec((1, 2 * rows, width), lambda t: (t, 0, 0)),
        shape((groups, 2 * rows, width), bf16),
        moved=groups * rows * width * 8,
        deps=deps,
    )(held, got)


def rest_one(held, got, route, first, deps=()):
    steps = len(high_bits())
    for i in range(first, steps):
        held = join_one(held, got, route, i, deps)
        if i + 1 < steps:
            got = send_one(held, route, i + 1)
    return held


def slice_one(gathered, start, stop, deps=()):
    groups, rows, width = gathered.shape

    def kernel(in_ref, out_ref):
        out_ref[0] = in_ref[0, :, start:stop]

    return call(
        kernel,
        (groups,),
        [spec((1, rows, width), lambda t: (t, 0, 0))],
        spec((1, rows, stop - start), lambda t: (t, 0, 0)),
        shape((groups, rows, stop - start), bf16),
        moved=groups * rows * width * 4,
        deps=deps,
    )(gathered)


def tile_of(width):
    return next(t for t in (1024, 768, 512, 256, 128) if width % t == 0)


def collect_send(left, right, deps=()):
    rows, depth = left.shape
    near = depth // 2
    width = right.shape[1]
    tile = tile_of(width)

    def kernel(left_ref, right_ref, out_ref):
        out_ref[...] = dot(left_ref[...], right_ref[...], TN).astype(bf16)

    send = call(
        kernel,
        (width // tile,),
        [spec((rows, near), lambda i: (0, 1)), spec((rows, tile), lambda i: (0, i))],
        spec((near, tile), lambda i: (0, i)),
        shape((near, width), bf16),
        flops=2 * rows * near * width,
        moved=(rows + near) * width * 2,
        deps=deps,
    )(left, right)
    return send, partner(send, 0)


def collect_keep(left, right, got, deps=(), route=None):
    rows, depth = left.shape
    near = depth // 2
    quarter = near // 4
    if route is not None:
        masks, bit = route_masks(route, 0)
        lists = split_masks(masks, bit)
    else:
        lists = [[2 * i, 2 * i + 1] for i in range(4)]
    size = near // sum(len(x) for x in lists) if route is not None else quarter // 2
    width = right.shape[1]
    tile = tile_of(width)

    def kernel(left_ref, right_ref, got_ref, *out_refs):
        total = dot(left_ref[...], right_ref[...], TN) + got_ref[...].astype(f32)
        for places, out_ref in zip(lists, out_refs):
            out_ref[...] = pick_rows(total, places, size).astype(bf16)

    high = near // len(lists)
    out = spec((high, tile), lambda i: (0, i))
    return call(
        kernel,
        (width // tile,),
        [
            spec((rows, near), lambda i: (0, 0)),
            spec((rows, tile), lambda i: (0, i)),
            spec((near, tile), lambda i: (0, i)),
        ],
        [out] * len(lists),
        [shape((high, width), bf16)] * len(lists),
        flops=2 * rows * near * width,
        moved=(rows + 2 * near) * width * 2,
        deps=deps,
    )(left, right, got)


def pick_rows(value, places, size):
    parts, at = [], 0
    while at < len(places):
        end = at + 1
        while end < len(places) and places[end] == places[end - 1] + 1:
            end += 1
        parts.append(value[places[at] * size : (places[end - 1] + 1) * size])
        at = end
    return jnp.concatenate(parts, axis=0) if len(parts) > 1 else parts[0]


def route_masks(route, step):
    bits = route_bits(route)[::-1]
    masks = block_masks()[: 2 << len(bits)]
    for bit in bits[:step]:
        masks = [m for m in masks if not m[0] >> bit & 1]
    return masks, bits[step] if step < len(bits) else None


def split_masks(masks, bit):
    return [
        [i for i, m in enumerate(masks) if (m[0] >> bit & 1) == side] for side in range(2)
    ]


def move_one(parts, route, step):
    return partner(parts[1], route_bits(route)[::-1][step])


def add_one(parts, got, route, step, deps=()):
    rows, width = parts[0].shape
    half = rows // 2
    tile = tile_of(width)
    masks, bit = route_masks(route, step + 1)
    lists = split_masks(masks, bit)
    size = rows // len(masks)

    def kernel(a_ref, b_ref, *out_refs):
        total = a_ref[...].astype(f32) + b_ref[...].astype(f32)
        for places, out_ref in zip(lists, out_refs):
            out_ref[...] = pick_rows(total, places, size).astype(bf16)

    block = spec((rows, tile), lambda i: (0, i))
    return call(
        kernel,
        (width // tile,),
        [block] * 2,
        [spec((half, tile), lambda i: (0, i))] * 2,
        [shape((half, width), bf16)] * 2,
        moved=rows * width * 6,
        deps=deps,
    )(parts[0], got)


def collect_move(parts, step):
    bits = high_bits()
    return partner(parts[1], bits[-1 - step]), partner(parts[3], bits[step])


def collect_add(parts, got, deps=()):
    rows, width = parts[0].shape
    half = rows // 2
    tile = tile_of(width)

    def kernel(a_ref, b_ref, c_ref, d_ref, *out_refs):
        for i, (own, other) in enumerate(((a_ref, b_ref), (c_ref, d_ref))):
            total = own[...].astype(f32) + other[...].astype(f32)
            out_refs[2 * i][...] = total[:half].astype(bf16)
            out_refs[2 * i + 1][...] = total[half:].astype(bf16)

    block = spec((rows, tile), lambda i: (0, i))
    return call(
        kernel,
        (width // tile,),
        [block] * 4,
        [spec((half, tile), lambda i: (0, i))] * 4,
        [shape((half, width), bf16)] * 4,
        moved=rows * width * 12,
        deps=deps,
    )(parts[0], got[0], parts[2], got[1])


def collect_end(pairs, deps=()):
    groups = lax.axis_size("tensor")
    args, in_specs, widths, counts = [], [], [], []
    for parts, got in pairs:
        width = parts[0].shape[1] // groups
        widths.append(width)
        both = len(parts) == 4
        add = [parts[0], got[0], parts[2], got[1]] if both else [parts[0], got]
        counts.append(len(add))
        args += add
        in_specs += [spec((parts[0].shape[0], width), lambda t: (0, t))] * len(add)
        rows = parts[0].shape[0] // (1 if both else 2)

    def kernel(*refs):
        at = first = 0
        for width, count in zip(widths, counts):
            values = [ref[...].astype(f32) for ref in refs[first : first + count]]
            sums = [values[i] + values[i + 1] for i in range(0, count, 2)]
            out = jnp.concatenate(sums, axis=0) if len(sums) > 1 else sums[0]
            refs[-1][0, :, at : at + width] = out.astype(bf16)
            at += width
            first += count

    total = sum(widths)
    return call(
        kernel,
        (groups,),
        in_specs,
        spec((1, 2 * rows, total), lambda t: (t, 0, 0)),
        shape((groups, 2 * rows, total), bf16),
        moved=groups * rows * total * 12,
        deps=deps,
    )(*args)


def block_masks():
    bits = high_bits()
    count = 1 << len(bits)
    masks = []
    for core in range(2):
        for part in range(2):
            for j in range(count):
                order = bits[::-1] if part else bits
                mask = sum(((j >> i) & 1) << bit for i, bit in enumerate(order))
                masks.append((mask | core, part))
    return masks


def take_blocks(value, sources):
    width = value.shape[-1] // len(sources)
    axis = value.ndim - 1
    return jnp.concatenate(
        [lax.dynamic_slice_in_dim(value, s * width, width, axis) for s in sources], axis=axis
    )


def permute_features(value):
    me = lax.axis_index("dp")
    return take_blocks(value, [(me ^ mask) * 2 + part for mask, part in block_masks()])


def restore_features(value):
    me = lax.axis_index("dp")
    masks = block_masks()
    count = lax.axis_size("dp")
    table = jnp.array(
        [[masks.index((m, part)) for part in range(2)] for m in range(count)], jnp.int32
    )
    return take_blocks(
        value, [table[me ^ block, part] for block in range(count) for part in range(2)]
    )


def restore_all(values, deps=()):
    count = lax.axis_size("dp")
    if values[0].shape[1] // count != 128:
        return [restore_features(v) for v in values]
    masks = block_masks()
    places = [[masks.index((m, part)) for part in range(2)] for m in range(count)]
    rows = jnp.array([[p[0] // 2, p[0] % 2, p[1] // 2, p[1] % 2] for p in places], jnp.int32)
    table = rows[lax.axis_index("dp") ^ jnp.arange(count, dtype=jnp.int32)].reshape(-1)
    late = jax.tree.leaves(deps)
    number = len(values)

    def kernel(table_ref, *refs):
        i = pl.program_id(0)
        out_refs = refs[2 * number + len(late) :]
        for n in range(number):
            front, back = refs[2 * n][...], refs[2 * n + 1][...]
            front = jnp.where(table_ref[4 * i + 1] > 0, pltpu.roll(front, 64, 1), front)
            back = jnp.where(table_ref[4 * i + 3] > 0, back, pltpu.roll(back, 64, 1))
            lane = lax.broadcasted_iota(jnp.int32, front.shape, 1)
            out_refs[n][...] = jnp.where(lane < 64, front, back)

    in_specs = []
    for v in values:
        for at in (0, 2):
            in_specs.append(spec((v.shape[0], 128), lambda i, t, at=at: (0, t[4 * i + at])))
    in_specs += [pl.BlockSpec(memory_space=pl.ANY)] * len(late)
    return pl.pallas_call(
        kernel,
        grid_spec=pltpu.PrefetchScalarGridSpec(
            num_scalar_prefetch=1,
            grid=(count,),
            in_specs=in_specs,
            out_specs=[spec((v.shape[0], 128), lambda i, t: (0, i)) for v in values],
        ),
        out_shape=[shape(v.shape, v.dtype) for v in values],
        compiler_params=pltpu.CompilerParams(vmem_limit_bytes=VMEM_BYTES),
        cost_estimate=pl.CostEstimate(flops=1, bytes_accessed=1, transcendentals=0),
    )(table, *[v for v in values for _ in range(2)], *late)


def sum_all(value):
    for axis in ("dp", "tensor"):
        count = lax.axis_size(axis)
        for bit in range(count.bit_length() - 1):
            value = value + lax.ppermute(value, axis, [(i, i ^ (1 << bit)) for i in range(count)])
    return value


def norm_of(rows):
    inv = lax.rsqrt(jnp.mean(rows * rows, axis=-1, keepdims=True) + epsilon)
    return rows * inv, inv


def norm_back(grad, gain, normed, inv):
    scaled = grad * gain
    return inv * (scaled - normed * jnp.mean(scaled * normed, axis=-1, keepdims=True))


def over_tensor(piece):
    return lax.all_gather(piece, "tensor", axis=0)


def shards(
    residual,
    mixer_in,
    step_in,
    shared_in,
    query_in,
    keyval_in,
    mixer_proj,
    attn_proj,
    gate_up,
    down_proj,
    norm_gain,
    mlp_gain,
    conv_filter,
    decay_log,
    skip_gain,
    step_bias,
    gated_gain,
    cotangent,
):
    tensor_count = lax.axis_size("tensor")
    rows, model = residual.shape
    depth = mixer_in.shape[0]
    ssm = conv_filter.shape[1] - 2 * NS
    heads = ssm // PH
    groups = heads // GROUP
    chunks = rows // CHUNK
    span = LEN // rows
    part = lax.axis_index("tensor") % span
    onward = [(i, i + 1) for i in range(tensor_count) if i % span != span - 1]
    backward = [(j, i) for i, j in onward]
    hidden_w = gate_up.shape[2]
    gate_w = mixer_in.shape[2]
    query_w = query_in.shape[1]
    shared_w = shared_in.shape[1]
    attn_w = AH * HD
    ff = hidden_w * tensor_count
    steps = len(high_bits())

    def finish_dp(parts, got, deps):
        for i in range(2, steps):
            parts = collect_add(parts, got, deps)
            got = collect_move(parts, i)
        return collect_end([(parts, got)], deps)

    def finish_tensor(joined):
        total = lax.psum_scatter(joined, "tensor", scatter_dimension=0, tiled=False)
        return total.astype(f32)

    before_rows = lax.ppermute(residual[rows - HALO :], "tensor", onward)
    ext_low = permute_features(jnp.concatenate([before_rows, residual], axis=0))
    cot = permute_features(cotangent)
    gain_first = permute_features(norm_gain)
    gain_second = permute_features(mlp_gain)
    ext_normed, ext_inv = norm_of(ext_low.astype(f32))
    ext_in = (ext_normed * gain_first).astype(bf16)
    normed_first = ext_normed[HALO:]
    inv_first = ext_inv[HALO:]
    normed_in = ext_in[HALO:]
    group_rows = ext_low[HALO:].astype(f32)
    wide_f32 = shape((rows, model), f32)
    wide_low = shape((rows, model), bf16)
    second_row = gain_second[None, :]

    half = HD // 2
    frequency = rope_base ** (-2.0 * jnp.arange(half, dtype=f32) / HD)
    place = (part * rows + jnp.arange(rows, dtype=jnp.int32)).astype(f32)
    angles = place[:, None] * frequency[None, :]
    cosine = jnp.cos(angles)
    sine = jnp.sin(angles)
    ones = jnp.ones((rows, HD), f32)
    cos_q = jnp.concatenate([cosine] * 4, axis=1)
    sin_q = jnp.concatenate([-sine, sine] * 2, axis=1)
    cos_kv = jnp.concatenate([cosine, cosine, ones], axis=1)
    sin_kv = jnp.concatenate([-sine, sine, 0.0 * ones], axis=1)

    def padded(parts):
        width = sum(p.shape[1] for p in parts)
        return jnp.concatenate(parts + [jnp.zeros((depth, -width % 128), bf16)], axis=1)

    val_in = padded([mixer_in[:, 1], shared_in, step_in])
    gate_in = padded([mixer_in[:, 0], query_in, keyval_in])
    val_w = val_in.shape[1]
    out_in = jnp.concatenate([mixer_proj, attn_proj], axis=0).T
    out_w = out_in.shape[1]
    back_in = jnp.concatenate([out_in, down_proj.T], axis=1)
    gate_in_w = gate_in.shape[1]
    rest_z = over_tensor(
        jnp.concatenate([gate_in, gate_up.reshape(depth, 2 * hidden_w), back_in], axis=1)
    )
    ff_at = gate_in_w
    out_at = ff_at + 2 * hidden_w
    down_at = out_at + out_w
    tables = (cos_q, sin_q, cos_kv, sin_kv)
    val_held = cut_exchanged(val_in, (ext_in, tables, cot, group_rows))
    val_held = spread_rest(val_held, spread_send(val_held, 0), 0)
    in_b = spread_end(val_held)

    (proj_b,) = times(
        ext_in,
        in_b,
        [shape((rows + HALO, val_w * tensor_count), f32)],
        store,
    )

    ext = rows + HALO
    whole = lambda *dims: spec(dims, lambda i: (0,) * len(dims))
    tail = lambda count, t: (lambda i: (0, count * t + count - 1))
    per_val = val_w // 128
    bias_row = jnp.pad(step_bias, (0, 128 - heads))[None, :]
    rate_row = jnp.pad(jnp.exp(decay_log), (0, 128 - heads))[None, :]
    shr, step_lin, cols, cum_rows, grow = call(
        prepare_kernel,
        (1,),
        [spec((ext, 128), tail(per_val, t)) for t in range(4)] + [whole(1, 128)] * 2,
        [
            whole(ext, 2 * NS),
            whole(rows, 128),
            whole(groups, rows, 2 * SLOT),
            whole(groups, SLOT, rows),
            whole(rows, 128),
        ],
        [
            shape((ext, 2 * NS), f32),
            shape((rows, 128), f32),
            shape((groups, rows, 2 * SLOT), f32),
            shape((groups, SLOT, rows), f32),
            shape((rows, 128), f32),
        ],
        moved=rows * 128 * 40,
    )(proj_b, proj_b, proj_b, proj_b, bias_row, rate_row)
    skip_lanes = jnp.repeat(skip_gain, PH)[None, :]
    (gate_held,) = cut_pieces(rest_z, [(0, gate_in_w)], cols)
    gate_held = join(gate_held, spread_send(gate_held, 0))
    gate_got = spread_send(gate_held, 1)
    (out_held,) = cut_pieces(rest_z, [(out_at, down_at)], gate_held)
    out_got = spread_send(out_held, 0)

    val_spec = spec((ext, val_w), lambda g: (0, g))
    shr_spec = whole(ext, 2 * NS)
    tapv_spec = spec((KC, GW), lambda g: (0, g))
    taps_spec = spec((KC, 2 * NS), lambda g: (0, ssm // (2 * NS)))
    col_spec = spec((1, rows, 2 * SLOT), lambda g: (g, 0, 0))
    row_spec = spec((1, SLOT, rows), lambda g: (g, 0, 0))
    lane_spec = spec((1, GW), lambda g: (0, g))
    bc_spec = whole(rows, 2 * NS)
    grp_spec = spec((rows, GW), lambda g: (0, g))
    state_spec = spec((NS, GW), lambda g: (0, g))
    y_local, state_local, bc_act = call(
        mixer_kernel,
        (groups,),
        [val_spec, shr_spec, tapv_spec, taps_spec, col_spec, row_spec, lane_spec],
        [grp_spec, state_spec, bc_spec],
        [shape((rows, ssm), f32), shape((NS, ssm), bf16), shape((rows, 2 * NS), bf16)],
        [pltpu.VMEM((chunks, CHUNK, CHUNK), f32)],
        flops=2 * rows * ssm * 512,
        moved=rows * ssm * 8,
        deps=(gate_held, out_held),
    )(proj_b, shr, conv_filter, conv_filter, cols, cum_rows, skip_lanes)
    entering = lax.ppermute(state_local, "tensor", onward)
    per_gate = gate_held[0].shape[2] // 128
    for i in range(1, steps - 1):
        gate_held = join(gate_held, gate_got, y_local)
        gate_got = spread_send(gate_held, i + 1)
    gate_held, out_held = join_all(
        [(gate_held, gate_got, True), (out_held, out_got, False)], y_local
    )
    in_a = spread_end(gate_held)
    out_got = spread_send(out_held, 1)
    (ff_held,) = cut_pieces(rest_z, [(ff_at, out_at)], gate_held)
    ff_got = spread_send(ff_held, 0)
    (proj_a,) = times(
        normed_in,
        in_a,
        [shape((rows, per_gate * 128 * tensor_count), f32)],
        store,
        deps=ff_held,
    )
    for i in range(1, steps - 1):
        out_held = join(out_held, out_got, proj_a)
        out_got = spread_send(out_held, i + 1)
    out_held, ff_held = join_all(
        [(out_held, out_got, True), (ff_held, ff_got, False)], (proj_a, entering)
    )
    out_full = spread_end(out_held)
    ff_got = spread_send(ff_held, 1)

    kv_w = 2 * KVH * HD
    own_kv = call(
        rotate_kernel,
        (1,),
        [spec((rows, 128), tail(per_gate, t)) for t in range(4)] + [whole(rows, 2 * HD)] * 2,
        whole(rows, kv_w),
        shape((rows, kv_w), bf16),
        moved=rows * kv_w * 12,
    )(proj_a, proj_a, proj_a, proj_a, cos_kv, sin_kv)
    before_kv = lax.ppermute(own_kv, "tensor", onward)
    part_arg = part.astype(jnp.int32).reshape(1)
    pairs = AH // 2
    per_kv = AH // KVH // 2
    smem = pl.BlockSpec(memory_space=pltpu.SMEM)
    q_spec = spec((rows, 2 * HD), lambda i: (0, per_gate * i + GW // 128))
    table_spec = spec((rows, 2 * HD), lambda i: (0, 0))
    kv_spec = spec((rows, 2 * HD), lambda i: (0, i // per_kv))
    pair_spec = spec((rows, 2 * HD), lambda i: (0, i))
    attn_heads = call(
        attend_kernel,
        (pairs,),
        [smem, q_spec, table_spec, table_spec, kv_spec, kv_spec],
        pair_spec,
        shape((rows, attn_w), bf16),
        flops=2 * AH * rows * LEN * 256,
        moved=rows * attn_w * 8,
        deps=ff_held,
    )(part_arg, proj_a, cos_q, sin_q, before_kv, own_kv)

    (down_held,) = cut_pieces(rest_z, [(down_at, rest_z.shape[2])], (attn_heads, out_full))
    down_got = spread_send(down_held, 0)
    block_rows = CHUNK
    wide = spec((block_rows, ssm), lambda i: (i, 0))
    gate_block = spec((block_rows, proj_a.shape[1]), lambda i: (i, 0))
    heads_block = spec((block_rows, ssm + attn_w), lambda i: (i, 0))
    attn_block = spec((block_rows, attn_w), lambda i: (i, 0))
    bc_block = spec((block_rows, 2 * NS), lambda i: (i, 0))
    grow_block = spec((block_rows, 128), lambda i: (i, 0))
    state_whole = whole(NS, ssm)
    gain_whole = whole(1, ssm)
    gated_row = gated_gain[None, :]
    scanned, heads_all = call(
        finish_kernel,
        (rows // block_rows,),
        [wide, gate_block, bc_block, grow_block, state_whole, gain_whole, attn_block],
        [wide, heads_block],
        [shape((rows, ssm), f32), shape((rows, ssm + attn_w), bf16)],
        flops=2 * rows * ssm * NS,
        moved=rows * ssm * 14,
        deps=down_held,
    )(y_local, proj_a, bc_act, grow, entering, gated_row, attn_heads)

    ff_held = spread_rest(ff_held, ff_got, 1, heads_all)
    ff_full = spread_end(ff_held)
    middle, mlp_rows = times_transposed(
        [heads_all],
        out_full,
        [wide_f32, wide_low],
        middle_finish,
        (group_rows, second_row),
        deps=ff_held,
    )
    down_held = join(down_held, down_got, middle)
    down_got = spread_send(down_held, 1)
    unit = spec((rows, hidden_w), lambda i: (0, i))
    ff_low = shape((rows, ff), bf16)
    hidden, by_gate, by_up = times(
        mlp_rows, ff_full, [ff_low] * 3, unit_finish, out_specs=[unit] * 3, deps=down_held
    )
    down_held = spread_rest(down_held, down_got, 1, hidden)
    down_full = spread_end(down_held)
    down_send, down_got = collect_send(cot, hidden, down_held)
    (both_grad,) = times(
        cot,
        down_full,
        [shape((rows, 2 * ff), bf16)],
        unit_back_finish,
        (by_gate, by_up),
        (unit, unit),
        [spec((rows, 2 * hidden_w), lambda i: (0, i))],
        deps=down_send,
    )
    down_sum = collect_keep(cot, hidden, down_got, both_grad)
    down_got = collect_move(down_sum, 0)
    ff_send, ff_got = collect_send(mlp_rows, both_grad, down_sum)
    middle_grad, branch_grad, mlp_gain_part = times_transposed(
        [both_grad],
        ff_full,
        [wide_f32, wide_low, shape((1, model), f32)],
        middle_back_finish,
        (middle, cot, second_row),
        deps=(ff_send, down_sum),
    )

    down_sum = collect_add(down_sum, down_got, branch_grad)
    down_got = collect_move(down_sum, 1)
    (heads_grad,) = times(
        branch_grad, out_full, [shape((rows, ssm + attn_w), f32)], store, deps=down_sum
    )
    out_send, out_got = collect_send(branch_grad, heads_all, heads_grad)
    ff_sum = collect_keep(mlp_rows, both_grad, ff_got, out_send)
    ff_got = collect_move(ff_sum, 0)
    dgate, dscan, gated_gain_part, dstate_local = call(
        ungate_kernel,
        (rows // block_rows,),
        [heads_block, wide, gate_block, bc_block, grow_block, gain_whole],
        [wide, wide, gain_whole, state_whole],
        [
            shape((rows, ssm), bf16),
            shape((rows, ssm), f32),
            shape((1, ssm), f32),
            shape((NS, ssm), f32),
        ],
        flops=2 * rows * ssm * NS,
        moved=rows * ssm * 18,
        deps=(out_send, ff_sum),
    )(heads_grad, scanned, proj_a, bc_act, grow, gated_row)
    leaving_grad = lax.ppermute(dstate_local.astype(bf16), "tensor", backward)
    down_z = finish_dp(down_sum, down_got, dgate)
    down_t = finish_tensor(down_z)
    gate_send, gate_got = collect_send(normed_in, dgate, down_z)
    out_sum = collect_keep(branch_grad, heads_all, out_got, gate_send, 0)
    out_got = move_one(out_sum, 0, 0)
    (output,) = times_transposed(
        [hidden], down_full, [wide_f32], add_store, (middle,), deps=out_sum
    )
    gate_sum = collect_keep(normed_in, dgate, gate_got, (output, leaving_grad), 1)
    gate_got = move_one(gate_sum, 1, 0)
    (output,) = restore_all([output], gate_sum)

    dout_spec = spec((rows, 2 * HD), lambda i: (0, 4 * i + 3))
    qk_low, before_grad, own_grad = call(
        unattend_kernel,
        (pairs,),
        [smem, q_spec, table_spec, table_spec, kv_spec, kv_spec, dout_spec],
        [spec((rows, 2 * HD), lambda i: (0, 2 * i)), kv_spec, kv_spec],
        [shape((rows, 4 * HD * pairs), bf16), shape((rows, kv_w), f32), shape((rows, kv_w), f32)],
        flops=2 * AH * rows * LEN * 640,
        moved=rows * attn_w * 16,
        deps=(out_sum, gate_sum, output),
    )(part_arg, proj_a, cos_q, sin_q, before_kv, own_kv, heads_grad)
    late_grad = lax.ppermute(before_grad.astype(bf16), "tensor", backward)

    ff_sum = collect_add(ff_sum, ff_got, before_grad)
    ff_got = collect_move(ff_sum, 1)
    out_sum = add_one(out_sum, out_got, 0, 0, ff_sum)
    out_got = move_one(out_sum, 0, 1)
    gate_sum = add_one(gate_sum, gate_got, 1, 0, out_sum)
    gate_got = move_one(gate_sum, 1, 1)
    half_spec = spec((rows, 2 * HD), lambda t: (0, t // 2))
    qk_low = call(
        unrotate_kernel,
        (tensor_count,),
        [pl.BlockSpec(memory_space=pl.ANY), half_spec, half_spec] + [whole(rows, 2 * HD)] * 2,
        spec((rows, 2 * HD), lambda t: (0, 2 * t + 1)),
        shape(qk_low.shape, bf16),
        moved=rows * kv_w * 16,
        aliases={0: 0},
        deps=(ff_sum, out_sum, gate_sum),
    )(qk_low, own_grad, late_grad, cos_kv, sin_kv)

    qk_send, qk_got = collect_send(normed_in, qk_low)

    low_v, dshr, dcols, drows, dlast, dtapv, dtaps, dskip = call(
        unmix_kernel,
        (groups,),
        [
            val_spec, shr_spec, tapv_spec, taps_spec, col_spec, row_spec, lane_spec,
            bc_spec, grp_spec, state_spec, state_spec,
        ],
        [
            val_spec,
            shr_spec,
            spec((1, rows, 128), lambda g: (g, 0, 0)),
            row_spec,
            spec((chunks, GW), lambda g: (0, g)),
            tapv_spec,
            whole(KC, 2 * NS),
            lane_spec,
        ],
        [
            shape((ext, val_w * tensor_count), bf16),
            shape((ext, 2 * NS), f32),
            shape((groups, rows, 128), f32),
            shape((groups, SLOT, rows), f32),
            shape((chunks, ssm), f32),
            shape((KC, ssm), f32),
            shape((KC, 2 * NS), f32),
            shape((1, ssm), f32),
        ],
        [
            pltpu.VMEM((chunks, CHUNK, CHUNK), f32),
            pltpu.VMEM((rows, 2 * NS), f32),
            pltpu.VMEM((chunks, CHUNK, CHUNK), f32),
            pltpu.VMEM((rows, GW), f32),
            pltpu.VMEM((chunks, NS, GW), f32),
            pltpu.VMEM((rows + HALO + 16, GW), f32),
        ],
        flops=2 * rows * ssm * 1280,
        moved=rows * ssm * 12,
        deps=(ff_sum, out_sum, gate_sum, qk_send),
    )(
        proj_b, shr, conv_filter, conv_filter, cols, cum_rows, skip_lanes,
        bc_act, dscan, entering, leaving_grad,
    )
    def rest_dp(parts, got, deps=()):
        for i in range(2, steps):
            parts = collect_add(parts, got, deps)
            got = collect_move(parts, i)
        return parts, got

    def rest_one_way(parts, got, route, deps):
        for i in range(2, steps):
            parts = add_one(parts, got, route, i - 1, deps)
            got = move_one(parts, route, i)
        return parts, got

    ends = collect_end(
        [
            rest_dp(ff_sum, ff_got, low_v),
            rest_one_way(out_sum, out_got, 0, low_v),
            rest_one_way(gate_sum, gate_got, 1, low_v),
        ],
        low_v,
    )
    ends_t = finish_tensor(ends)
    ff_t = ends_t[:, : 2 * hidden_w]
    out_t = ends_t[:, 2 * hidden_w : 2 * hidden_w + out_w]
    gate_t = ends_t[:, 2 * hidden_w + out_w :]
    low_v, decay_part, bias_part = call(
        settle_kernel,
        (tensor_count,),
        [
            pl.BlockSpec(memory_space=pl.ANY),
            shr_spec,
            whole(groups, rows, 128),
            whole(groups, SLOT, rows),
            whole(chunks, ssm),
            whole(rows, 128),
            whole(1, 128),
        ],
        [
            spec((ext, 128), lambda t: (0, per_val * t + per_val - 1)),
            whole(1, 128),
            whole(1, 128),
        ],
        [shape(low_v.shape, bf16), shape((1, 128), f32), shape((1, 128), f32)],
        [pltpu.VMEM((rows, 128), f32)],
        moved=rows * 128 * 60,
        aliases={0: 0},
        deps=ends,
    )(low_v, dshr, dcols, drows, dlast, step_lin, rate_row)
    qk_sum = collect_keep(normed_in, qk_low, qk_got, ends)
    qk_got = collect_move(qk_sum, 0)
    val_send, val_got = collect_send(ext_in, low_v, qk_sum)
    (grad_a,) = times_transposed([dgate, qk_low], in_a, [wide_f32], store, deps=val_send)
    val_sum = collect_keep(ext_in, low_v, val_got, grad_a)
    val_got = collect_move(val_sum, 0)
    qk_sum = collect_add(qk_sum, qk_got, val_sum)
    qk_got = collect_move(qk_sum, 1)
    (grad_b,) = times_transposed(
        [low_v], in_b, [shape((ext, model), f32)], store, deps=(val_sum, qk_sum)
    )
    val_sum = collect_add(val_sum, val_got, grad_b)
    val_got = collect_move(val_sum, 1)
    late_rows = lax.ppermute(grad_b[:HALO], "tensor", backward)
    residual_grad, gain_sums = call(
        first_back_kernel,
        (1,),
        [
            whole(rows, model), whole(ext, model), whole(HALO, model), whole(rows, model),
            whole(rows, model), whole(1, model), whole(1, model),
        ],
        [whole(rows, model), whole(8, model)],
        [wide_f32, shape((8, model), f32)],
        deps=val_sum,
    )(
        grad_a, grad_b, late_rows, ext_low[HALO:], middle_grad, gain_first[None, :], mlp_gain_part
    )
    last_z = collect_end(
        [rest_dp(val_sum, val_got), rest_dp(qk_sum, qk_got)], residual_grad
    )
    residual_grad, gain_sums = restore_all([residual_grad, gain_sums], last_z)
    last_t = finish_tensor(last_z)
    gate_up_sum = ff_t.reshape(depth, 2, hidden_w)
    val_t = last_t[:, :val_w]
    qk_t = last_t[:, val_w:]
    skip_part = dskip.reshape(heads, PH).sum(axis=-1)

    small = [
        gain_sums[0],
        gain_sums[1],
        jnp.concatenate([dtapv, dtaps], axis=1).reshape(-1),
        decay_part[0, :heads],
        skip_part,
        bias_part[0, :heads],
        gated_gain_part[0],
    ]
    sizes = [item.shape[0] for item in small]
    total = sum_all(jnp.concatenate(small))
    marks = [sum(sizes[:i]) for i in range(len(sizes) + 1)]
    sums = [total[marks[i] : marks[i + 1]] for i in range(len(sizes))]
    return (
        output,
        residual_grad,
        jnp.stack([gate_t, val_t[:, :gate_w]], axis=1),
        val_t[:, gate_w + shared_w : gate_w + shared_w + step_in.shape[1]],
        val_t[:, gate_w : gate_w + shared_w],
        qk_t[:, :query_w],
        qk_t[:, query_w : query_w + keyval_in.shape[1]],
        out_t[:, :gate_w].T,
        out_t[:, gate_w:].T,
        gate_up_sum,
        down_t.T,
        sums[0],
        sums[1],
        sums[2].reshape(conv_filter.shape),
        sums[3],
        sums[4],
        sums[5],
        sums[6],
    )


def solution(mesh):
    rows_spec = P(("dp", "tensor"), None)
    into = P("dp", "tensor")
    out_of = P("tensor", "dp")
    double = P("dp", None, "tensor")
    weights = (double, into, into, into, into, out_of, out_of, double, out_of)
    return jax.shard_map(
        shards,
        mesh=mesh,
        in_specs=(rows_spec,) + weights + (P(),) * 7 + (rows_spec,),
        out_specs=(rows_spec, rows_spec) + weights + (P(),) * 7,
        check_vma=False,
    )
```

```python
import functools

import jax
import jax.numpy as jnp
from jax import lax
from jax.experimental import pallas as pl
from jax.experimental.pallas import tpu as pltpu
from jax.sharding import PartitionSpec as P

PH = 64
NS = 128
KC = 4
AH = 8
KVH = 2
HD = 64
LEN = 1024
CHUNK = 128
HALO = 16
GROUP = 6
SLOT = 8
GW = GROUP * PH

epsilon = 1e-05
rope_base = 100000000000.0
masked_fill = -1e30
highest = lax.Precision.HIGHEST
f32 = jnp.float32
bf16 = jnp.bfloat16
VMEM_BYTES = 52 * 1024 * 1024


def call(
    kernel, grid, in_specs, out_specs, out_shape, scratch=(), flops=0, moved=0, aliases=None, deps=()
):
    late = jax.tree.leaves(deps)
    count = len(in_specs)

    def body(*refs):
        kernel(*refs[:count], *refs[count + len(late) :])

    run = pl.pallas_call(
        body,
        grid=grid,
        in_specs=list(in_specs) + [pl.BlockSpec(memory_space=pl.ANY)] * len(late),
        out_specs=out_specs,
        out_shape=out_shape,
        scratch_shapes=list(scratch),
        input_output_aliases=aliases or {},
        compiler_params=pltpu.CompilerParams(
            vmem_limit_bytes=VMEM_BYTES, dimension_semantics=("arbitrary",) * len(grid)
        ),
        cost_estimate=pl.CostEstimate(flops=1, bytes_accessed=1, transcendentals=0),
    )
    return lambda *args: run(*args, *late)


def spec(block, index):
    return pl.BlockSpec(block, index)


def shape(dims, kind):
    return jax.ShapeDtypeStruct(dims, kind)


def dot(left, right, dims):
    return lax.dot_general(left, right, ((dims[:1], dims[1:]), ((), ())), preferred_element_type=f32)


NN = (1, 0)
NT = (1, 1)
TN = (0, 0)


def sigmoid(value):
    return 1.0 / (1.0 + jnp.exp(-value))


def pair_lanes(left, right, rows):
    lane = lax.broadcasted_iota(jnp.int32, (rows, 2 * PH), 1)
    return jnp.where(lane < PH, left, right)


def spread_heads(columns, first, count, rows):
    parts = [
        pair_lanes(
            columns[:, first + 2 * p : first + 2 * p + 1],
            columns[:, first + 2 * p + 1 : first + 2 * p + 2],
            rows,
        )
        for p in range(count // 2)
    ]
    return jnp.concatenate(parts, axis=1) if len(parts) > 1 else parts[0]


def conv_of(ref, taps, rows):
    width = taps.shape[1]
    total = ref[pl.ds(HALO - KC + 1, rows), :width] * taps[0:1, :]
    for offset in range(1, KC):
        moved = ref[pl.ds(HALO - KC + 1 + offset, rows), :width]
        total = total + moved * taps[offset : offset + 1, :]
    return total


def causal_mask(transposed):
    row = lax.broadcasted_iota(jnp.int32, (CHUNK, CHUNK), 0)
    col = lax.broadcasted_iota(jnp.int32, (CHUNK, CHUNK), 1)
    return col >= row if transposed else row >= col


def exact(left, right, dims):
    return lax.dot_general(
        left,
        right,
        ((dims[:1], dims[1:]), ((), ())),
        precision=highest,
        preferred_element_type=f32,
    )


def lower_ones():
    return jnp.where(causal_mask(False), 1.0, 0.0)


def softplus(value):
    return jnp.maximum(value, 0.0) + jnp.log1p(jnp.exp(-jnp.abs(value)))


def prepare_kernel(
    t0_ref, t1_ref, t2_ref, t3_ref, bias_ref, rate_ref,
    shr_ref, step_ref, cols_ref, rows_ref, grow_ref,
):
    tails = [t0_ref[...], t1_ref[...], t2_ref[...], t3_ref[...]]
    ext = tails[0].shape[0]
    shr_ref[:, :NS] = pair_lanes(tails[0], pltpu.roll(tails[1], PH, 1), ext)
    shr_ref[:, NS:] = pair_lanes(tails[2], pltpu.roll(tails[3], PH, 1), ext)
    rows = ext - HALO
    lane = lax.broadcasted_iota(jnp.int32, (rows, 128), 1)
    steps = jnp.zeros((rows, 128), f32)
    for t in range(4):
        moved = pltpu.roll(tails[t][HALO:], (GROUP * t - PH) % 128, 1)
        steps = jnp.where(lane // GROUP == t, moved, steps)
    steps = steps + bias_ref[...]
    step_ref[...] = steps
    dt = softplus(steps)
    decay = -rate_ref[...] * dt
    lower = lower_ones()
    prefix = jnp.zeros((1, 128), f32)
    parts = []
    for c in range(rows // CHUNK):
        sl = slice(c * CHUNK, (c + 1) * CHUNK)
        cum = exact(lower, decay[sl], NN)
        parts.append(cum)
        grow_ref[sl, :] = jnp.exp(cum + prefix)
        prefix = prefix + cum[CHUNK - 1 : CHUNK]
    cum = jnp.concatenate(parts, axis=0)
    for t in range(4):
        shift = (-GROUP * t) % 128
        dt_own = pltpu.roll(dt, shift, 1) if t else dt
        cum_own = pltpu.roll(cum, shift, 1) if t else cum
        both = jnp.where(lane < SLOT, dt_own, pltpu.roll(cum_own, SLOT, 1))
        cols_ref[t] = both[:, : 2 * SLOT]
        rows_ref[t] = jnp.transpose(cum_own)[:SLOT]


def mixer_kernel(
    val_ref, shr_ref, tapv_ref, taps_ref, cols_ref, cumr_ref, skip_ref,
    y_ref, state_ref, bc_ref, aff_ref,
):
    rows = y_ref.shape[0]
    chunks = rows // CHUNK

    @pl.when(pl.program_id(0) == 0)
    def _():
        pre = conv_of(shr_ref, taps_ref[...], rows)
        bc_ref[...] = (pre * sigmoid(pre)).astype(bf16)
        for c in range(chunks):
            sl = pl.ds(c * CHUNK, CHUNK)
            aff_ref[c] = dot(bc_ref[sl, NS:], bc_ref[sl, :NS], NT)

    pre = conv_of(val_ref, tapv_ref[...], rows)
    head_in = pre * sigmoid(pre)
    mask = causal_mask(False)
    skip = skip_ref[...]
    state = jnp.zeros((NS, GW), f32)
    for c in range(chunks):
        sl = pl.ds(c * CHUNK, CHUNK)
        x = head_in[c * CHUNK : (c + 1) * CHUNK]
        cols = cols_ref[0, sl, :]
        cumc = cols[:, SLOT:]
        cumr = cumr_ref[0, :, sl]
        w = x * spread_heads(cols, 0, GROUP, CHUNK)
        w_low = w.astype(bf16)
        inner = []
        for p in range(GROUP // 2):
            both = []
            for h in (2 * p, 2 * p + 1):
                gap = cumc[:, h : h + 1] - cumr[h : h + 1, :]
                decay = jnp.exp(jnp.where(mask, gap, masked_fill))
                weight = (aff_ref[c] * decay).astype(bf16)
                both.append(dot(weight, w_low[:, p * 2 * PH : (p + 1) * 2 * PH], NN))
            inner.append(pair_lanes(both[0], both[1], CHUNK))
        out = jnp.concatenate(inner, axis=1) + skip * x
        b_now = bc_ref[sl, :NS]
        c_now = bc_ref[sl, NS:]
        last = cumc[CHUNK - 1 : CHUNK, :]
        if c > 0:
            grown = spread_heads(jnp.exp(cumc), 0, GROUP, CHUNK)
            out = out + dot(c_now, state.astype(bf16), NN) * grown
        y_ref[sl, :] = out
        to_end = spread_heads(jnp.exp(last - cumc), 0, GROUP, CHUNK)
        added = dot(b_now, (w * to_end).astype(bf16), TN)
        fall = spread_heads(jnp.exp(last), 0, GROUP, 1)
        state = state * fall + added
    state_ref[...] = state.astype(bf16)


def gate_lanes(ref, width):
    count = ref.shape[1] // (width + 2 * PH * 2)
    step = ref.shape[1] // count
    return jnp.concatenate([ref[:, t * step : t * step + width] for t in range(count)], axis=1)


def finish_kernel(
    y_ref, gate_ref, bc_ref, grow_ref, state_ref, gain_ref, attn_ref, scan_ref, heads_ref
):
    rows, width = y_ref.shape
    grown = spread_heads(grow_ref[...], 0, width // PH, rows)
    scan = y_ref[...] + dot(bc_ref[:, NS:], state_ref[...], NN) * grown
    scan_ref[...] = scan
    gate = gate_lanes(gate_ref, GW)
    pre = scan * gate * sigmoid(gate)
    inv = lax.rsqrt(jnp.mean(pre * pre, axis=1, keepdims=True) + epsilon)
    low = (pre * inv * gain_ref[...]).astype(bf16)
    step = GW + 2 * HD
    for t in range(width // GW):
        heads_ref[:, t * step : t * step + GW] = low[:, t * GW : (t + 1) * GW]
        heads_ref[:, t * step + GW : (t + 1) * step] = attn_ref[:, t * 2 * HD : (t + 1) * 2 * HD]


def ungate_kernel(
    grad_ref, scan_ref, gate_ref, bc_ref, grow_ref, gain_ref,
    dgate_ref, dscan_ref, dgain_ref, dstate_ref,
):
    rows, width = scan_ref.shape
    scan = scan_ref[...]
    gate = gate_lanes(gate_ref, GW)
    sig = sigmoid(gate)
    silu = gate * sig
    pre = scan * silu
    inv = lax.rsqrt(jnp.mean(pre * pre, axis=1, keepdims=True) + epsilon)
    normed = pre * inv
    step = GW + 2 * HD
    grad = jnp.concatenate(
        [grad_ref[:, t * step : t * step + GW] for t in range(width // GW)], axis=1
    )
    u = grad * gain_ref[...]
    cross = jnp.mean(u * normed, axis=1, keepdims=True)
    dpre = inv * (u - normed * cross)
    dscan = dpre * silu
    dgate_ref[...] = (dpre * scan * sig * (1.0 + gate * (1.0 - sig))).astype(bf16)
    dscan_ref[...] = dscan
    grown = spread_heads(grow_ref[...], 0, width // PH, rows)
    dstate = dot(bc_ref[:, NS:], (dscan * grown).astype(bf16), TN)
    dgain = jnp.sum(grad * normed, axis=0, keepdims=True)
    first = pl.program_id(0) == 0

    @pl.when(first)
    def _():
        dgain_ref[...] = dgain
        dstate_ref[...] = dstate

    @pl.when(jnp.logical_not(first))
    def _():
        dgain_ref[...] += dgain
        dstate_ref[...] += dstate


def split_sum(value, ones_at):
    high = value.astype(bf16)
    low = (value - high.astype(f32)).astype(bf16)
    return dot(high, ones_at, NN) + dot(low, ones_at, NN)


def unconv(ref, taps, dact, pad_ref, out_ref, dtaps_ref, rows):
    pre = conv_of(ref, taps, rows)
    sig = sigmoid(pre)
    dpre = dact * sig * (1.0 + pre * (1.0 - sig))
    lead = HALO + 8
    width = dact.shape[1]
    pad_ref[pl.ds(0, lead), :width] = jnp.zeros((lead, width), f32)
    pad_ref[pl.ds(lead + rows, 8), :width] = jnp.zeros((8, width), f32)
    pad_ref[pl.ds(lead, rows), :width] = dpre
    total = None
    dtaps = []
    for offset in range(KC):
        part = pad_ref[pl.ds(8 + KC - 1 - offset, rows + HALO), :width]
        part = part * taps[offset : offset + 1, :]
        total = part if total is None else total + part
        moved = ref[pl.ds(HALO - KC + 1 + offset, rows), :width]
        dtaps.append(jnp.sum(dpre * moved, axis=0, keepdims=True))
    out_ref[:, :width] = total.astype(out_ref.dtype)
    dtaps_ref[...] = jnp.concatenate(dtaps, axis=0)


def unmix_kernel(
    val_ref, shr_ref, tapv_ref, taps_ref, in_ref, cumr_ref, skip_ref, bc_ref,
    dscan_ref, enter_ref, dleave_ref,
    dval_ref, dshr_ref, cols_ref, rows_ref, dlast_ref, dtapv_ref, dtaps_ref, dskip_ref,
    daff_ref, dbc_ref, aff_ref, dx_ref, states_ref, pad_ref,
):
    rows = dscan_ref.shape[0]
    chunks = rows // CHUNK
    step = pl.program_id(0)

    @pl.when(step == 0)
    def _():
        for c in range(chunks):
            sl = pl.ds(c * CHUNK, CHUNK)
            aff_ref[c] = dot(bc_ref[sl, :NS], bc_ref[sl, NS:], NT)
        daff_ref[...] = jnp.zeros(daff_ref.shape, f32)
        dbc_ref[...] = jnp.zeros(dbc_ref.shape, f32)

    pre = conv_of(val_ref, tapv_ref[...], rows)
    dx_ref[...] = pre * sigmoid(pre)
    mask = causal_mask(True)
    skip = skip_ref[...]
    lane = lax.broadcasted_iota(jnp.int32, (GW, 128), 0) // PH
    slot = lax.broadcasted_iota(jnp.int32, (GW, 128), 1)
    ones_dt = jnp.where(lane == slot, 1.0, 0.0).astype(bf16)
    ones_cum = jnp.where(lane + SLOT == slot, 1.0, 0.0).astype(bf16)
    half_lane = lax.broadcasted_iota(jnp.int32, (CHUNK, 2 * PH), 1) // PH
    slot_lane = lax.broadcasted_iota(jnp.int32, (CHUNK, 128), 1)

    state = enter_ref[...].astype(f32)
    states_ref[0] = state
    for c in range(chunks - 1):
        sl = pl.ds(c * CHUNK, CHUNK)
        cumc = in_ref[0, sl, SLOT:]
        last = cumc[CHUNK - 1 : CHUNK, :]
        scale = spread_heads(in_ref[0, sl, :SLOT] * jnp.exp(last - cumc), 0, GROUP, CHUNK)
        added = dot(bc_ref[sl, :NS], (dx_ref[sl, :] * scale).astype(bf16), TN)
        state = state * spread_heads(jnp.exp(last), 0, GROUP, 1) + added
        states_ref[c + 1] = state

    dstate = dleave_ref[...].astype(f32)
    dskip = jnp.zeros((1, GW), f32)
    for c in reversed(range(chunks)):
        sl = pl.ds(c * CHUNK, CHUNK)
        x = dx_ref[sl, :]
        dy = dscan_ref[sl, :]
        dy_low = dy.astype(bf16)
        cumc = in_ref[0, sl, SLOT:]
        cumr = cumr_ref[0, :, sl]
        last = cumc[CHUNK - 1 : CHUNK, :]
        dt = spread_heads(in_ref[0, sl, :SLOT], 0, GROUP, CHUNK)
        w = x * dt
        w_low = w.astype(bf16)
        b_now = bc_ref[sl, :NS]
        c_now = bc_ref[sl, NS:]
        affinity = aff_ref[c]
        dcum = jnp.zeros((CHUNK, 128), f32)
        daff = daff_ref[c]
        dw_parts = []
        for p in range(GROUP // 2):
            pair = slice(p * 2 * PH, (p + 1) * 2 * PH)
            both = []
            for h in (2 * p, 2 * p + 1):
                gap = cumr[h : h + 1, :] - cumc[:, h : h + 1]
                decay = jnp.exp(jnp.where(mask, gap, masked_fill))
                weight = affinity * decay
                w_own = jnp.where(half_lane == h - 2 * p, w[:, pair], 0.0).astype(bf16)
                dweight = dot(w_own, dy_low[:, pair], NT)
                daff = daff + dweight * decay
                moved = dweight * weight
                rows_ref[0, h : h + 1, sl] = jnp.sum(moved, axis=0, keepdims=True)
                dcum = dcum - jnp.where(
                    slot_lane == SLOT + h, jnp.sum(moved, axis=1, keepdims=True), 0.0
                )
                both.append(dot(weight.astype(bf16), dy_low[:, pair], NN))
            dw_parts.append(pair_lanes(both[0], both[1], CHUNK))
        daff_ref[c] = daff
        state = states_ref[c]
        state_low = state.astype(bf16)
        dstate_low = dstate.astype(bf16)
        grown = spread_heads(jnp.exp(cumc), 0, GROUP, CHUNK)
        to_end = spread_heads(jnp.exp(last - cumc), 0, GROUP, CHUNK)
        fall = spread_heads(jnp.exp(last), 0, GROUP, 1)
        dy_grown = (dy * grown).astype(bf16)
        carried = dot(c_now, state_low, NN) * grown
        from_end = dot(b_now, dstate_low, NN) * to_end
        dbc_ref[sl, NS:] += dot(dy_grown, state_low, NT)
        dbc_ref[sl, :NS] += dot((w * to_end).astype(bf16), dstate_low, NT)
        dw = jnp.concatenate(dw_parts, axis=1) + from_end
        ended = w * from_end
        cols_ref[0, sl, :] = (
            dcum + split_sum(dw * x, ones_dt) + split_sum(dy * carried - ended, ones_cum)
        )
        dlast_ref[c : c + 1, :] = jnp.sum(ended, axis=0, keepdims=True) + fall * jnp.sum(
            state * dstate, axis=0, keepdims=True
        )
        dstate = fall * dstate + dot(c_now, dy_grown, TN)
        dskip = dskip + jnp.sum(dy * x, axis=0, keepdims=True)
        dx_ref[sl, :] = dw * dt + skip * dy
    dskip_ref[...] = dskip
    unconv(val_ref, tapv_ref[...], dx_ref[...], pad_ref, dval_ref, dtapv_ref, rows)

    @pl.when(step == pl.num_programs(0) - 1)
    def _():
        for c in range(chunks):
            sl = pl.ds(c * CHUNK, CHUNK)
            daff_low = daff_ref[c].astype(bf16)
            dbc_ref[sl, :NS] += dot(daff_low, bc_ref[sl, NS:], NN)
            dbc_ref[sl, NS:] += dot(daff_low, bc_ref[sl, :NS], TN)
        unconv(shr_ref, taps_ref[...], dbc_ref[...], pad_ref, dshr_ref, dtaps_ref, rows)


def settle_kernel(
    low_in_ref, dshr_ref, cols_ref, rows_ref, dlast_ref, step_ref, rate_ref,
    low_ref, ddecay_ref, dbias_ref, dstep_ref,
):
    rows = step_ref.shape[0]
    t = pl.program_id(0)
    lane = lax.broadcasted_iota(jnp.int32, (rows, 128), 1)

    @pl.when(t == 0)
    def _():
        ddt = jnp.zeros((rows, 128), f32)
        dcum = jnp.zeros((rows, 128), f32)
        for i in range(4):
            own = lane // GROUP == i
            cols = cols_ref[i]
            ddt = jnp.where(own, pltpu.roll(cols, GROUP * i, 1) if i else cols, ddt)
            dcum = jnp.where(own, pltpu.roll(cols, (GROUP * i - SLOT) % 128, 1), dcum)
        filled = jnp.concatenate(
            [rows_ref[i] for i in range(4)] + [jnp.zeros((128 - 4 * SLOT, rows), f32)], axis=0
        )
        turned = jnp.transpose(filled)
        for i in range(4):
            moved = pltpu.roll(turned, ((GROUP - SLOT) * i) % 128, 1) if i else turned
            dcum = dcum + jnp.where(lane // GROUP == i, moved, 0.0)
        width = dlast_ref.shape[1]
        head = lax.broadcasted_iota(jnp.int32, (width, 128), 0) // PH
        place = lax.broadcasted_iota(jnp.int32, (width, 128), 1)
        at_end = exact(dlast_ref[...], jnp.where(head == place, 1.0, 0.0), NN)
        lower = lower_ones()
        steps = step_ref[...]
        rate = rate_ref[...]
        decay = -rate * softplus(steps)
        ddecay = jnp.zeros((1, 128), f32)
        dbias = jnp.zeros((1, 128), f32)
        for c in range(rows // CHUNK):
            sl = slice(c * CHUNK, (c + 1) * CHUNK)
            dlog = exact(lower, dcum[sl], TN) + at_end[c : c + 1]
            ddecay = ddecay + jnp.sum(dlog * decay[sl], axis=0, keepdims=True)
            dstep = (ddt[sl] - rate * dlog) * sigmoid(steps[sl])
            dbias = dbias + jnp.sum(dstep, axis=0, keepdims=True)
            dstep_ref[sl, :] = dstep
        ddecay_ref[...] = ddecay
        dbias_ref[...] = dbias

    for i in range(4):

        @pl.when(t == i)
        def _(i=i):
            shared = dshr_ref[:, (i // 2) * 2 * PH : (i // 2 + 1) * 2 * PH]
            if i % 2:
                shared = pltpu.roll(shared, PH, 1)
            steps = pltpu.roll(dstep_ref[...], (PH - GROUP * i) % 128, 1)
            steps = jnp.where((lane >= PH) & (lane < PH + GROUP), steps, 0.0)
            low_ref[pl.ds(0, HALO), :] = jnp.where(lane < PH, 1.0, 0.0)[:HALO].astype(bf16) * (
                shared[:HALO].astype(bf16)
            )
            low_ref[pl.ds(HALO, rows), :] = jnp.where(lane < PH, shared[HALO:], steps).astype(bf16)


def first_back_kernel(
    a_ref, b_ref, late_ref, rows_ref, middle_ref, gain_ref, more_ref, out_ref, gains_ref
):
    rows = a_ref.shape[0]
    out_ref[...] = a_ref[...] + b_ref[pl.ds(HALO, rows), :]
    out_ref[pl.ds(rows - HALO, HALO), :] += late_ref[...]
    grad = out_ref[...]
    values = rows_ref[...].astype(f32)
    inv = lax.rsqrt(jnp.mean(values * values, axis=1, keepdims=True) + epsilon)
    normed = values * inv
    gains_ref[...] = jnp.zeros(gains_ref.shape, f32)
    gains_ref[0:1, :] = jnp.sum(grad * normed, axis=0, keepdims=True)
    gains_ref[1:2, :] = more_ref[...]
    scaled = grad * gain_ref[...]
    cross = jnp.mean(scaled * normed, axis=1, keepdims=True)
    out_ref[...] = middle_ref[...] + inv * (scaled - normed * cross)


def swap_halves(value):
    half = HD // 2
    width = value.shape[1]
    lane = lax.broadcasted_iota(jnp.int32, value.shape, 1) % HD
    return jnp.where(
        lane < half, pltpu.roll(value, width - half, 1), pltpu.roll(value, half, 1)
    )


def rotate_kernel(t0_ref, t1_ref, t2_ref, t3_ref, cos_ref, sin_ref, out_ref):
    rows = cos_ref.shape[0]
    for head, (key, value) in enumerate(((t0_ref, t1_ref), (t2_ref, t3_ref))):
        both = pair_lanes(key[...], pltpu.roll(value[...], HD, 1), rows)
        out = both * cos_ref[...] + swap_halves(both) * sin_ref[...]
        out_ref[:, head * 2 * HD : (head + 1) * 2 * HD] = out.astype(bf16)


def unrotate_kernel(low_in_ref, own_ref, late_ref, cos_ref, sin_ref, out_ref):
    value = own_ref[...] + late_ref[...].astype(f32)
    value = value * cos_ref[...] + swap_halves(value * sin_ref[...])
    odd = lax.rem(pl.program_id(0), 2) == 1
    value = jnp.where(odd, pltpu.roll(value, HD, 1), value)
    lane = lax.broadcasted_iota(jnp.int32, value.shape, 1)
    out_ref[...] = jnp.where(lane < HD, value, 0.0).astype(bf16)


def head_queries(query, which):
    lane = lax.broadcasted_iota(jnp.int32, query.shape, 1)
    moved = pltpu.roll(query, HD, 1) if which else query
    return jnp.where(lane < HD, moved, 0.0)


def score_weights(query, before, own, allowed):
    early = jnp.where(allowed, dot(query, before, NT), masked_fill)
    late = dot(query, own, NT)
    row = lax.broadcasted_iota(jnp.int32, late.shape, 0)
    col = lax.broadcasted_iota(jnp.int32, late.shape, 1)
    late = jnp.where(row >= col, late, masked_fill)
    top = jnp.maximum(
        jnp.max(early, axis=1, keepdims=True), jnp.max(late, axis=1, keepdims=True)
    )
    early = jnp.exp(early - top)
    late = jnp.exp(late - top)
    total = jnp.sum(early, axis=1, keepdims=True) + jnp.sum(late, axis=1, keepdims=True)
    return early, late, 1.0 / total


def rotated_queries(q_ref, cos_ref, sin_ref):
    query = q_ref[...]
    return (query * cos_ref[...] + swap_halves(query) * sin_ref[...]) * (HD**-0.5)


def attend_kernel(part_ref, q_ref, cos_ref, sin_ref, before_ref, own_ref, out_ref):
    allowed = part_ref[0] > 0
    query = rotated_queries(q_ref, cos_ref, sin_ref)
    before = before_ref[...]
    own = own_ref[...]
    results = []
    for which in range(2):
        q_low = head_queries(query, which).astype(bf16)
        early, late, scale = score_weights(q_low, before, own, allowed)
        result = dot(early.astype(bf16), before, NN) + dot(late.astype(bf16), own, NN)
        results.append(result * scale)
    out_ref[...] = pair_lanes(pltpu.roll(results[0], HD, 1), results[1], query.shape[0]).astype(
        bf16
    )


def unattend_kernel(
    part_ref, q_ref, cos_ref, sin_ref, before_ref, own_ref, dout_ref,
    dq_ref, dbefore_ref, down_ref,
):
    allowed = part_ref[0] > 0
    query = rotated_queries(q_ref, cos_ref, sin_ref)
    before = before_ref[...]
    own = own_ref[...]
    dout = dout_ref[...]
    lane = lax.broadcasted_iota(jnp.int32, dout.shape, 1)
    dqs = []
    dbefore = None
    down = None
    for which in range(2):
        q_low = head_queries(query, which).astype(bf16)
        early, late, scale = score_weights(q_low, before, own, allowed)
        early = early * scale
        late = late * scale
        dout_own = dout if which else pltpu.roll(dout, HD, 1)
        dout_low = jnp.where(lane >= HD, dout_own, 0.0).astype(bf16)
        dearly = dot(dout_low, before, NT)
        dlate = dot(dout_low, own, NT)
        cross = jnp.sum(early * dearly, axis=1, keepdims=True) + jnp.sum(
            late * dlate, axis=1, keepdims=True
        )
        dearly = (early * (dearly - cross)).astype(bf16)
        dlate = (late * (dlate - cross)).astype(bf16)
        dqs.append(dot(dearly, before, NN) + dot(dlate, own, NN))
        part_before = dot(dearly, q_low, TN) + dot(early.astype(bf16), dout_low, TN)
        part_own = dot(dlate, q_low, TN) + dot(late.astype(bf16), dout_low, TN)
        dbefore = part_before if dbefore is None else dbefore + part_before
        down = part_own if down is None else down + part_own
    dq = pair_lanes(dqs[0], pltpu.roll(dqs[1], HD, 1), dout.shape[0]) * (HD**-0.5)
    dq_ref[...] = (dq * cos_ref[...] + swap_halves(dq * sin_ref[...])).astype(bf16)
    first = lax.rem(pl.program_id(0), AH // KVH // 2) == 0

    @pl.when(first)
    def _():
        dbefore_ref[...] = dbefore
        down_ref[...] = down

    @pl.when(jnp.logical_not(first))
    def _():
        dbefore_ref[...] += dbefore
        down_ref[...] += down


def times(rows_in, blocks, outs, finish, extras=(), specs=(), out_specs=None, deps=()):
    rows, depth = rows_in.shape
    groups, _, width = blocks[0].shape
    tile = width
    count = len(blocks)
    tile_spec = spec((rows, tile), lambda i: (0, i))

    def kernel(rows_ref, *refs):
        weight = jnp.concatenate([ref[0] for ref in refs[:count]], axis=0)
        finish(dot(rows_ref[...], weight, NN), *refs[count:])

    return call(
        kernel,
        (groups,),
        [spec((rows, depth), lambda i: (0, 0))]
        + [spec((1, b.shape[1], tile), lambda i: (i, 0, 0)) for b in blocks]
        + list(specs),
        out_specs or [tile_spec] * len(outs),
        outs,
        flops=2 * rows * depth * width * groups,
        moved=depth * width * groups * 2 + rows * width * groups * 4,
        deps=deps,
    )(rows_in, *blocks, *extras)


def times_transposed(lefts, blocks, outs, finish, extras=(), deps=()):
    rows = lefts[0].shape[0]
    groups, _, width = blocks[0].shape
    count = len(blocks)
    depth = sum(b.shape[1] for b in blocks)
    whole = lambda item: spec(item.shape, lambda i: (0, 0))

    def kernel(*refs):
        left = [ref[...] for ref in refs[: len(lefts)]]
        left = jnp.concatenate(left, axis=1) if len(left) > 1 else left[0]
        refs = refs[len(lefts) :]
        weight = jnp.concatenate([ref[0] for ref in refs[:count]], axis=0)
        part = dot(left, weight, NT)
        total = refs[-1]
        step = pl.program_id(0)

        @pl.when(step == 0)
        def _():
            total[...] = part

        @pl.when(step > 0)
        def _():
            total[...] += part

        @pl.when(step == pl.num_programs(0) - 1)
        def _():
            finish(total[...], *refs[count:-1])

    return call(
        kernel,
        (groups,),
        [spec((rows, item.shape[1] // groups), lambda i: (0, i)) for item in lefts]
        + [spec((1, b.shape[1], width), lambda i: (i, 0, 0)) for b in blocks]
        + [whole(e) for e in extras],
        [whole(o) for o in outs],
        outs,
        [pltpu.VMEM((rows, depth), f32)],
        flops=2 * rows * depth * width * groups,
        moved=depth * width * groups * 2 + rows * depth * 8,
        deps=deps,
    )(*lefts, *blocks, *extras)


def store(value, out_ref):
    out_ref[...] = value.astype(out_ref.dtype)


def add_store(value, other_ref, out_ref):
    out_ref[...] = value + other_ref[...]


def middle_finish(value, rows_ref, gain_ref, middle_ref, low_ref):
    middle = rows_ref[...] + value
    middle_ref[...] = middle
    inv = lax.rsqrt(jnp.mean(middle * middle, axis=1, keepdims=True) + epsilon)
    low_ref[...] = (middle * inv * gain_ref[...]).astype(bf16)


def unit_finish(value, hidden_ref, by_gate_ref, by_up_ref):
    half = value.shape[1] // 2
    gate = value[:, :half]
    up = value[:, half:]
    sig = sigmoid(gate)
    silu = gate * sig
    hidden_ref[...] = (silu * up).astype(bf16)
    by_gate_ref[...] = (up * sig * (1.0 + gate * (1.0 - sig))).astype(bf16)
    by_up_ref[...] = silu.astype(bf16)


def unit_back_finish(value, by_gate_ref, by_up_ref, out_ref):
    half = value.shape[1]
    out_ref[:, :half] = (value * by_gate_ref[...].astype(f32)).astype(bf16)
    out_ref[:, half:] = (value * by_up_ref[...].astype(f32)).astype(bf16)


def middle_back_finish(value, middle_ref, cot_ref, gain_ref, grad_ref, low_ref, dgain_ref):
    middle = middle_ref[...]
    inv = lax.rsqrt(jnp.mean(middle * middle, axis=1, keepdims=True) + epsilon)
    normed = middle * inv
    dgain_ref[...] = jnp.sum(value * normed, axis=0, keepdims=True)
    scaled = value * gain_ref[...]
    cross = jnp.mean(scaled * normed, axis=1, keepdims=True)
    grad = cot_ref[...].astype(f32) + inv * (scaled - normed * cross)
    grad_ref[...] = grad
    low_ref[...] = grad.astype(bf16)


def partner(value, bit):
    count = lax.axis_size("dp")
    return lax.ppermute(value, "dp", [(i, i ^ (1 << bit)) for i in range(count)])


def high_bits():
    return list(range(1, lax.axis_size("dp").bit_length() - 1))


def put_rows(out_ref, parts):
    if parts[0].shape[0] % 16:
        parts = [jnp.concatenate([p.astype(f32) for p in parts], axis=0).astype(bf16)]
    at = 0
    for p in parts:
        out_ref[0, at : at + p.shape[0], :] = p
        at += p.shape[0]


def cut_pieces(gathered, ranges, deps=()):
    groups, rows, width = gathered.shape
    half = rows // 2

    def kernel(in_ref, *out_refs):
        for i, (start, stop) in enumerate(ranges):
            part = in_ref[0, :, start:stop]
            if half % 16:
                part = part.astype(f32)
            out_refs[2 * i][0] = part[:half].astype(bf16)
            out_refs[2 * i + 1][0] = part[half:].astype(bf16)

    sizes = [stop - start for start, stop in ranges for _ in range(2)]
    outs = call(
        kernel,
        (groups,),
        [spec((1, rows, width), lambda t: (t, 0, 0))],
        [spec((1, half, w), lambda t: (t, 0, 0)) for w in sizes],
        [shape((groups, half, w), bf16) for w in sizes],
        moved=groups * rows * width * 4,
        deps=deps,
    )(gathered)
    return [(outs[2 * i], outs[2 * i + 1]) for i in range(len(ranges))]


def cut_exchanged(own, deps=()):
    count = lax.axis_size("tensor")
    pieces = [own]
    for far in range(1, count):
        pieces.append(lax.ppermute(own, "tensor", [(i, i ^ far) for i in range(count)]))
    rows, width = own.shape
    half = rows // 2

    def kernel(me_ref, *refs):
        upper_ref, lower_ref = refs[-2:]
        source = jnp.bitwise_xor(pl.program_id(0), me_ref[0])
        for i in range(count):

            @pl.when(source == i)
            def _(i=i):
                part = refs[i][...]
                if half % 16:
                    part = part.astype(f32)
                upper_ref[0] = part[:half].astype(bf16)
                lower_ref[0] = part[half:].astype(bf16)

    return call(
        kernel,
        (count,),
        [pl.BlockSpec(memory_space=pltpu.SMEM)] + [spec((rows, width), lambda t: (0, 0))] * count,
        [spec((1, half, width), lambda t: (t, 0, 0))] * 2,
        [shape((count, half, width), bf16)] * 2,
        moved=count * rows * width * 4,
        deps=deps,
    )(lax.axis_index("tensor").astype(jnp.int32).reshape(1), *pieces)


def spread_send(held, step):
    bits = high_bits()
    return partner(held[0], bits[step]), partner(held[1], bits[-1 - step])


def join_all(items, deps=()):
    groups = items[0][0][0].shape[0]
    args, in_specs, out_specs, outs, moved = [], [], [], [], 0
    for held, got, last in items:
        _, rows, width = held[0].shape
        args += [held[0], got[0], held[1], got[1]]
        in_specs += [spec((1, rows, width), lambda t: (t, 0, 0))] * 4
        size = 4 if last else 2
        number = 1 if last else 2
        out_specs += [spec((1, size * rows, width), lambda t: (t, 0, 0))] * number
        outs += [shape((groups, size * rows, width), bf16)] * number
        moved += groups * rows * width * 16

    def kernel(*refs):
        out_refs = list(refs[len(args) :])
        for i, (_, _, last) in enumerate(items):
            a_ref, b_ref, c_ref, d_ref = refs[4 * i : 4 * i + 4]
            upper = [a_ref[0], b_ref[0]]
            lower = [c_ref[0], d_ref[0]]
            if last:
                put_rows(out_refs.pop(0), upper + lower)
            else:
                put_rows(out_refs.pop(0), upper)
                put_rows(out_refs.pop(0), lower)

    out = list(
        call(kernel, (groups,), in_specs, out_specs, outs, moved=moved, deps=deps)(*args)
    )
    return [[out.pop(0)] if last else [out.pop(0), out.pop(0)] for _, _, last in items]


def join(held, got, deps=(), last=False):
    return join_all([(held, got, last)], deps)[0]


def spread_rest(held, got, first, deps=()):
    steps = len(high_bits())
    for i in range(first, steps):
        held = join(held, got, deps, i + 1 == steps)
        if i + 1 < steps:
            got = spread_send(held, i + 1)
    return held


def spread_end(held):
    return held[0], partner(held[0], 0)


def route_bits(route):
    return high_bits()[::-1] if route else high_bits()


def send_one(held, route, step):
    return partner(held, route_bits(route)[step])


def join_one(held, got, route, step, deps=()):
    groups, rows, width = held.shape
    bits = route_bits(route)
    masks = [(0, 0), (0, 1)]
    for bit in bits[: step + 1]:
        masks = masks + [(m | (1 << bit), p) for m, p in masks]
    places = list(range(len(masks)))
    if step + 1 == len(bits):
        goal = block_masks()[: len(masks)]
        places = [masks.index(m) for m in goal]
    size = 2 * rows // len(masks)

    def kernel(a_ref, b_ref, out_ref):
        if step + 1 < len(bits):
            put_rows(out_ref, [a_ref[0], b_ref[0]])
            return
        parts = []
        for place in places:
            ref, at = (a_ref, place * size) if place * size < rows else (b_ref, place * size - rows)
            parts.append(ref[0, at : at + size, :])
        put_rows(out_ref, parts)

    one = spec((1, rows, width), lambda t: (t, 0, 0))
    return call(
        kernel,
        (groups,),
        [one] * 2,
        spec((1, 2 * rows, width), lambda t: (t, 0, 0)),
        shape((groups, 2 * rows, width), bf16),
        moved=groups * rows * width * 8,
        deps=deps,
    )(held, got)


def rest_one(held, got, route, first, deps=()):
    steps = len(high_bits())
    for i in range(first, steps):
        held = join_one(held, got, route, i, deps)
        if i + 1 < steps:
            got = send_one(held, route, i + 1)
    return held


def slice_one(gathered, start, stop, deps=()):
    groups, rows, width = gathered.shape

    def kernel(in_ref, out_ref):
        out_ref[0] = in_ref[0, :, start:stop]

    return call(
        kernel,
        (groups,),
        [spec((1, rows, width), lambda t: (t, 0, 0))],
        spec((1, rows, stop - start), lambda t: (t, 0, 0)),
        shape((groups, rows, stop - start), bf16),
        moved=groups * rows * width * 4,
        deps=deps,
    )(gathered)


def tile_of(width):
    return next(t for t in (1024, 768, 512, 256, 128) if width % t == 0)


def collect_send(left, right, deps=()):
    rows, depth = left.shape
    near = depth // 2
    width = right.shape[1]
    tile = tile_of(width)

    def kernel(left_ref, right_ref, out_ref):
        out_ref[...] = dot(left_ref[...], right_ref[...], TN).astype(bf16)

    send = call(
        kernel,
        (width // tile,),
        [spec((rows, near), lambda i: (0, 1)), spec((rows, tile), lambda i: (0, i))],
        spec((near, tile), lambda i: (0, i)),
        shape((near, width), bf16),
        flops=2 * rows * near * width,
        moved=(rows + near) * width * 2,
        deps=deps,
    )(left, right)
    return send, partner(send, 0)


def collect_keep(left, right, got, deps=(), route=None):
    rows, depth = left.shape
    near = depth // 2
    quarter = near // 4
    if route is not None:
        masks, bit = route_masks(route, 0)
        lists = split_masks(masks, bit)
    else:
        lists = [[2 * i, 2 * i + 1] for i in range(4)]
    size = near // sum(len(x) for x in lists) if route is not None else quarter // 2
    width = right.shape[1]
    tile = tile_of(width)

    def kernel(left_ref, right_ref, got_ref, *out_refs):
        total = dot(left_ref[...], right_ref[...], TN) + got_ref[...].astype(f32)
        for places, out_ref in zip(lists, out_refs):
            out_ref[...] = pick_rows(total, places, size).astype(bf16)

    high = near // len(lists)
    out = spec((high, tile), lambda i: (0, i))
    return call(
        kernel,
        (width // tile,),
        [
            spec((rows, near), lambda i: (0, 0)),
            spec((rows, tile), lambda i: (0, i)),
            spec((near, tile), lambda i: (0, i)),
        ],
        [out] * len(lists),
        [shape((high, width), bf16)] * len(lists),
        flops=2 * rows * near * width,
        moved=(rows + 2 * near) * width * 2,
        deps=deps,
    )(left, right, got)


def pick_rows(value, places, size):
    parts, at = [], 0
    while at < len(places):
        end = at + 1
        while end < len(places) and places[end] == places[end - 1] + 1:
            end += 1
        parts.append(value[places[at] * size : (places[end - 1] + 1) * size])
        at = end
    return jnp.concatenate(parts, axis=0) if len(parts) > 1 else parts[0]


def route_masks(route, step):
    bits = route_bits(route)[::-1]
    masks = block_masks()[: 2 << len(bits)]
    for bit in bits[:step]:
        masks = [m for m in masks if not m[0] >> bit & 1]
    return masks, bits[step] if step < len(bits) else None


def split_masks(masks, bit):
    return [
        [i for i, m in enumerate(masks) if (m[0] >> bit & 1) == side] for side in range(2)
    ]


def move_one(parts, route, step):
    return partner(parts[1], route_bits(route)[::-1][step])


def add_one(parts, got, route, step, deps=()):
    rows, width = parts[0].shape
    half = rows // 2
    tile = tile_of(width)
    masks, bit = route_masks(route, step + 1)
    lists = split_masks(masks, bit)
    size = rows // len(masks)

    def kernel(a_ref, b_ref, *out_refs):
        total = a_ref[...].astype(f32) + b_ref[...].astype(f32)
        for places, out_ref in zip(lists, out_refs):
            out_ref[...] = pick_rows(total, places, size).astype(bf16)

    block = spec((rows, tile), lambda i: (0, i))
    return call(
        kernel,
        (width // tile,),
        [block] * 2,
        [spec((half, tile), lambda i: (0, i))] * 2,
        [shape((half, width), bf16)] * 2,
        moved=rows * width * 6,
        deps=deps,
    )(parts[0], got)


def collect_move(parts, step):
    bits = high_bits()
    return partner(parts[1], bits[-1 - step]), partner(parts[3], bits[step])


def collect_add(parts, got, deps=()):
    rows, width = parts[0].shape
    half = rows // 2
    tile = tile_of(width)

    def kernel(a_ref, b_ref, c_ref, d_ref, *out_refs):
        for i, (own, other) in enumerate(((a_ref, b_ref), (c_ref, d_ref))):
            total = own[...].astype(f32) + other[...].astype(f32)
            out_refs[2 * i][...] = total[:half].astype(bf16)
            out_refs[2 * i + 1][...] = total[half:].astype(bf16)

    block = spec((rows, tile), lambda i: (0, i))
    return call(
        kernel,
        (width // tile,),
        [block] * 4,
        [spec((half, tile), lambda i: (0, i))] * 4,
        [shape((half, width), bf16)] * 4,
        moved=rows * width * 12,
        deps=deps,
    )(parts[0], got[0], parts[2], got[1])


def collect_end(pairs, deps=()):
    groups = lax.axis_size("tensor")
    args, in_specs, widths, counts = [], [], [], []
    for parts, got in pairs:
        width = parts[0].shape[1] // groups
        widths.append(width)
        both = len(parts) == 4
        add = [parts[0], got[0], parts[2], got[1]] if both else [parts[0], got]
        counts.append(len(add))
        args += add
        in_specs += [spec((parts[0].shape[0], width), lambda t: (0, t))] * len(add)
        rows = parts[0].shape[0] // (1 if both else 2)

    def kernel(*refs):
        at = first = 0
        for width, count in zip(widths, counts):
            values = [ref[...].astype(f32) for ref in refs[first : first + count]]
            sums = [values[i] + values[i + 1] for i in range(0, count, 2)]
            out = jnp.concatenate(sums, axis=0) if len(sums) > 1 else sums[0]
            refs[-1][0, :, at : at + width] = out.astype(bf16)
            at += width
            first += count

    total = sum(widths)
    return call(
        kernel,
        (groups,),
        in_specs,
        spec((1, 2 * rows, total), lambda t: (t, 0, 0)),
        shape((groups, 2 * rows, total), bf16),
        moved=groups * rows * total * 12,
        deps=deps,
    )(*args)


def block_masks():
    bits = high_bits()
    count = 1 << len(bits)
    masks = []
    for core in range(2):
        for part in range(2):
            for j in range(count):
                order = bits[::-1] if part else bits
                mask = sum(((j >> i) & 1) << bit for i, bit in enumerate(order))
                masks.append((mask | core, part))
    return masks


def take_blocks(value, sources):
    width = value.shape[-1] // len(sources)
    axis = value.ndim - 1
    return jnp.concatenate(
        [lax.dynamic_slice_in_dim(value, s * width, width, axis) for s in sources], axis=axis
    )


def permute_features(value):
    me = lax.axis_index("dp")
    return take_blocks(value, [(me ^ mask) * 2 + part for mask, part in block_masks()])


def restore_features(value):
    me = lax.axis_index("dp")
    masks = block_masks()
    count = lax.axis_size("dp")
    table = jnp.array(
        [[masks.index((m, part)) for part in range(2)] for m in range(count)], jnp.int32
    )
    return take_blocks(
        value, [table[me ^ block, part] for block in range(count) for part in range(2)]
    )


def restore_all(values, deps=()):
    count = lax.axis_size("dp")
    if values[0].shape[1] // count != 128:
        return [restore_features(v) for v in values]
    masks = block_masks()
    places = [[masks.index((m, part)) for part in range(2)] for m in range(count)]
    rows = jnp.array([[p[0] // 2, p[0] % 2, p[1] // 2, p[1] % 2] for p in places], jnp.int32)
    table = rows[lax.axis_index("dp") ^ jnp.arange(count, dtype=jnp.int32)].reshape(-1)
    late = jax.tree.leaves(deps)
    number = len(values)

    def kernel(table_ref, *refs):
        i = pl.program_id(0)
        out_refs = refs[2 * number + len(late) :]
        for n in range(number):
            front, back = refs[2 * n][...], refs[2 * n + 1][...]
            front = jnp.where(table_ref[4 * i + 1] > 0, pltpu.roll(front, 64, 1), front)
            back = jnp.where(table_ref[4 * i + 3] > 0, back, pltpu.roll(back, 64, 1))
            lane = lax.broadcasted_iota(jnp.int32, front.shape, 1)
            out_refs[n][...] = jnp.where(lane < 64, front, back)

    in_specs = []
    for v in values:
        for at in (0, 2):
            in_specs.append(spec((v.shape[0], 128), lambda i, t, at=at: (0, t[4 * i + at])))
    in_specs += [pl.BlockSpec(memory_space=pl.ANY)] * len(late)
    return pl.pallas_call(
        kernel,
        grid_spec=pltpu.PrefetchScalarGridSpec(
            num_scalar_prefetch=1,
            grid=(count,),
            in_specs=in_specs,
            out_specs=[spec((v.shape[0], 128), lambda i, t: (0, i)) for v in values],
        ),
        out_shape=[shape(v.shape, v.dtype) for v in values],
        compiler_params=pltpu.CompilerParams(vmem_limit_bytes=VMEM_BYTES),
        cost_estimate=pl.CostEstimate(flops=1, bytes_accessed=1, transcendentals=0),
    )(table, *[v for v in values for _ in range(2)], *late)


def sum_all(value):
    for axis in ("dp", "tensor"):
        count = lax.axis_size(axis)
        for bit in range(count.bit_length() - 1):
            value = value + lax.ppermute(value, axis, [(i, i ^ (1 << bit)) for i in range(count)])
    return value


def norm_of(rows):
    inv = lax.rsqrt(jnp.mean(rows * rows, axis=-1, keepdims=True) + epsilon)
    return rows * inv, inv


def norm_back(grad, gain, normed, inv):
    scaled = grad * gain
    return inv * (scaled - normed * jnp.mean(scaled * normed, axis=-1, keepdims=True))


def over_tensor(piece):
    return lax.all_gather(piece, "tensor", axis=0)


def shards(
    residual,
    mixer_in,
    step_in,
    shared_in,
    query_in,
    keyval_in,
    mixer_proj,
    attn_proj,
    gate_up,
    down_proj,
    norm_gain,
    mlp_gain,
    conv_filter,
    decay_log,
    skip_gain,
    step_bias,
    gated_gain,
    cotangent,
):
    tensor_count = lax.axis_size("tensor")
    rows, model = residual.shape
    depth = mixer_in.shape[0]
    ssm = conv_filter.shape[1] - 2 * NS
    heads = ssm // PH
    groups = heads // GROUP
    chunks = rows // CHUNK
    span = LEN // rows
    part = lax.axis_index("tensor") % span
    onward = [(i, i + 1) for i in range(tensor_count) if i % span != span - 1]
    backward = [(j, i) for i, j in onward]
    hidden_w = gate_up.shape[2]
    gate_w = mixer_in.shape[2]
    query_w = query_in.shape[1]
    shared_w = shared_in.shape[1]
    attn_w = AH * HD
    ff = hidden_w * tensor_count
    steps = len(high_bits())

    def finish_dp(parts, got, deps):
        for i in range(2, steps):
            parts = collect_add(parts, got, deps)
            got = collect_move(parts, i)
        return collect_end([(parts, got)], deps)

    def finish_tensor(joined):
        total = lax.psum_scatter(joined, "tensor", scatter_dimension=0, tiled=False)
        return total.astype(f32)

    before_rows = lax.ppermute(residual[rows - HALO :], "tensor", onward)
    ext_low = permute_features(jnp.concatenate([before_rows, residual], axis=0))
    cot = permute_features(cotangent)
    gain_first = permute_features(norm_gain)
    gain_second = permute_features(mlp_gain)
    ext_normed, ext_inv = norm_of(ext_low.astype(f32))
    ext_in = (ext_normed * gain_first).astype(bf16)
    normed_first = ext_normed[HALO:]
    inv_first = ext_inv[HALO:]
    normed_in = ext_in[HALO:]
    group_rows = ext_low[HALO:].astype(f32)
    wide_f32 = shape((rows, model), f32)
    wide_low = shape((rows, model), bf16)
    second_row = gain_second[None, :]

    half = HD // 2
    frequency = rope_base ** (-2.0 * jnp.arange(half, dtype=f32) / HD)
    place = (part * rows + jnp.arange(rows, dtype=jnp.int32)).astype(f32)
    angles = place[:, None] * frequency[None, :]
    cosine = jnp.cos(angles)
    sine = jnp.sin(angles)
    ones = jnp.ones((rows, HD), f32)
    cos_q = jnp.concatenate([cosine] * 4, axis=1)
    sin_q = jnp.concatenate([-sine, sine] * 2, axis=1)
    cos_kv = jnp.concatenate([cosine, cosine, ones], axis=1)
    sin_kv = jnp.concatenate([-sine, sine, 0.0 * ones], axis=1)

    def padded(parts):
        width = sum(p.shape[1] for p in parts)
        return jnp.concatenate(parts + [jnp.zeros((depth, -width % 128), bf16)], axis=1)

    val_in = padded([mixer_in[:, 1], shared_in, step_in])
    gate_in = padded([mixer_in[:, 0], query_in, keyval_in])
    val_w = val_in.shape[1]
    out_in = jnp.concatenate([mixer_proj, attn_proj], axis=0).T
    out_w = out_in.shape[1]
    back_in = jnp.concatenate([out_in, down_proj.T], axis=1)
    gate_in_w = gate_in.shape[1]
    rest_z = over_tensor(
        jnp.concatenate([gate_in, gate_up.reshape(depth, 2 * hidden_w), back_in], axis=1)
    )
    ff_at = gate_in_w
    out_at = ff_at + 2 * hidden_w
    down_at = out_at + out_w
    tables = (cos_q, sin_q, cos_kv, sin_kv)
    val_held = cut_exchanged(val_in, (ext_in, tables, cot, group_rows))
    val_held = spread_rest(val_held, spread_send(val_held, 0), 0)
    in_b = spread_end(val_held)

    (proj_b,) = times(
        ext_in,
        in_b,
        [shape((rows + HALO, val_w * tensor_count), f32)],
        store,
    )

    ext = rows + HALO
    whole = lambda *dims: spec(dims, lambda i: (0,) * len(dims))
    tail = lambda count, t: (lambda i: (0, count * t + count - 1))
    per_val = val_w // 128
    bias_row = jnp.pad(step_bias, (0, 128 - heads))[None, :]
    rate_row = jnp.pad(jnp.exp(decay_log), (0, 128 - heads))[None, :]
    shr, step_lin, cols, cum_rows, grow = call(
        prepare_kernel,
        (1,),
        [spec((ext, 128), tail(per_val, t)) for t in range(4)] + [whole(1, 128)] * 2,
        [
            whole(ext, 2 * NS),
            whole(rows, 128),
            whole(groups, rows, 2 * SLOT),
            whole(groups, SLOT, rows),
            whole(rows, 128),
        ],
        [
            shape((ext, 2 * NS), f32),
            shape((rows, 128), f32),
            shape((groups, rows, 2 * SLOT), f32),
            shape((groups, SLOT, rows), f32),
            shape((rows, 128), f32),
        ],
        moved=rows * 128 * 40,
    )(proj_b, proj_b, proj_b, proj_b, bias_row, rate_row)
    skip_lanes = jnp.repeat(skip_gain, PH)[None, :]
    (gate_held,) = cut_pieces(rest_z, [(0, gate_in_w)], cols)
    gate_held = join(gate_held, spread_send(gate_held, 0))
    gate_got = spread_send(gate_held, 1)
    (out_held,) = cut_pieces(rest_z, [(out_at, down_at)], gate_held)
    out_got = spread_send(out_held, 0)

    val_spec = spec((ext, val_w), lambda g: (0, g))
    shr_spec = whole(ext, 2 * NS)
    tapv_spec = spec((KC, GW), lambda g: (0, g))
    taps_spec = spec((KC, 2 * NS), lambda g: (0, ssm // (2 * NS)))
    col_spec = spec((1, rows, 2 * SLOT), lambda g: (g, 0, 0))
    row_spec = spec((1, SLOT, rows), lambda g: (g, 0, 0))
    lane_spec = spec((1, GW), lambda g: (0, g))
    bc_spec = whole(rows, 2 * NS)
    grp_spec = spec((rows, GW), lambda g: (0, g))
    state_spec = spec((NS, GW), lambda g: (0, g))
    y_local, state_local, bc_act = call(
        mixer_kernel,
        (groups,),
        [val_spec, shr_spec, tapv_spec, taps_spec, col_spec, row_spec, lane_spec],
        [grp_spec, state_spec, bc_spec],
        [shape((rows, ssm), f32), shape((NS, ssm), bf16), shape((rows, 2 * NS), bf16)],
        [pltpu.VMEM((chunks, CHUNK, CHUNK), f32)],
        flops=2 * rows * ssm * 512,
        moved=rows * ssm * 8,
        deps=(gate_held, out_held),
    )(proj_b, shr, conv_filter, conv_filter, cols, cum_rows, skip_lanes)
    entering = lax.ppermute(state_local, "tensor", onward)
    per_gate = gate_held[0].shape[2] // 128
    for i in range(1, steps - 1):
        gate_held = join(gate_held, gate_got, y_local)
        gate_got = spread_send(gate_held, i + 1)
    gate_held, out_held = join_all(
        [(gate_held, gate_got, True), (out_held, out_got, False)], y_local
    )
    in_a = spread_end(gate_held)
    out_got = spread_send(out_held, 1)
    (ff_held,) = cut_pieces(rest_z, [(ff_at, out_at)], gate_held)
    ff_got = spread_send(ff_held, 0)
    (proj_a,) = times(
        normed_in,
        in_a,
        [shape((rows, per_gate * 128 * tensor_count), f32)],
        store,
        deps=ff_held,
    )
    for i in range(1, steps - 1):
        out_held = join(out_held, out_got, proj_a)
        out_got = spread_send(out_held, i + 1)
    out_held, ff_held = join_all(
        [(out_held, out_got, True), (ff_held, ff_got, False)], (proj_a, entering)
    )
    out_full = spread_end(out_held)
    ff_got = spread_send(ff_held, 1)

    kv_w = 2 * KVH * HD
    own_kv = call(
        rotate_kernel,
        (1,),
        [spec((rows, 128), tail(per_gate, t)) for t in range(4)] + [whole(rows, 2 * HD)] * 2,
        whole(rows, kv_w),
        shape((rows, kv_w), bf16),
        moved=rows * kv_w * 12,
    )(proj_a, proj_a, proj_a, proj_a, cos_kv, sin_kv)
    before_kv = lax.ppermute(own_kv, "tensor", onward)
    part_arg = part.astype(jnp.int32).reshape(1)
    pairs = AH // 2
    per_kv = AH // KVH // 2
    smem = pl.BlockSpec(memory_space=pltpu.SMEM)
    q_spec = spec((rows, 2 * HD), lambda i: (0, per_gate * i + GW // 128))
    table_spec = spec((rows, 2 * HD), lambda i: (0, 0))
    kv_spec = spec((rows, 2 * HD), lambda i: (0, i // per_kv))
    pair_spec = spec((rows, 2 * HD), lambda i: (0, i))
    attn_heads = call(
        attend_kernel,
        (pairs,),
        [smem, q_spec, table_spec, table_spec, kv_spec, kv_spec],
        pair_spec,
        shape((rows, attn_w), bf16),
        flops=2 * AH * rows * LEN * 256,
        moved=rows * attn_w * 8,
        deps=ff_held,
    )(part_arg, proj_a, cos_q, sin_q, before_kv, own_kv)

    (down_held,) = cut_pieces(rest_z, [(down_at, rest_z.shape[2])], (attn_heads, out_full))
    down_got = spread_send(down_held, 0)
    block_rows = CHUNK
    wide = spec((block_rows, ssm), lambda i: (i, 0))
    gate_block = spec((block_rows, proj_a.shape[1]), lambda i: (i, 0))
    heads_block = spec((block_rows, ssm + attn_w), lambda i: (i, 0))
    attn_block = spec((block_rows, attn_w), lambda i: (i, 0))
    bc_block = spec((block_rows, 2 * NS), lambda i: (i, 0))
    grow_block = spec((block_rows, 128), lambda i: (i, 0))
    state_whole = whole(NS, ssm)
    gain_whole = whole(1, ssm)
    gated_row = gated_gain[None, :]
    scanned, heads_all = call(
        finish_kernel,
        (rows // block_rows,),
        [wide, gate_block, bc_block, grow_block, state_whole, gain_whole, attn_block],
        [wide, heads_block],
        [shape((rows, ssm), f32), shape((rows, ssm + attn_w), bf16)],
        flops=2 * rows * ssm * NS,
        moved=rows * ssm * 14,
        deps=down_held,
    )(y_local, proj_a, bc_act, grow, entering, gated_row, attn_heads)

    ff_held = spread_rest(ff_held, ff_got, 1, heads_all)
    ff_full = spread_end(ff_held)
    middle, mlp_rows = times_transposed(
        [heads_all],
        out_full,
        [wide_f32, wide_low],
        middle_finish,
        (group_rows, second_row),
        deps=ff_held,
    )
    down_held = join(down_held, down_got, middle)
    down_got = spread_send(down_held, 1)
    unit = spec((rows, hidden_w), lambda i: (0, i))
    ff_low = shape((rows, ff), bf16)
    hidden, by_gate, by_up = times(
        mlp_rows, ff_full, [ff_low] * 3, unit_finish, out_specs=[unit] * 3, deps=down_held
    )
    down_held = spread_rest(down_held, down_got, 1, hidden)
    down_full = spread_end(down_held)
    down_send, down_got = collect_send(cot, hidden, down_held)
    (both_grad,) = times(
        cot,
        down_full,
        [shape((rows, 2 * ff), bf16)],
        unit_back_finish,
        (by_gate, by_up),
        (unit, unit),
        [spec((rows, 2 * hidden_w), lambda i: (0, i))],
        deps=down_send,
    )
    down_sum = collect_keep(cot, hidden, down_got, both_grad)
    down_got = collect_move(down_sum, 0)
    ff_send, ff_got = collect_send(mlp_rows, both_grad, down_sum)
    middle_grad, branch_grad, mlp_gain_part = times_transposed(
        [both_grad],
        ff_full,
        [wide_f32, wide_low, shape((1, model), f32)],
        middle_back_finish,
        (middle, cot, second_row),
        deps=(ff_send, down_sum),
    )

    down_sum = collect_add(down_sum, down_got, branch_grad)
    down_got = collect_move(down_sum, 1)
    (heads_grad,) = times(
        branch_grad, out_full, [shape((rows, ssm + attn_w), f32)], store, deps=down_sum
    )
    out_send, out_got = collect_send(branch_grad, heads_all, heads_grad)
    ff_sum = collect_keep(mlp_rows, both_grad, ff_got, out_send)
    ff_got = collect_move(ff_sum, 0)
    dgate, dscan, gated_gain_part, dstate_local = call(
        ungate_kernel,
        (rows // block_rows,),
        [heads_block, wide, gate_block, bc_block, grow_block, gain_whole],
        [wide, wide, gain_whole, state_whole],
        [
            shape((rows, ssm), bf16),
            shape((rows, ssm), f32),
            shape((1, ssm), f32),
            shape((NS, ssm), f32),
        ],
        flops=2 * rows * ssm * NS,
        moved=rows * ssm * 18,
        deps=(out_send, ff_sum),
    )(heads_grad, scanned, proj_a, bc_act, grow, gated_row)
    leaving_grad = lax.ppermute(dstate_local.astype(bf16), "tensor", backward)
    down_z = finish_dp(down_sum, down_got, dgate)
    down_t = finish_tensor(down_z)
    gate_send, gate_got = collect_send(normed_in, dgate, down_z)
    out_sum = collect_keep(branch_grad, heads_all, out_got, gate_send, 0)
    out_got = move_one(out_sum, 0, 0)
    (output,) = times_transposed(
        [hidden], down_full, [wide_f32], add_store, (middle,), deps=out_sum
    )
    gate_sum = collect_keep(normed_in, dgate, gate_got, (output, leaving_grad), 1)
    gate_got = move_one(gate_sum, 1, 0)
    (output,) = restore_all([output], gate_sum)

    dout_spec = spec((rows, 2 * HD), lambda i: (0, 4 * i + 3))
    qk_low, before_grad, own_grad = call(
        unattend_kernel,
        (pairs,),
        [smem, q_spec, table_spec, table_spec, kv_spec, kv_spec, dout_spec],
        [spec((rows, 2 * HD), lambda i: (0, 2 * i)), kv_spec, kv_spec],
        [shape((rows, 4 * HD * pairs), bf16), shape((rows, kv_w), f32), shape((rows, kv_w), f32)],
        flops=2 * AH * rows * LEN * 640,
        moved=rows * attn_w * 16,
        deps=(out_sum, gate_sum, output),
    )(part_arg, proj_a, cos_q, sin_q, before_kv, own_kv, heads_grad)
    late_grad = lax.ppermute(before_grad.astype(bf16), "tensor", backward)

    ff_sum = collect_add(ff_sum, ff_got, before_grad)
    ff_got = collect_move(ff_sum, 1)
    out_sum = add_one(out_sum, out_got, 0, 0, ff_sum)
    out_got = move_one(out_sum, 0, 1)
    gate_sum = add_one(gate_sum, gate_got, 1, 0, out_sum)
    gate_got = move_one(gate_sum, 1, 1)
    half_spec = spec((rows, 2 * HD), lambda t: (0, t // 2))
    qk_low = call(
        unrotate_kernel,
        (tensor_count,),
        [pl.BlockSpec(memory_space=pl.ANY), half_spec, half_spec] + [whole(rows, 2 * HD)] * 2,
        spec((rows, 2 * HD), lambda t: (0, 2 * t + 1)),
        shape(qk_low.shape, bf16),
        moved=rows * kv_w * 16,
        aliases={0: 0},
        deps=(ff_sum, out_sum, gate_sum),
    )(qk_low, own_grad, late_grad, cos_kv, sin_kv)

    qk_send, qk_got = collect_send(normed_in, qk_low)

    low_v, dshr, dcols, drows, dlast, dtapv, dtaps, dskip = call(
        unmix_kernel,
        (groups,),
        [
            val_spec, shr_spec, tapv_spec, taps_spec, col_spec, row_spec, lane_spec,
            bc_spec, grp_spec, state_spec, state_spec,
        ],
        [
            val_spec,
            shr_spec,
            spec((1, rows, 128), lambda g: (g, 0, 0)),
            row_spec,
            spec((chunks, GW), lambda g: (0, g)),
            tapv_spec,
            whole(KC, 2 * NS),
            lane_spec,
        ],
        [
            shape((ext, val_w * tensor_count), bf16),
            shape((ext, 2 * NS), f32),
            shape((groups, rows, 128), f32),
            shape((groups, SLOT, rows), f32),
            shape((chunks, ssm), f32),
            shape((KC, ssm), f32),
            shape((KC, 2 * NS), f32),
            shape((1, ssm), f32),
        ],
        [
            pltpu.VMEM((chunks, CHUNK, CHUNK), f32),
            pltpu.VMEM((rows, 2 * NS), f32),
            pltpu.VMEM((chunks, CHUNK, CHUNK), f32),
            pltpu.VMEM((rows, GW), f32),
            pltpu.VMEM((chunks, NS, GW), f32),
            pltpu.VMEM((rows + HALO + 16, GW), f32),
        ],
        flops=2 * rows * ssm * 1280,
        moved=rows * ssm * 12,
        deps=(ff_sum, out_sum, gate_sum, qk_send),
    )(
        proj_b, shr, conv_filter, conv_filter, cols, cum_rows, skip_lanes,
        bc_act, dscan, entering, leaving_grad,
    )
    def rest_dp(parts, got, deps=()):
        for i in range(2, steps):
            parts = collect_add(parts, got, deps)
            got = collect_move(parts, i)
        return parts, got

    def rest_one_way(parts, got, route, deps):
        for i in range(2, steps):
            parts = add_one(parts, got, route, i - 1, deps)
            got = move_one(parts, route, i)
        return parts, got

    ends = collect_end(
        [
            rest_dp(ff_sum, ff_got, low_v),
            rest_one_way(out_sum, out_got, 0, low_v),
            rest_one_way(gate_sum, gate_got, 1, low_v),
        ],
        low_v,
    )
    ends_t = finish_tensor(ends)
    ff_t = ends_t[:, : 2 * hidden_w]
    out_t = ends_t[:, 2 * hidden_w : 2 * hidden_w + out_w]
    gate_t = ends_t[:, 2 * hidden_w + out_w :]
    low_v, decay_part, bias_part = call(
        settle_kernel,
        (tensor_count,),
        [
            pl.BlockSpec(memory_space=pl.ANY),
            shr_spec,
            whole(groups, rows, 128),
            whole(groups, SLOT, rows),
            whole(chunks, ssm),
            whole(rows, 128),
            whole(1, 128),
        ],
        [
            spec((ext, 128), lambda t: (0, per_val * t + per_val - 1)),
            whole(1, 128),
            whole(1, 128),
        ],
        [shape(low_v.shape, bf16), shape((1, 128), f32), shape((1, 128), f32)],
        [pltpu.VMEM((rows, 128), f32)],
        moved=rows * 128 * 60,
        aliases={0: 0},
        deps=ends,
    )(low_v, dshr, dcols, drows, dlast, step_lin, rate_row)
    qk_sum = collect_keep(normed_in, qk_low, qk_got, ends)
    qk_got = collect_move(qk_sum, 0)
    val_send, val_got = collect_send(ext_in, low_v, qk_sum)
    (grad_a,) = times_transposed([dgate, qk_low], in_a, [wide_f32], store, deps=val_send)
    val_sum = collect_keep(ext_in, low_v, val_got, grad_a)
    val_got = collect_move(val_sum, 0)
    (grad_b,) = times_transposed(
        [low_v], in_b, [shape((ext, model), f32)], store, deps=val_sum
    )
    val_sum = collect_add(val_sum, val_got, grad_b)
    val_got = collect_move(val_sum, 1)
    qk_sum = collect_add(qk_sum, qk_got, val_sum)
    qk_got = collect_move(qk_sum, 1)
    late_rows = lax.ppermute(grad_b[:HALO], "tensor", backward)
    residual_grad, gain_sums = call(
        first_back_kernel,
        (1,),
        [
            whole(rows, model), whole(ext, model), whole(HALO, model), whole(rows, model),
            whole(rows, model), whole(1, model), whole(1, model),
        ],
        [whole(rows, model), whole(8, model)],
        [wide_f32, shape((8, model), f32)],
        deps=(val_sum, qk_sum),
    )(
        grad_a, grad_b, late_rows, ext_low[HALO:], middle_grad, gain_first[None, :], mlp_gain_part
    )
    last_z = collect_end(
        [rest_dp(val_sum, val_got), rest_dp(qk_sum, qk_got)], residual_grad
    )
    residual_grad, gain_sums = restore_all([residual_grad, gain_sums], last_z)
    last_t = finish_tensor(last_z)
    gate_up_sum = ff_t.reshape(depth, 2, hidden_w)
    val_t = last_t[:, :val_w]
    qk_t = last_t[:, val_w:]
    skip_part = dskip.reshape(heads, PH).sum(axis=-1)

    small = [
        gain_sums[0],
        gain_sums[1],
        jnp.concatenate([dtapv, dtaps], axis=1).reshape(-1),
        decay_part[0, :heads],
        skip_part,
        bias_part[0, :heads],
        gated_gain_part[0],
    ]
    sizes = [item.shape[0] for item in small]
    total = sum_all(jnp.concatenate(small))
    marks = [sum(sizes[:i]) for i in range(len(sizes) + 1)]
    sums = [total[marks[i] : marks[i + 1]] for i in range(len(sizes))]
    return (
        output,
        residual_grad,
        jnp.stack([gate_t, val_t[:, :gate_w]], axis=1),
        val_t[:, gate_w + shared_w : gate_w + shared_w + step_in.shape[1]],
        val_t[:, gate_w : gate_w + shared_w],
        qk_t[:, :query_w],
        qk_t[:, query_w : query_w + keyval_in.shape[1]],
        out_t[:, :gate_w].T,
        out_t[:, gate_w:].T,
        gate_up_sum,
        down_t.T,
        sums[0],
        sums[1],
        sums[2].reshape(conv_filter.shape),
        sums[3],
        sums[4],
        sums[5],
        sums[6],
    )


def solution(mesh):
    rows_spec = P(("dp", "tensor"), None)
    into = P("dp", "tensor")
    out_of = P("tensor", "dp")
    double = P("dp", None, "tensor")
    weights = (double, into, into, into, into, out_of, out_of, double, out_of)
    return jax.shard_map(
        shards,
        mesh=mesh,
        in_specs=(rows_spec,) + weights + (P(),) * 7 + (rows_spec,),
        out_specs=(rows_spec, rows_spec) + weights + (P(),) * 7,
        check_vma=False,
    )
```
